32 devices in a mesh: dp: 2 (over core), seq: 4 (over z), fsdp: 4 (over y, x).
Axes of the slice: x: 2, y: 2, z: 4, core: 2. Of those that a mesh axis runs over, the one named last changes fastest.
Arguments:
- block_input: bfloat16 [8, 512, 1536], P(('dp', 'fsdp'), 'seq'), may hold values from -6 to 6
- in_proj: bfloat16 [1536, 4608], P('fsdp'), may hold values from -0.15625 to 0.15625
- out_proj: bfloat16 [1536, 1536], P('fsdp'), may hold values from -0.15625 to 0.15625
- gate_proj: bfloat16 [1536, 6912], P('fsdp'), may hold values from -0.15625 to 0.15625
- up_proj: bfloat16 [1536, 6912], P('fsdp'), may hold values from -0.15625 to 0.15625
- down_proj: bfloat16 [6912, 1536], P('fsdp'), may hold values from -0.078125 to 0.078125
- norm_one: bfloat16 [1536], P('fsdp'), may hold values from 0.5 to 1.5
- norm_two: bfloat16 [1536], P('fsdp'), may hold values from 0.5 to 1.5
- conv_kernel: bfloat16 [3, 1536], P(None, 'fsdp'), may hold values from -3.5 to 3.5
- out_cotangent: bfloat16 [8, 512, 1536], P(('dp', 'fsdp'), 'seq'), may hold values from -6 to 6
Outputs:
- block_output: bfloat16 [8, 512, 1536], P(('dp', 'fsdp'), 'seq')
- input_grad: float32 [8, 512, 1536], P(('dp', 'fsdp'), 'seq')
- in_proj_grad: float32 [1536, 4608], P(('dp', 'seq', 'fsdp'))
- out_proj_grad: float32 [1536, 1536], P(('dp', 'seq', 'fsdp'))
- gate_proj_grad: float32 [1536, 6912], P(('dp', 'seq', 'fsdp'))
- up_proj_grad: float32 [1536, 6912], P(('dp', 'seq', 'fsdp'))
- down_projection_gradient: float32 [6912, 1536], P(None, ('dp', 'seq', 'fsdp'))
- norm_one_grad: float32 [1536], P(('dp', 'seq', 'fsdp'))
- norm_two_grad: float32 [1536], P(('dp', 'seq', 'fsdp'))
- conv_kernel_grad: float32 [3, 1536], P(None, ('dp', 'seq', 'fsdp'))
The draws below stay inside these ranges and needn't reach their ends.
All inputs are finite; a program needn't handle non-finite values.
Results may differ from the reference program's by a relative error of at most 0.0086.
Values may be sent and summed in bfloat16 or wider, within the bound.
No kernel may reach another device: no remote copies, remote signals or barrier semaphores. Data moves between devices by JAX's collectives and lax.ppermute only.
A program may use at most 256 MiB of HBM per device.

```python
import math
import jax
import jax.numpy as jnp
from jax import lax

D = 1536
FF = 6912
KW = 3
SEQS = 8
LEN = 512


def levels(stream_key, extent, cuts, smallest, top_value):
    loudness, own = 1.0, jax.random.fold_in(stream_key, 6)
    for axis_at, blocks in cuts:
        heights = jnp.exp(jax.random.uniform(jax.random.fold_in(own, axis_at), (blocks,), jnp.float32, smallest / len(cuts), top_value / len(cuts)))
        loudness = loudness * jnp.repeat(heights, extent[axis_at] // blocks).reshape([-1 if axis == axis_at else 1 for axis in range(len(extent))])
    return loudness


def normal_values(key, dims, scale, bound, cuts=(), dtype=jnp.bfloat16):
    values = jax.random.normal(key, dims, jnp.float32) * scale
    if len(cuts) > 0:
        values = levels(key, dims, cuts, -0.22, 0.18) * values
    return jnp.clip(values, min=-bound, max=bound).astype(dtype)


def setup_inputs(seed: int = 0) -> dict:
    key_list = jax.random.split(jax.random.key(seed), 11)
    block_input = normal_values(key_list[0], (SEQS, LEN, D), 1.0, 6.0, ((0, 8), (1, 4)))
    in_proj = normal_values(key_list[1], (D, 3 * D), D ** -0.5, 0.15625, ((0, 4),))
    out_proj = normal_values(key_list[2], (D, D), D ** -0.5, 0.15625, ((0, 4),))
    gate_proj = normal_values(key_list[3], (D, FF), D ** -0.5, 0.15625, ((0, 4),))
    up_proj = normal_values(key_list[4], (D, FF), D ** -0.5, 0.15625, ((0, 4),))
    down_proj = normal_values(key_list[5], (FF, D), FF ** -0.5, 0.078125, ((0, 4),))
    norm_one = jnp.clip(1.0 + 0.1 * jax.random.normal(key_list[6], (D,), jnp.float32), 0.5, 1.5).astype(jnp.bfloat16)
    norm_two = jnp.clip(1.0 + 0.1 * jax.random.normal(key_list[7], (D,), jnp.float32), 0.5, 1.5).astype(jnp.bfloat16)
    conv_kernel = normal_values(key_list[8], (KW, D), KW ** -0.5, 3.5, ((1, 4),))
    out_cotangent = normal_values(key_list[9], (SEQS, LEN, D), 1.0, 6.0, ((0, 8), (1, 4)))
    return {"block_input": block_input, "in_proj": in_proj, "out_proj": out_proj, "gate_proj": gate_proj, "up_proj": up_proj, "down_proj": down_proj, "norm_one": norm_one, "norm_two": norm_two, "conv_kernel": conv_kernel, "out_cotangent": out_cotangent}


epsilon = 1e-05

@jax.custom_vjp
def low(v):
    return lax.optimization_barrier(v.astype(jnp.bfloat16)).astype(jnp.float32)

@jax.custom_vjp
def low_back(v):
    return v

def low_keep(v):
    return (low(v), None)

def low_pass(kept, grad):
    return (grad,)

def back_keep(v):
    return (v, None)

def back_low(kept, grad):
    return (low(grad),)
low.defvjp(low_keep, low_pass)
low_back.defvjp(back_keep, back_low)

def rms_norm(values, gain):
    factor = lax.rsqrt(lax.optimization_barrier(jnp.mean(values * values, axis=-1, keepdims=True)) + epsilon)
    return values * factor * gain

def project(left_branch, right_branch):
    return jnp.einsum('mzw,wu->mzu', left_branch, right_branch, precision=lax.Precision.HIGHEST)

def mixer_block(values, in_proj, out_proj, gate_proj, up_proj, down_proj, norm_one, norm_two, conv_kernel):
    length = values.shape[1]
    model_width = values.shape[2]
    normed = low(rms_norm(values, norm_one))
    projected = low_back(project(normed, in_proj))
    b_part = projected[..., :model_width]
    c_part = projected[..., model_width:2 * model_width]
    x_part = projected[..., 2 * model_width:]
    product = b_part * x_part
    padded = jnp.pad(product, ((0, 0), (KW - 1, 0), (0, 0)))
    convolved = jnp.zeros_like(product)
    for tap_index in range(KW):
        convolved = convolved + conv_kernel[tap_index] * padded[:, tap_index:tap_index + length]
    gated = low(c_part * convolved)
    second_operand = values + low_back(project(gated, out_proj))
    normed_two = low(rms_norm(second_operand, norm_two))
    gate = low_back(project(normed_two, gate_proj))
    upward = low_back(project(normed_two, up_proj))
    hidden = low(jax.nn.silu(gate) * upward)
    return second_operand + project(hidden, down_proj)

def reference(block_input, in_proj, out_proj, gate_proj, up_proj, down_proj, norm_one, norm_two, conv_kernel, out_cotangent):
    weights = tuple((weight.astype(jnp.float32) for weight in (in_proj, out_proj, gate_proj, up_proj, down_proj, norm_one, norm_two, conv_kernel)))
    group_size = math.gcd(SEQS, max(1, 4096 // LEN))
    groups = SEQS // group_size
    inputs = block_input.reshape(groups, group_size, LEN, D)
    cotangents = out_cotangent.reshape(groups, group_size, LEN, D)

    def scan_step(totals, pieces):
        values, cotangent = pieces
        result, pullback = jax.vjp(mixer_block, values.astype(jnp.float32), *weights)
        grads = pullback(cotangent.astype(jnp.float32))
        totals = tuple((left_branch + right_branch for left_branch, right_branch in zip(totals, grads[1:])))
        return (totals, (result.astype(jnp.bfloat16), grads[0]))
    start = tuple((jnp.zeros(weight.shape, jnp.float32) for weight in weights))
    totals, (outputs, input_grads) = lax.scan(scan_step, start, (inputs, cotangents))
    return (outputs.reshape(SEQS, LEN, D), input_grads.reshape(SEQS, LEN, D), totals[0], totals[1], totals[2], totals[3], totals[4], totals[5], totals[6], totals[7])
```

```python
import jax
import jax.numpy as jnp
from jax import lax
from jax.sharding import PartitionSpec as P

epsilon = 1e-05
f32 = jnp.float32
bf16 = jnp.bfloat16


def dot(a, b, out=f32):
    return lax.dot_general(a, b, (((1,), (0,)), ((), ())), preferred_element_type=f32).astype(out)


def dot_rows(a, b, out=f32):
    return lax.dot_general(a, b, (((1,), (1,)), ((), ())), preferred_element_type=f32).astype(out)


def dot_tokens(a, b, out=f32):
    return lax.dot_general(a, b, (((0,), (0,)), ((), ())), preferred_element_type=f32).astype(out)


def after(value, *others):
    return lax.optimization_barrier((value, *others))[0]


def swap(value, axis, k):
    return lax.ppermute(value, axis, [(i, i ^ k) for i in range(lax.axis_size(axis))])


def shifted(block, axis, distance):
    devices = range(lax.axis_size(axis))
    route = [(i - distance, i) for i in devices if i - distance in devices]
    return lax.ppermute(block, axis, route)


def sum_everywhere(value):
    for axis in ("dp", "fsdp", "seq"):
        k = 1
        while k < lax.axis_size(axis):
            value = value + swap(value, axis, k)
            k *= 2
    return value


def on_device(
    block_input,
    in_proj,
    out_proj,
    gate_proj,
    up_proj,
    down_proj,
    norm_one,
    norm_two,
    conv_kernel,
    out_cotangent,
):
    shards = lax.axis_size("fsdp")
    blocks = lax.axis_size("seq")
    f = lax.axis_index("fsdp")
    c = lax.axis_index("dp")
    z = lax.axis_index("seq")
    others = range(1, shards)
    seqs, length, width = block_input.shape
    rows = seqs * length
    part = in_proj.shape[0]
    hidden_part = down_proj.shape[0]
    taps = conv_kernel.shape[0]
    rim = taps - 1
    half_part = part // 2
    groups = blocks * lax.axis_size("dp")
    slab = width // (groups * shards)

    def gather_tokens(local):
        return jnp.concatenate([local] + [swap(local, "fsdp", k) for k in others], axis=0)

    def scatter_tokens(partial):
        got = [swap(partial[k * rows : (k + 1) * rows], "fsdp", k) for k in others]
        total = partial[:rows].astype(f32)
        for piece in got:
            total = total + piece.astype(f32)
        return total

    def column_pieces(pick):
        own = pick(f)
        mine = [swap(lax.dynamic_slice_in_dim(pick(f ^ k), c * half_part, half_part, 0), "fsdp", k) for k in others]
        theirs = swap(jnp.stack(mine), "dp", 1)
        full = jnp.zeros((shards, 2, half_part, own.shape[1]), own.dtype)
        full = lax.dynamic_update_slice(full, own.reshape(1, 2, half_part, -1), (f, 0, 0, 0))
        for k in others:
            full = lax.dynamic_update_slice(full, mine[k - 1][None, None], (f ^ k, c, 0, 0))
            full = lax.dynamic_update_slice(full, theirs[k - 1][None, None], (f ^ k, 1 - c, 0, 0))
        return full.reshape(width, -1)

    small = jnp.concatenate([norm_one[None], norm_two[None], conv_kernel], axis=0)
    x_local = block_input.reshape(rows, width)
    x_all = gather_tokens(x_local)
    small_parts = [small] + [swap(small, "fsdp", k) for k in others]
    small_full = jnp.zeros((taps + 2, shards, part), bf16)
    for k in range(shards):
        small_full = lax.dynamic_update_slice(small_full, small_parts[k][:, None], (0, f ^ k, 0))
    small_full = small_full.reshape(taps + 2, width)
    gain_one = small_full[0].astype(f32)
    gain_two = small_full[1].astype(f32)
    taps_f = conv_kernel.astype(f32)

    in_parts = in_proj.reshape(part, 3, shards, part)

    def pick_in(j):
        return lax.dynamic_index_in_dim(in_parts, j, 2, keepdims=False).reshape(part, 3 * part)

    w_in = column_pieces(pick_in)

    def pick_hidden(weight):
        return lambda j: lax.dynamic_slice_in_dim(weight, j * hidden_part, hidden_part, 1)

    gate_late = after(gate_proj, x_all, w_in)
    w_gate = column_pieces(pick_hidden(gate_late))
    cot_local = out_cotangent.reshape(rows, width)
    cot_all = gather_tokens(after(cot_local, x_all, w_in))
    up_late = after(up_proj, w_gate)
    w_up = column_pieces(pick_hidden(up_late))

    xf = x_all.astype(f32)
    scale_one_all = lax.rsqrt(jnp.mean(xf * xf, axis=-1, keepdims=True) + epsilon)
    normed_one = (xf * scale_one_all * gain_one).astype(bf16)
    projected = dot(normed_one, w_in)
    b_part = projected[:, :part].reshape(-1, length, part)
    c_part = projected[:, part : 2 * part].reshape(-1, length, part)
    x_part = projected[:, 2 * part :].reshape(-1, length, part)
    product = b_part * x_part
    before = shifted(product[:, length - rim :], "seq", 1)
    extended = jnp.concatenate([before, product], axis=1)
    convolved = jnp.zeros_like(product)
    for t in range(taps):
        convolved = convolved + taps_f[t] * extended[:, t : t + length]
    gated = (c_part * convolved).astype(bf16).reshape(-1, part)

    by_owner = gated.reshape(-1, part // (shards * slab), shards, slab)
    channels = part // shards
    gated_rows = jnp.zeros((gated.shape[0], shards, channels), bf16)
    for k in range(shards):
        piece = lax.dynamic_index_in_dim(by_owner, f ^ k, 2, keepdims=False).reshape(-1, channels)
        if k:
            piece = swap(piece, "fsdp", k)
            piece = piece.reshape(shards, rows, channels)
            piece = jnp.stack([piece[b ^ k] for b in range(shards)]).reshape(-1, channels)
        gated_rows = lax.dynamic_update_slice(gated_rows, piece[:, None], (0, f ^ k, 0))
    gated_rows = gated_rows.reshape(-1, part)

    residual = x_local.astype(f32)
    scale_one = lax.rsqrt(jnp.mean(residual * residual, axis=-1, keepdims=True) + epsilon)
    second = residual + scatter_tokens(dot(gated, out_proj, bf16))
    scale_two = lax.rsqrt(jnp.mean(second * second, axis=-1, keepdims=True) + epsilon)
    normed_two = gather_tokens((second * scale_two * gain_two).astype(bf16))

    d_hidden = dot_rows(cot_all, down_proj)
    gate = dot(normed_two, w_gate)
    sigma = jax.nn.sigmoid(gate)
    activated = gate * sigma
    d_up = (d_hidden * activated).astype(bf16)
    upward = dot(normed_two, w_up)
    hidden = (activated * upward).astype(bf16)
    d_gate = (d_hidden * upward * sigma * (1.0 + gate * (1.0 - sigma))).astype(bf16)

    def weight_gradient(left, right):
        half = left.shape[1] // 2
        there = dot_tokens(lax.dynamic_slice_in_dim(left, (1 - c) * half, half, 1), right, bf16)
        come = swap(there, "dp", 1)
        here = dot_tokens(lax.dynamic_slice_in_dim(left, c * half, half, 1), right)
        both = (here + come.astype(f32)).astype(bf16)
        return lax.psum_scatter(both, "seq", scatter_dimension=0, tiled=True)

    def spread_rows(reduced):
        pieces = reduced.reshape(shards, slab, -1)
        full = jnp.zeros((shards, slab, pieces.shape[2]), bf16)
        for k in range(shards):
            piece = lax.dynamic_index_in_dim(pieces, f ^ k, 0, keepdims=False)
            if k:
                piece = swap(piece, "fsdp", k)
            full = lax.dynamic_update_slice(full, piece[None], (f ^ k, 0, 0))
        return full.astype(f32)

    up_sum = weight_gradient(normed_two, d_up)
    gate_sum = weight_gradient(normed_two, d_gate)
    down_sum = weight_gradient(cot_all, hidden)

    d_normed_two = scatter_tokens((dot_rows(d_gate, w_gate) + dot_rows(d_up, w_up)).astype(bf16))
    grad_two_term = jnp.sum(d_normed_two * second * scale_two, axis=0)
    weighted_two = d_normed_two * gain_two
    d_second = (
        cot_local.astype(f32)
        + scale_two * weighted_two
        - second * scale_two**3 * jnp.mean(weighted_two * second, axis=-1, keepdims=True)
    )
    d_mix = gather_tokens(d_second.astype(bf16))
    final = second + scatter_tokens(dot(hidden, down_proj, bf16))
    block_output = final.astype(bf16).reshape(seqs, length, width)

    d_gated = dot_rows(d_mix, out_proj).reshape(-1, length, part)
    d_c = d_gated * convolved
    d_conv = d_gated * c_part
    behind = shifted(d_conv[:, :rim], "seq", -1)
    d_extended = jnp.concatenate([d_conv, behind], axis=1)
    d_product = jnp.zeros_like(d_conv)
    kernel_terms = []
    for t in range(taps):
        offset = rim - t
        d_product = d_product + taps_f[t] * d_extended[:, offset : offset + length]
        kernel_terms.append(jnp.sum(d_conv * extended[:, t : t + length], axis=(0, 1)))
    kernel_term = jnp.stack(kernel_terms, axis=0)
    d_projected = jnp.concatenate([d_product * x_part, d_c, d_product * b_part], axis=2)
    d_projected = d_projected.astype(bf16).reshape(-1, 3 * part)
    in_sum = weight_gradient(normed_one, d_projected)
    out_grad = weight_gradient(gated_rows, d_mix).astype(f32)
    d_normed_one = scatter_tokens(dot_rows(d_projected, w_in, bf16))
    grad_one_term = jnp.sum(d_normed_one * residual * scale_one, axis=0)
    weighted_one = d_normed_one * gain_one
    input_grad = (
        d_second
        + scale_one * weighted_one
        - residual * scale_one**3 * jnp.mean(weighted_one * residual, axis=-1, keepdims=True)
    ).reshape(seqs, length, width)

    terms = jnp.concatenate([grad_one_term[None], grad_two_term[None], jnp.zeros((taps, width), f32)], axis=0)
    terms = lax.dynamic_update_slice(terms, kernel_term, (2, f * part))
    terms = sum_everywhere(terms)
    own = lax.dynamic_slice_in_dim(terms, ((c * blocks + z) * shards + f) * slab, slab, 1)

    def by_rows(reduced):
        return jnp.transpose(spread_rows(reduced), (1, 0, 2)).reshape(slab, -1)

    up_grad = by_rows(up_sum)
    gate_grad = by_rows(gate_sum)
    down_grad = jnp.transpose(spread_rows(down_sum), (0, 2, 1)).reshape(-1, slab)
    in_grad = spread_rows(in_sum).reshape(shards, slab, 3, part)
    in_grad = jnp.transpose(in_grad, (1, 2, 0, 3)).reshape(slab, 3 * width)
    return (
        block_output,
        input_grad,
        in_grad,
        out_grad,
        gate_grad,
        up_grad,
        down_grad,
        own[0],
        own[1],
        own[2:],
    )


def solution(mesh):
    placed = (
        P(("dp", "fsdp"), "seq", None),
        P("fsdp", None),
        P("fsdp", None),
        P("fsdp", None),
        P("fsdp", None),
        P("fsdp", None),
        P("fsdp"),
        P("fsdp"),
        P(None, "fsdp"),
        P(("dp", "fsdp"), "seq", None),
    )
    return jax.shard_map(
        on_device,
        mesh=mesh,
        in_specs=placed,
        out_specs=(
            P(("dp", "fsdp"), "seq", None),
            P(("dp", "fsdp"), "seq", None),
            P(("dp", "seq", "fsdp"), None),
            P(("dp", "seq", "fsdp"), None),
            P(("dp", "seq", "fsdp"), None),
            P(("dp", "seq", "fsdp"), None),
            P(None, ("dp", "seq", "fsdp")),
            P(("dp", "seq", "fsdp")),
            P(("dp", "seq", "fsdp")),
            P(None, ("dp", "seq", "fsdp")),
        ),
        check_vma=False,
    )
```

```python
import jax
import jax.numpy as jnp
from jax import lax
from jax.experimental import pallas as pl
from jax.experimental.pallas import tpu as pltpu
from jax.sharding import PartitionSpec as P

epsilon = 1e-05
f32 = jnp.float32
bf16 = jnp.bfloat16
MIB = 1 << 20
SCALE = 1e8
ANY = pl.BlockSpec(memory_space=pl.ANY)


def shape(dims, dtype=bf16):
    return jax.ShapeDtypeStruct(dims, dtype)


def far(dims, dtype=bf16):
    return pltpu.HBM(dims, dtype)


def in_far(value):
    return pltpu.with_memory_space_constraint(value, pltpu.HBM)


def whole(array):
    dims = array.shape
    return pl.BlockSpec(dims, lambda *steps: (0,) * len(dims), pipeline_mode=pl.Buffered(1))


def tiles(dims, axis):
    return pl.BlockSpec(dims, lambda step: tuple(step if i == axis else 0 for i in range(len(dims))))


def run(body, outs, ins, grid=(1,), in_specs=None, out_specs=None, scratch=(), after=(), limit=6, us=1.0, aliases=None):
    in_specs = [whole(a) for a in ins] if in_specs is None else in_specs
    out_specs = [whole(o) for o in outs] if out_specs is None else out_specs
    n, m = len(ins), len(after)

    def kernel(*refs):
        body(*refs[:n], *refs[n + m :])

    return pl.pallas_call(
        kernel,
        out_shape=tuple(outs),
        grid=grid,
        in_specs=list(in_specs) + [ANY] * m,
        out_specs=tuple(out_specs),
        scratch_shapes=list(scratch),
        compiler_params=pltpu.CompilerParams(vmem_limit_bytes=limit * MIB),
        cost_estimate=pl.CostEstimate(flops=int(us * SCALE), bytes_accessed=1000, transcendentals=0),
        input_output_aliases=aliases or {},
    )(*ins, *after)


def mm(a, b):
    return lax.dot_general(a, b, (((1,), (0,)), ((), ())), preferred_element_type=f32)


def mm_t(a, b):
    return lax.dot_general(a, b, (((1,), (1,)), ((), ())), preferred_element_type=f32)


def swap(value, axis, k):
    return lax.ppermute(value, axis, [(i, i ^ k) for i in range(lax.axis_size(axis))])


def shifted(block, axis, distance):
    devices = range(lax.axis_size(axis))
    route = [(i - distance, i) for i in devices if i - distance in devices]
    return lax.ppermute(block, axis, route)


def sum_everywhere(value):
    for axis in ("dp", "fsdp", "seq"):
        k = 1
        while k < lax.axis_size(axis):
            value = value + swap(value, axis, k)
            k *= 2
    return value


def wait_body(value_ref, out_ref):
    pass


def wait_for(value, *after):
    return run(
        wait_body,
        [shape(value.shape, value.dtype)],
        [value],
        in_specs=[ANY],
        out_specs=[ANY],
        after=after,
        limit=4,
        us=0.3,
        aliases={0: 0},
    )[0]


def token_body(out_ref):
    out_ref[0] = jnp.int32(0)


def token(*after):
    return run(
        token_body,
        [shape((1,), jnp.int32)],
        [],
        out_specs=[pl.BlockSpec(memory_space=pltpu.SMEM)],
        after=after,
        limit=4,
        us=0.3,
    )[0][0]


def hold_body(value_ref, out_ref, sem):
    copy = pltpu.make_async_copy(value_ref, out_ref, sem)
    copy.start()
    copy.wait()


def hold(value, *after):
    return run(
        hold_body,
        [shape(value.shape, value.dtype)],
        [value],
        in_specs=[ANY],
        out_specs=[ANY],
        scratch=[pltpu.SemaphoreType.DMA(())],
        after=after,
        limit=4,
    )[0]


def on_device(
    block_input,
    in_proj,
    out_proj,
    gate_proj,
    up_proj,
    down_proj,
    norm_one,
    norm_two,
    conv_kernel,
    out_cotangent,
):
    shards = lax.axis_size("fsdp")
    blocks = lax.axis_size("seq")
    f = lax.axis_index("fsdp")
    c = lax.axis_index("dp")
    z = lax.axis_index("seq")
    others = range(1, shards)
    seqs, length, width = block_input.shape
    rows = seqs * length
    group = shards * rows
    part = in_proj.shape[0]
    hidden = down_proj.shape[0]
    taps = conv_kernel.shape[0]
    rim = taps - 1
    edge = 16
    half_part = part // 2
    half = width // 2
    slab = width // (blocks * 2 * shards)
    tile = 512
    h_steps = pl.cdiv(hidden, tile)
    d_steps = width // tile
    chunk = half // blocks
    place = jnp.stack([f, c]).astype(jnp.int32)
    SMEM = pl.BlockSpec(memory_space=pltpu.SMEM)
    VMEM = pl.BlockSpec(memory_space=pltpu.VMEM)

    def send_tokens(local):
        return [swap(local, "fsdp", k) for k in others]

    def pack(pieces, after=()):
        count = len(pieces)

        def body(*refs):
            got, out_ref, sems = refs[:count], refs[count], refs[count + 1]
            copies = [pltpu.make_async_copy(got[i], out_ref.at[i], sems.at[i]) for i in range(count)]
            for copy in copies:
                copy.start()
            for copy in copies:
                copy.wait()

        return run(
            body,
            [shape((count, *pieces[0].shape))],
            pieces,
            in_specs=[ANY] * count,
            out_specs=[VMEM],
            scratch=[pltpu.SemaphoreType.DMA((count,))],
            after=after,
            limit=6,
        )[0]

    def assemble(own, parts, after=(), out=shape, out_spec=VMEM, limit=14):
        planes, _, columns = own.shape
        count = len(others)
        arrays = [p for p, _ in parts]
        starts = jnp.stack([f] + [h for _, h in parts]).astype(jnp.int32)

        def body(place_ref, own_ref, *refs):
            got, out_ref, sems = refs[: len(arrays)], refs[-2], refs[-1]
            f_ = place_ref[0]
            copies = []
            for p in range(planes):
                target = out_ref.at[p, pl.ds(pl.multiple_of(f_ * part, part), part)]
                copies.append(pltpu.make_async_copy(own_ref.at[p], target, sems.at[len(copies)]))
                for j, ref in enumerate(got):
                    size = ref.shape[2]
                    for i, k in enumerate(others):
                        start = pl.multiple_of((f_ ^ k) * part + place_ref[1 + j], size)
                        target = out_ref.at[p, pl.ds(start, size)]
                        copies.append(pltpu.make_async_copy(ref.at[i, p], target, sems.at[len(copies)]))
            for copy in copies:
                copy.start()
            for copy in copies:
                copy.wait()

        return run(
            body,
            [out((planes, width, columns))],
            [starts, own, *arrays],
            in_specs=[SMEM] + [VMEM] * (1 + len(arrays)),
            out_specs=[out_spec],
            scratch=[pltpu.SemaphoreType.DMA((planes * (1 + len(arrays) * count),))],
            after=after,
            limit=limit,
        )[0]

    quarter = half_part // 2
    here, there = (z % 2) * quarter, (1 - z % 2) * quarter

    def both_piece(j, start, size):
        return jnp.stack(
            [lax.dynamic_slice(weight, (start, j * hidden), (size, hidden)) for weight in (gate_proj, up_proj)]
        )

    both_sent = [both_piece(f ^ k, c * half_part + here, quarter) for k in others]
    both_got = [swap(piece, "fsdp", k) for piece, k in zip(both_sent, others)]

    def in_body(place_ref, w_ref, *refs):
        outs, sems = refs[: len(others)], refs[-1]
        copies = []
        for i, k in enumerate(others):
            for t in range(3):
                start = pl.multiple_of(t * width + (place_ref[0] ^ k) * part, part)
                first = pl.multiple_of(place_ref[1] * half_part, half_part)
                source = w_ref.at[pl.ds(first, half_part), pl.ds(start, part)]
                target = outs[i].at[:, pl.ds(t * part, part)]
                copies.append(pltpu.make_async_copy(source, target, sems.at[i * 3 + t]))
        for copy in copies:
            copy.start()
        for copy in copies:
            copy.wait()

    in_sent = run(
        in_body,
        [shape((half_part, 3 * part))] * len(others),
        [place, in_proj],
        in_specs=[SMEM, ANY],
        out_specs=[VMEM] * len(others),
        scratch=[pltpu.SemaphoreType.DMA((3 * len(others),))],
        after=(both_sent[0],),
    )
    in_got = [swap(m, "fsdp", k) for m, k in zip(in_sent, others)]

    x_local = block_input.reshape(rows, width)
    cot_local = out_cotangent.reshape(rows, width)
    tail = shifted(x_local[rows - edge :], "seq", 1)
    small = jnp.concatenate([norm_one[None], norm_two[None], conv_kernel], axis=0)
    small = jnp.pad(small, ((0, edge - taps - 2), (0, 0)))
    small_at = rows + edge

    def join_body(x_ref, t_ref, small_ref, out_ref):
        out_ref[:rows] = x_ref[...]
        out_ref[rows:small_at] = t_ref[...]
        out_ref[small_at:] = jnp.zeros((edge, width), bf16)
        out_ref[small_at:, :part] = small_ref[...]

    (message,) = run(join_body, [shape((small_at + edge, width))], [x_local, tail, small])
    messages = [message] + send_tokens(message)
    taps_own = conv_kernel.astype(f32)

    both_mine = pack(both_got, (message, in_sent[0]))
    both_next = swap(both_mine, "seq", 1)
    in_mine = pack(in_got, (both_mine,))
    in_own = jnp.concatenate([lax.dynamic_slice_in_dim(in_proj, t * width + f * part, part, 1) for t in range(3)], axis=1)

    def norm_body(place_ref, *refs):
        xs, (n_ref, nh_ref, gain_ref) = refs[:shards], refs[shards:]
        for s in range(shards):
            pick = xs[0][small_at:, :part]
            for k in others:
                pick = jnp.where((place_ref[0] ^ k) == s, xs[k][small_at:, :part], pick)
            gain_ref[:, s * part : (s + 1) * part] = pick[:8].astype(f32)
        gain = gain_ref[0:1]

        def normed(v):
            v = v.astype(f32)
            r = lax.rsqrt(jnp.mean(v * v, axis=-1, keepdims=True) + epsilon)
            return (v * r * gain).astype(bf16)

        for k in range(shards):
            n_ref[k * rows : (k + 1) * rows] = normed(xs[k][:rows])
            nh_ref[k * edge : (k + 1) * edge] = normed(xs[k][rows:small_at])

    normed_one, normed_edge, gains = run(
        norm_body,
        [shape((group, width)), shape((shards * edge, width)), shape((8, width), f32)],
        [place, *messages],
        in_specs=[SMEM] + [whole(m) for m in messages],
        after=(in_mine,),
        us=2,
    )
    in_mine = in_mine[:, None]
    w_in = assemble(
        in_own[None], [(in_mine, c * half_part), (swap(in_mine, "dp", 1), (1 - c) * half_part)], (normed_one,)
    )[0]

    cot_held = hold(cot_local, in_mine)
    cot_blocks = [cot_held] + send_tokens(cot_held)

    def mixer_body(n_ref, nh_ref, taps_ref, w_ref, o_ref, proj_ref, edge_ref, gated_ref, *refs):
        p_refs, (ph_ref, ext_ref) = refs[:shards], refs[shards:]
        for t in range(3):
            cols = slice(t * part, (t + 1) * part)
            w = w_ref[:, cols]
            proj_ref[:, cols] = mm(n_ref[...], w)
            if t != 1:
                ph_ref[:, cols] = mm(nh_ref[...], w)
        edge_ref[...] = ph_ref[:, :part] * ph_ref[:, 2 * part :]
        for k in range(shards):
            r = slice(k * rows, (k + 1) * rows)
            ext_ref[:edge] = edge_ref[k * edge : (k + 1) * edge]
            ext_ref[edge:] = proj_ref[r, :part] * proj_ref[r, 2 * part :]
            conv = taps_ref[rim : rim + 1] * ext_ref[edge:]
            for t in range(rim):
                conv = conv + taps_ref[t : t + 1] * ext_ref[edge - rim + t : edge - rim + t + rows]
            gated_ref[r] = (proj_ref[r, part : 2 * part] * conv).astype(bf16)
        for t in range(width // 512):
            cols = slice(t * 512, (t + 1) * 512)
            o = mm(gated_ref[...], o_ref[:, cols]).astype(bf16)
            for k in range(shards):
                p_refs[k][:, cols] = o[k * rows : (k + 1) * rows]

    projected, edge_product, gated, *mix_parts = run(
        mixer_body,
        [
            shape((group, 3 * part), f32),
            shape((shards * edge, part), f32),
            shape((group, part)),
        ]
        + [shape((rows, width))] * shards,
        [normed_one, normed_edge, taps_own, w_in, out_proj],
        scratch=[pltpu.VMEM((shards * edge, 3 * part), f32), pltpu.VMEM((edge + rows, part), f32)],
        after=(cot_held,),
        us=5.5,
        limit=6,
    )

    def cot_body(*refs):
        blocks_, down_ref, dh_ref, t_ref, all_ref = refs[:shards], *refs[shards:]

        @pl.when(pl.program_id(0) == 0)
        def _():
            for k in range(shards):
                all_ref[k * rows : (k + 1) * rows] = blocks_[k][...]
            for h in range(2):
                t_ref[h] = all_ref[:, h * half : (h + 1) * half].T

        dh_ref[...] = mm_t(all_ref[...], down_ref[...])

    d_hidden, cot_turned = run(
        cot_body,
        [far((group, hidden), f32), shape((2, half, group))],
        [*cot_blocks, in_far(down_proj)],
        grid=(h_steps,),
        in_specs=[whole(b) for b in cot_blocks] + [tiles((tile, width), 0)],
        out_specs=[tiles((group, tile), 1), whole(shape((2, half, group)))],
        scratch=[pltpu.VMEM((group, width), bf16)],
        after=(gated,),
        us=5,
        limit=14,
    )

    d_hidden = in_far(d_hidden)
    mix_got = [swap(mix_parts[k], "fsdp", k) for k in others]

    def second_body(*refs):
        parts, x_ref, gain_ref, s_ref, n_ref = refs[:shards], *refs[shards:]
        total = x_ref[...].astype(f32)
        for p in parts:
            total = total + p[...].astype(f32)
        s_ref[...] = total
        r = lax.rsqrt(jnp.mean(total * total, axis=-1, keepdims=True) + epsilon)
        n_ref[...] = (total * r * gain_ref[1:2]).astype(bf16)

    second, normed_two = run(
        second_body,
        [shape((rows, width), f32), shape((rows, width))],
        [mix_parts[0], *mix_got, x_local, gains],
        after=(d_hidden,),
    )
    two_blocks = [normed_two] + send_tokens(normed_two)

    w_both = assemble(
        both_piece(f, 0, part),
        [
            (both_mine, c * half_part + here),
            (both_next, c * half_part + there),
            (swap(both_mine, "dp", 1), (1 - c) * half_part + here),
            (swap(wait_for(both_next, normed_two), "dp", 1), (1 - c) * half_part + there),
        ],
        (normed_two,),
        far,
        ANY,
        20,
    )
    w_both = in_far(w_both)
    ff_tile = 256
    ff_steps = pl.cdiv(hidden, ff_tile)

    def feed_body(place_ref, *refs):
        blocks_, (w_ref, dh_ref, ct_ref) = refs[:shards], refs[shards : shards + 3]
        du_ref, dg_ref, h_ref, t_ref, up_ref, two_ref, all_ref = refs[shards + 3 :]

        @pl.when(pl.program_id(0) == 0)
        def _():
            for k in range(shards):
                all_ref[k * rows : (k + 1) * rows] = blocks_[k][...]
            for h in range(2):
                t_ref[h] = all_ref[:, h * half : (h + 1) * half].T

        other = 1 - place_ref[1]
        gate = mm(all_ref[...], w_ref[0])
        upward = mm(all_ref[...], w_ref[1])
        s = jax.nn.sigmoid(gate)
        dh = dh_ref[...]
        du = (dh * (gate * s)).astype(bf16)
        dg = (dh * upward * s * (1.0 + gate * (1.0 - s))).astype(bf16)
        hid = (gate * s * upward).astype(bf16)
        du_ref[...] = du
        dg_ref[...] = dg
        h_ref[...] = hid
        up_ref[...] = mm(t_ref[other], du).astype(bf16).reshape(blocks, chunk, ff_tile)
        two_ref[:, 0] = mm(t_ref[other], dg).astype(bf16).reshape(blocks, chunk, ff_tile)
        two_ref[:, 1] = mm(ct_ref[other], hid).astype(bf16).reshape(blocks, chunk, ff_tile)

    d_up, d_gate, hidden_all, two_turned, up_there, two_there = run(
        feed_body,
        [
            far((group, hidden)),
            far((group, hidden)),
            far((group, hidden)),
            shape((2, half, group)),
            far((blocks, chunk, hidden)),
            far((blocks, 2, chunk, hidden)),
        ],
        [place, *two_blocks, w_both, d_hidden, cot_turned],
        grid=(ff_steps,),
        in_specs=[SMEM]
        + [whole(b) for b in two_blocks]
        + [tiles((2, width, ff_tile), 2), tiles((group, ff_tile), 1), whole(cot_turned)],
        out_specs=[
            tiles((group, ff_tile), 1),
            tiles((group, ff_tile), 1),
            tiles((group, ff_tile), 1),
            whole(shape((2, half, group))),
            tiles((blocks, chunk, ff_tile), 2),
            tiles((blocks, 2, chunk, ff_tile), 3),
        ],
        scratch=[pltpu.VMEM((group, width), bf16)],
        us=18,
        limit=22,
    )
    d_up, d_gate, hidden_all = in_far(d_up), in_far(d_gate), in_far(hidden_all)
    up_come = swap(up_there, "dp", 1)
    two_come = swap(two_there, "dp", 1)

    def up_sum_body(place_ref, t_ref, du_ref, come_ref, out_ref):
        here_ = mm(t_ref[place_ref[1]], du_ref[...])
        here_ = here_.reshape(blocks, chunk, tile)
        out_ref[...] = (here_ + come_ref[...].astype(f32)).astype(bf16)

    (up_both,) = run(
        up_sum_body,
        [far((blocks, chunk, hidden))],
        [place, two_turned, d_up, up_come],
        grid=(h_steps,),
        in_specs=[SMEM, whole(two_turned), tiles((group, tile), 1), tiles((blocks, chunk, tile), 2)],
        out_specs=[tiles((blocks, chunk, tile), 2)],
        us=3.5,
        limit=12,
    )
    up_sum = lax.psum_scatter(up_both, "seq", scatter_dimension=0, tiled=True).reshape(chunk, hidden)

    def two_sum_body(place_ref, t_ref, ct_ref, dg_ref, h_ref, come_ref, out_ref):
        own = place_ref[1]
        gate_here = mm(t_ref[own], dg_ref[...]).reshape(blocks, chunk, tile)
        down_here = mm(ct_ref[own], h_ref[...]).reshape(blocks, chunk, tile)
        out_ref[:, 0] = (gate_here + come_ref[:, 0].astype(f32)).astype(bf16)
        out_ref[:, 1] = (down_here + come_ref[:, 1].astype(f32)).astype(bf16)

    (two_both,) = run(
        two_sum_body,
        [far((blocks, 2, chunk, hidden))],
        [place, two_turned, cot_turned, d_gate, hidden_all, two_come],
        grid=(h_steps,),
        in_specs=[
            SMEM,
            whole(two_turned),
            whole(cot_turned),
            tiles((group, tile), 1),
            tiles((group, tile), 1),
            tiles((blocks, 2, chunk, tile), 3),
        ],
        out_specs=[tiles((blocks, 2, chunk, tile), 3)],
        after=(up_both,),
        us=6,
        limit=18,
    )
    two_both = wait_for(two_both, up_sum)
    two_sum = lax.psum_scatter(two_both, "seq", scatter_dimension=0, tiled=True)
    two_sum = two_sum.reshape(2, chunk, hidden)

    def back_two_body(dg_ref, du_ref, wg_ref, wu_ref, *p_refs):
        d = (mm_t(dg_ref[...], wg_ref[...]) + mm_t(du_ref[...], wu_ref[...])).astype(bf16)
        for k in range(shards):
            p_refs[k][...] = d[k * rows : (k + 1) * rows]

    back_two = run(
        back_two_body,
        [shape((rows, width))] * shards,
        [d_gate, d_up, w_both, w_both],
        grid=(d_steps,),
        in_specs=[
            whole(d_gate),
            whole(d_up),
            pl.BlockSpec((None, tile, hidden), lambda step: (0, step, 0)),
            pl.BlockSpec((None, tile, hidden), lambda step: (1, step, 0)),
        ],
        out_specs=[tiles((rows, tile), 1)] * shards,
        after=(up_both,),
        us=7,
        limit=16,
    )
    back_two_got = [swap(back_two[k], "fsdp", k) for k in others]

    def final_body(h_ref, w_ref, *p_refs):
        d = mm(h_ref[...], w_ref[...]).astype(bf16)
        for k in range(shards):
            p_refs[k][...] = d[k * rows : (k + 1) * rows]

    final_parts = run(
        final_body,
        [shape((rows, width))] * shards,
        [hidden_all, in_far(down_proj)],
        grid=(d_steps,),
        in_specs=[whole(hidden_all), tiles((hidden, tile), 1)],
        out_specs=[tiles((rows, tile), 1)] * shards,
        after=(back_two[0],),
        us=4,
        limit=12,
    )

    def second_grad_body(*refs):
        parts, (s_ref, cot_ref, gain_ref, d_ref, mix_ref, term_ref) = refs[:shards], refs[shards:]
        dn = parts[0][...].astype(f32)
        for p in parts[1:]:
            dn = dn + p[...].astype(f32)
        s = s_ref[...]
        r = lax.rsqrt(jnp.mean(s * s, axis=-1, keepdims=True) + epsilon)
        term_ref[...] = jnp.sum(dn * s * r, axis=0, keepdims=True)
        a = dn * gain_ref[1:2]
        d = cot_ref[...].astype(f32) + r * a - s * (r * r * r) * jnp.mean(a * s, axis=-1, keepdims=True)
        d_ref[...] = d
        mix_ref[...] = d.astype(bf16)

    d_second, d_mix, two_term = run(
        second_grad_body,
        [shape((rows, width), f32), shape((rows, width)), shape((1, width), f32)],
        [back_two[0], *back_two_got, second, cot_local, gains],
        after=(two_both,),
    )
    mix_blocks = [d_mix] + send_tokens(d_mix)

    runs = part // (shards * slab)
    channels = part // shards

    def owner_body(place_ref, g_ref, *out_refs):
        row = lax.broadcasted_iota(jnp.int32, (part, channels), 0)
        col = lax.broadcasted_iota(jnp.int32, (part, channels), 1)
        for k in range(shards):
            source = (col // slab) * (shards * slab) + (place_ref[0] ^ k) * slab + col % slab
            out_refs[k][...] = mm(g_ref[...], (row == source).astype(bf16)).astype(bf16)

    owner = run(
        owner_body,
        [shape((group, channels))] * shards,
        [place, gated],
        in_specs=[SMEM, whole(gated)],
        after=(two_both,),
    )
    owner_got = [owner[0]] + [swap(owner[k], "fsdp", k) for k in others]

    final_got = [swap(final_parts[k], "fsdp", k) for k in others]
    total = second + final_parts[0].astype(f32)
    for piece in final_got:
        total = total + piece.astype(f32)
    block_output = total.astype(bf16).reshape(seqs, length, width)

    def gated_grad_body(*refs):
        blocks_, (o_ref, proj_ref, edge_ref, taps_ref) = refs[:shards], refs[shards : shards + 4]
        all_ref, dc_ref, dconv_ref, head_ref, term_ref, ext_ref = refs[shards + 4 :]
        for k in range(shards):
            all_ref[k * rows : (k + 1) * rows] = blocks_[k][...]
        dg = mm_t(all_ref[...], o_ref[...])
        dconv_ref[...] = dg * proj_ref[:, part : 2 * part]
        terms = [jnp.zeros((1, part), f32)] * taps
        for k in range(shards):
            r = slice(k * rows, (k + 1) * rows)
            d = dconv_ref[r]
            head_ref[k * 8 : (k + 1) * 8] = d[:8]
            ext_ref[:edge] = edge_ref[k * edge : (k + 1) * edge]
            ext_ref[edge:] = proj_ref[r, :part] * proj_ref[r, 2 * part :]
            conv = jnp.zeros((rows, part), f32)
            for t in range(taps):
                e = ext_ref[edge - rim + t : edge - rim + t + rows]
                conv = conv + taps_ref[t : t + 1] * e
                terms[t] = terms[t] + jnp.sum(d * e, axis=0, keepdims=True)
            dc_ref[r] = (dg[k * rows : (k + 1) * rows] * conv).astype(bf16)
        for t in range(taps):
            term_ref[t : t + 1] = terms[t]

    mix_all, d_c, d_conv, heads, tap_terms = run(
        gated_grad_body,
        [
            shape((group, width)),
            shape((group, part)),
            shape((group, part), f32),
            shape((shards * 8, part), f32),
            shape((taps, part), f32),
        ],
        [*mix_blocks, out_proj, projected, edge_product, taps_own],
        scratch=[pltpu.VMEM((edge + rows, part), f32)],
    )
    behind = shifted(heads, "seq", -1)

    def turn_body(place_ref, n_ref, *refs):
        got, (nt_ref, ot_ref) = refs[:shards], refs[shards:]
        for h in range(2):
            nt_ref[h] = n_ref[:, h * half : (h + 1) * half].T
        row = lax.broadcasted_iota(jnp.int32, (channels, part), 0)
        col = lax.broadcasted_iota(jnp.int32, (channels, part), 1)
        for b in range(shards):
            both = jnp.zeros((rows, part), f32)
            for k in range(shards):
                spread = (col == row + (place_ref[0] ^ k) * channels).astype(bf16)
                both = both + mm(got[k][(b ^ k) * rows : ((b ^ k) + 1) * rows], spread)
            both = both.astype(bf16)
            for h in range(2):
                wide = both[:, h * (part // 2) : (h + 1) * (part // 2)]
                ot_ref[h, :, b * rows : (b + 1) * rows] = wide.astype(f32).T.astype(bf16)

    one_turned, own_turned = run(
        turn_body,
        [shape((2, half, group)), shape((2, part // 2, group))],
        [place, normed_one, *owner_got],
        in_specs=[SMEM, whole(normed_one)] + [whole(o) for o in owner_got],
        after=(mix_blocks[0],),
    )

    def projected_grad_body(
        place_ref, dconv_ref, behind_ref, taps_ref, proj_ref, dc_ref, nt_ref, ot_ref, mix_ref,
        dp_ref, in_ref, out_ref, ext_ref,
    ):
        other = 1 - place_ref[1]
        for k in range(shards):
            r = slice(k * rows, (k + 1) * rows)
            ext_ref[:rows] = dconv_ref[r]
            ext_ref[rows:] = behind_ref[k * 8 : (k + 1) * 8]
            d = taps_ref[rim : rim + 1] * ext_ref[:rows]
            for t in range(rim):
                d = d + taps_ref[t : t + 1] * ext_ref[rim - t : rim - t + rows]
            dp_ref[r, :part] = (d * proj_ref[r, 2 * part :]).astype(bf16)
            dp_ref[r, part : 2 * part] = dc_ref[r]
            dp_ref[r, 2 * part :] = (d * proj_ref[r, :part]).astype(bf16)
        for t in range(3):
            cols = slice(t * part, (t + 1) * part)
            in_ref[:, :, cols] = mm(nt_ref[other], dp_ref[:, cols]).astype(bf16).reshape(blocks, chunk, part)
        for t in range(width // 512):
            cols = slice(t * 512, (t + 1) * 512)
            out_ref[:, cols] = mm(ot_ref[other], mix_ref[:, cols]).astype(bf16)

    d_projected, in_there, out_there = run(
        projected_grad_body,
        [shape((group, 3 * part)), shape((blocks, chunk, 3 * part)), shape((part // 2, width))],
        [place, d_conv, behind, taps_own, projected, d_c, one_turned, own_turned, mix_all],
        in_specs=[SMEM] + [whole(a) for a in (d_conv, behind, taps_own, projected, d_c, one_turned, own_turned, mix_all)],
        scratch=[pltpu.VMEM((rows + 8, part), f32)],
        us=3,
    )
    in_come = swap(in_there, "dp", 1)
    out_come = swap(out_there, "dp", 1)

    def back_one_body(dp_ref, w_ref, *p_refs):
        d = mm_t(dp_ref[...], w_ref[...]).astype(bf16)
        for k in range(shards):
            p_refs[k][...] = d[k * rows : (k + 1) * rows]

    back_one = run(
        back_one_body,
        [shape((rows, width))] * shards,
        [d_projected, w_in],
        grid=(d_steps,),
        in_specs=[whole(d_projected), tiles((tile, 3 * part), 0)],
        out_specs=[tiles((rows, tile), 1)] * shards,
        us=4,
        limit=12,
    )
    back_one_got = [swap(back_one[k], "fsdp", k) for k in others]

    def mixer_sum_body(place_ref, nt_ref, dp_ref, in_come_ref, ot_ref, mix_ref, out_come_ref, in_ref, out_ref):
        own = place_ref[1]
        for t in range(3):
            cols = slice(t * part, (t + 1) * part)
            here = mm(nt_ref[own], dp_ref[:, cols]).reshape(blocks, chunk, part)
            in_ref[:, :, cols] = (here + in_come_ref[:, :, cols].astype(f32)).astype(bf16)
        for t in range(width // 512):
            cols = slice(t * 512, (t + 1) * 512)
            here = mm(ot_ref[own], mix_ref[:, cols])
            out_ref[:, cols] = (here + out_come_ref[:, cols].astype(f32)).astype(bf16)

    in_both, out_both = run(
        mixer_sum_body,
        [shape((blocks, chunk, 3 * part)), shape((part // 2, width))],
        [place, one_turned, d_projected, in_come, own_turned, mix_all, out_come],
        in_specs=[SMEM]
        + [whole(a) for a in (one_turned, d_projected, in_come, own_turned, mix_all, out_come)],
        after=(back_one[0],),
    )

    def own_rows(k):
        return lax.dynamic_slice_in_dim(out_both, (z ^ k) * slab, slab, 0)

    out_got = [own_rows(0)] + [swap(own_rows(k), "seq", k) for k in range(1, blocks)]

    def out_sum_body(*refs):
        total = refs[0][...].astype(f32)
        for ref in refs[1:-1]:
            total = total + ref[...].astype(f32)
        refs[-1][...] = total

    (out_grad,) = run(out_sum_body, [shape((slab, width), f32)], out_got)

    def input_grad_body(*refs):
        parts, (x_ref, d_ref, gain_ref, out_ref, term_ref) = refs[:shards], refs[shards:]
        dn = parts[0][...].astype(f32)
        for p in parts[1:]:
            dn = dn + p[...].astype(f32)
        x = x_ref[...].astype(f32)
        r = lax.rsqrt(jnp.mean(x * x, axis=-1, keepdims=True) + epsilon)
        term_ref[...] = jnp.sum(dn * x * r, axis=0, keepdims=True)
        a = dn * gain_ref[0:1]
        out_ref[...] = d_ref[...] + r * a - x * (r * r * r) * jnp.mean(a * x, axis=-1, keepdims=True)

    input_grad, one_term = run(
        input_grad_body,
        [shape((rows, width), f32), shape((1, width), f32)],
        [back_one[0], *back_one_got, x_local, d_second, gains],
        after=(in_both,),
    )
    input_grad = input_grad.reshape(seqs, length, width)

    in_both = wait_for(in_both, two_sum, input_grad, block_output)
    in_sum = lax.psum_scatter(in_both, "seq", scatter_dimension=0, tiled=True)
    in_sum = in_sum.reshape(chunk, 3 * part)

    spread_taps = [jnp.where(f == s, tap_terms, 0.0) for s in range(shards)]
    terms = jnp.concatenate([one_term, two_term, jnp.concatenate(spread_taps, axis=1)], axis=0)
    terms = sum_everywhere(terms)
    own = lax.dynamic_slice_in_dim(terms, ((c * blocks + z) * shards + f) * slab, slab, 1)

    def spread_rows(reduced, dims, put):
        parts = [lax.dynamic_slice_in_dim(reduced, f * slab, slab, 0)]
        parts += [swap(lax.dynamic_slice_in_dim(reduced, (f ^ k) * slab, slab, 0), "fsdp", k) for k in others]

        def body(place_ref, *refs):
            got, out_ref = refs[:shards], refs[shards]
            for s in range(shards):
                pick = got[0][...].astype(f32)
                for k in others:
                    pick = jnp.where((place_ref[0] ^ k) == s, got[k][...].astype(f32), pick)
                put(out_ref, s, pick)

        return run(body, [shape(dims, f32)], [place, *parts], in_specs=[SMEM] + [whole(p) for p in parts])[0]

    def put_columns(out_ref, s, value):
        out_ref[:, s * hidden : (s + 1) * hidden] = value

    def put_streams(out_ref, s, value):
        for t in range(3):
            out_ref[:, t * width + s * part : t * width + (s + 1) * part] = value[:, t * part : (t + 1) * part]

    up_grad = spread_rows(up_sum, (slab, shards * hidden), put_columns)
    gate_grad = spread_rows(two_sum[0], (slab, shards * hidden), put_columns)
    down_rows = spread_rows(two_sum[1], (slab, shards * hidden), put_columns)
    down_grad = jnp.transpose(down_rows)
    in_sum = wait_for(in_sum, up_grad, gate_grad, down_rows, terms, out_grad, block_output)
    in_grad = spread_rows(in_sum, (slab, 3 * width), put_streams)
    return (
        block_output,
        input_grad,
        in_grad,
        out_grad,
        gate_grad,
        up_grad,
        down_grad,
        own[0],
        own[1],
        own[2:],
    )


def solution(mesh):
    placed = (
        P(("dp", "fsdp"), "seq", None),
        P("fsdp", None),
        P("fsdp", None),
        P("fsdp", None),
        P("fsdp", None),
        P("fsdp", None),
        P("fsdp"),
        P("fsdp"),
        P(None, "fsdp"),
        P(("dp", "fsdp"), "seq", None),
    )
    return jax.shard_map(
        on_device,
        mesh=mesh,
        in_specs=placed,
        out_specs=(
            P(("dp", "fsdp"), "seq", None),
            P(("dp", "fsdp"), "seq", None),
            P(("dp", "seq", "fsdp"), None),
            P(("dp", "seq", "fsdp"), None),
            P(("dp", "seq", "fsdp"), None),
            P(("dp", "seq", "fsdp"), None),
            P(None, ("dp", "seq", "fsdp")),
            P(("dp", "seq", "fsdp")),
            P(("dp", "seq", "fsdp")),
            P(None, ("dp", "seq", "fsdp")),
        ),
        check_vma=False,
    )
```

```python
import math

import jax
import jax.numpy as jnp
from jax import lax
from jax.experimental import pallas as pl
from jax.experimental.pallas import tpu as pltpu
from jax.sharding import PartitionSpec as P

epsilon = 1e-05
f32 = jnp.float32
bf16 = jnp.bfloat16
MIB = 1 << 20
SCALE = 1e8
ANY = pl.BlockSpec(memory_space=pl.ANY)


def shape(dims, dtype=bf16):
    return jax.ShapeDtypeStruct(dims, dtype)


def far(dims, dtype=bf16):
    return pltpu.HBM(dims, dtype)


def in_far(value):
    return pltpu.with_memory_space_constraint(value, pltpu.HBM)


def whole(array):
    dims = array.shape
    return pl.BlockSpec(dims, lambda *steps: (0,) * len(dims), pipeline_mode=pl.Buffered(1))


def tiles(dims, axis):
    return pl.BlockSpec(dims, lambda step: tuple(step if i == axis else 0 for i in range(len(dims))))


def run(body, outs, ins, grid=(1,), in_specs=None, out_specs=None, scratch=(), after=(), limit=6, us=1.0, aliases=None, hbm=False, near=()):
    in_specs = [whole(a) for a in ins] if in_specs is None else in_specs
    out_specs = [whole(o) for o in outs] if out_specs is None else out_specs
    n, m = len(ins), len(after)
    if hbm:
        ins = [in_far(a) if a.size > 1024 and i not in near else a for i, a in enumerate(ins)]
        outs = [far(o.shape, o.dtype) if math.prod(o.shape) > 1024 else o for o in outs]

    def kernel(*refs):
        body(*refs[:n], *refs[n + m :])

    return pl.pallas_call(
        kernel,
        out_shape=tuple(outs),
        grid=grid,
        in_specs=list(in_specs) + [ANY] * m,
        out_specs=tuple(out_specs),
        scratch_shapes=list(scratch),
        compiler_params=pltpu.CompilerParams(vmem_limit_bytes=limit * MIB),
        cost_estimate=pl.CostEstimate(flops=int(us * SCALE), bytes_accessed=1000, transcendentals=0),
        input_output_aliases=aliases or {},
    )(*ins, *after)


def mm(a, b):
    return lax.dot_general(a, b, (((1,), (0,)), ((), ())), preferred_element_type=f32)


def mm_t(a, b):
    return lax.dot_general(a, b, (((1,), (1,)), ((), ())), preferred_element_type=f32)


def swap(value, axis, k):
    return lax.ppermute(value, axis, [(i, i ^ k) for i in range(lax.axis_size(axis))])


def shifted(block, axis, distance):
    devices = range(lax.axis_size(axis))
    route = [(i - distance, i) for i in devices if i - distance in devices]
    return lax.ppermute(block, axis, route)


def sum_everywhere(value):
    for axis in ("dp", "fsdp", "seq"):
        k = 1
        while k < lax.axis_size(axis):
            value = value + swap(value, axis, k)
            k *= 2
    return value


def wait_body(value_ref, out_ref):
    pass


def wait_for(value, *after, keep=False):
    return run(
        wait_body,
        [far(value.shape, value.dtype) if keep else shape(value.shape, value.dtype)],
        [in_far(value) if keep else value],
        in_specs=[ANY],
        out_specs=[ANY],
        after=after,
        limit=4,
        us=0.3,
        aliases={0: 0},
    )[0]


def wait_all_body(*refs):
    pass


def wait_all(values, *after):
    count = len(values)
    return run(
        wait_all_body,
        [shape(v.shape, v.dtype) for v in values],
        values,
        in_specs=[ANY] * count,
        out_specs=[ANY] * count,
        after=after,
        limit=4,
        us=0.3,
        aliases={i: i for i in range(count)},
    )


def hold_body(value_ref, out_ref, sem):
    copy = pltpu.make_async_copy(value_ref, out_ref, sem)
    copy.start()
    copy.wait()


def hold(value, *after):
    return run(
        hold_body,
        [shape(value.shape, value.dtype)],
        [value],
        in_specs=[ANY],
        out_specs=[ANY],
        scratch=[pltpu.SemaphoreType.DMA(())],
        after=after,
        limit=4,
    )[0]


def on_device(
    block_input,
    in_proj,
    out_proj,
    gate_proj,
    up_proj,
    down_proj,
    norm_one,
    norm_two,
    conv_kernel,
    out_cotangent,
):
    shards = lax.axis_size("fsdp")
    blocks = lax.axis_size("seq")
    f = lax.axis_index("fsdp")
    c = lax.axis_index("dp")
    z = lax.axis_index("seq")
    others = range(1, shards)
    seqs, length, width = block_input.shape
    rows = seqs * length
    group = shards * rows
    part = in_proj.shape[0]
    hidden = down_proj.shape[0]
    taps = conv_kernel.shape[0]
    rim = taps - 1
    edge = 16
    half_part = part // 2
    half = width // 2
    slab = width // (blocks * 2 * shards)
    tile = 512
    h_steps = pl.cdiv(hidden, tile)
    d_steps = width // tile
    chunk = half // blocks
    place = jnp.stack([f, c, z % 2]).astype(jnp.int32)
    SMEM = pl.BlockSpec(memory_space=pltpu.SMEM)
    VMEM = pl.BlockSpec(memory_space=pltpu.VMEM)

    def send_tokens(local):
        return [swap(local, "fsdp", k) for k in others]

    def turn(all_ref, own, keep_ref, send_ref):
        for h in range(2):
            value = all_ref[:, h * half : (h + 1) * half].T

            @pl.when(own == h)
            def _():
                keep_ref[...] = value

            @pl.when(own != h)
            def _():
                send_ref[...] = value

    def pack(pieces, after=()):
        count = len(pieces)

        def body(*refs):
            got, out_ref, sems = refs[:count], refs[count], refs[count + 1]
            copies = [pltpu.make_async_copy(got[i], out_ref.at[i], sems.at[i]) for i in range(count)]
            for copy in copies:
                copy.start()
            for copy in copies:
                copy.wait()

        return run(
            body,
            [shape((count, *pieces[0].shape))],
            pieces,
            in_specs=[ANY] * count,
            out_specs=[VMEM],
            scratch=[pltpu.SemaphoreType.DMA((count,))],
            after=after,
            limit=6,
        )[0]

    def assemble(own, parts, after=(), out=shape, out_spec=VMEM, limit=14):
        planes, columns = parts[0][0].shape[1], parts[0][0].shape[3]
        count = len(others)
        arrays = [p for p, _ in parts]
        starts = jnp.stack([f] + [h for _, h in parts]).astype(jnp.int32)

        def body(place_ref, own_ref, *refs):
            got, out_ref, sems = refs[: len(arrays)], refs[-2], refs[-1]
            f_ = place_ref[0]
            copies = []
            for p in range(planes):
                row = pl.ds(pl.multiple_of(f_ * part, part), part)
                if own.ndim == 3:
                    copies.append(pltpu.make_async_copy(own_ref.at[p], out_ref.at[p, row], sems.at[len(copies)]))
                else:
                    for t in range(columns // part):
                        source = own_ref.at[:, pl.ds(pl.multiple_of(t * width + f_ * part, part), part)]
                        target = out_ref.at[p, row, pl.ds(t * part, part)]
                        copies.append(pltpu.make_async_copy(source, target, sems.at[len(copies)]))
                for j, ref in enumerate(got):
                    size = ref.shape[2]
                    for i, k in enumerate(others):
                        start = pl.multiple_of((f_ ^ k) * part + place_ref[1 + j], size)
                        target = out_ref.at[p, pl.ds(start, size)]
                        copies.append(pltpu.make_async_copy(ref.at[i, p], target, sems.at[len(copies)]))
            for copy in copies:
                copy.start()
            for copy in copies:
                copy.wait()

        return run(
            body,
            [out((planes, width, columns))],
            [starts, own, *arrays],
            in_specs=[SMEM] + [ANY] * (1 + len(arrays)),
            out_specs=[out_spec],
            scratch=[pltpu.SemaphoreType.DMA((planes * (4 + len(arrays) * count),))],
            after=after,
            limit=limit,
        )[0]

    quarter = half_part // 2
    here, there = (z % 2) * quarter, (1 - z % 2) * quarter

    def in_body(place_ref, w_ref, *refs):
        outs, sems = refs[: len(others)], refs[-1]
        copies = []
        first = pl.multiple_of(place_ref[1] * half_part + place_ref[2] * quarter, quarter)
        for i, k in enumerate(others):
            for t in range(3):
                start = pl.multiple_of(t * width + (place_ref[0] ^ k) * part, part)
                source = w_ref.at[pl.ds(first, quarter), pl.ds(start, part)]
                target = outs[i].at[:, pl.ds(t * part, part)]
                copies.append(pltpu.make_async_copy(source, target, sems.at[i * 3 + t]))
        for copy in copies:
            copy.start()
        for copy in copies:
            copy.wait()

    in_sent = run(
        in_body,
        [shape((quarter, 3 * part))] * len(others),
        [place, in_far(in_proj)],
        in_specs=[SMEM, ANY],
        out_specs=[VMEM] * len(others),
        scratch=[pltpu.SemaphoreType.DMA((3 * len(others),))],
    )
    in_got = [swap(m, "fsdp", k) for m, k in zip(in_sent, others)]

    x_local = block_input.reshape(rows, width)
    cot_local = out_cotangent.reshape(rows, width)
    tail = shifted(x_local[rows - edge :], "seq", 1)
    small = jnp.concatenate([norm_one[None], norm_two[None], conv_kernel], axis=0)
    small = jnp.pad(small, ((0, edge - taps - 2), (0, 0)))

    def join_body(x_ref, t_ref, small_ref, out_ref):
        out_ref[:rows] = x_ref[...]
        out_ref[rows:] = t_ref[...]
        row = lax.broadcasted_iota(jnp.int32, (edge, part), 0)
        out_ref[rows:, :part] = jnp.where(row < taps + 2, small_ref[...], t_ref[:, :part])

    (message,) = run(join_body, [shape((rows + edge, width))], [x_local, tail, small])
    messages = [message] + send_tokens(message)
    taps_own = conv_kernel.astype(f32)

    in_mine = pack(in_got, (message,))
    in_next = swap(in_mine, "seq", 1)

    def both_piece(j, start, size):
        return jnp.stack(
            [lax.dynamic_slice(weight, (start, j * hidden), (size, hidden)) for weight in (gate_proj, up_proj)]
        )

    both_sent = [both_piece(f ^ k, c * half_part + here, quarter) for k in others]
    both_sent = wait_all(both_sent, *in_got)
    both_got = [swap(piece, "fsdp", k) for piece, k in zip(both_sent, others)]

    def norm_body(place_ref, *refs):
        xs, (n_ref, nh_ref, gain_ref) = refs[:shards], refs[shards:]
        for s in range(shards):
            pick = xs[0][rows:, :part]
            for k in others:
                pick = jnp.where((place_ref[0] ^ k) == s, xs[k][rows:, :part], pick)
            gain_ref[:, s * part : (s + 1) * part] = pick[:8].astype(f32)
        gain = gain_ref[0:1]

        def normed(v):
            v = v.astype(f32)
            r = lax.rsqrt(jnp.mean(v * v, axis=-1, keepdims=True) + epsilon)
            return (v * r * gain).astype(bf16)

        for k in range(shards):
            n_ref[k * rows : (k + 1) * rows] = normed(xs[k][:rows])
            nh_ref[k * edge : (k + 1) * edge] = normed(xs[k][rows:])

    normed_one, normed_edge, gains = run(
        norm_body,
        [shape((group, width)), shape((shards * edge, width)), shape((8, width), f32)],
        [place, *[in_far(m) for m in messages]],
        in_specs=[SMEM] + [whole(m) for m in messages],
        after=(in_mine,),
        us=2,
    )

    both_mine = pack(both_got, (normed_one, in_next))
    both_next = swap(both_mine, "seq", 1)
    w_in = assemble(
        in_far(in_proj),
        [
            (in_mine[:, None], c * half_part + here),
            (in_next[:, None], c * half_part + there),
            (swap(in_mine, "dp", 1)[:, None], (1 - c) * half_part + here),
            (swap(in_next, "dp", 1)[:, None], (1 - c) * half_part + there),
        ],
        (both_mine,),
    )[0]

    cot_held = hold(cot_local, both_mine)
    cot_blocks = [cot_held] + send_tokens(cot_held)

    def mixer_body(n_ref, nh_ref, taps_ref, w_ref, o_ref, proj_ref, edge_ref, gated_ref, *refs):
        p_refs, (ph_ref, ext_ref) = refs[:shards], refs[shards:]
        for t in range(3):
            cols = slice(t * part, (t + 1) * part)
            w = w_ref[:, cols]
            proj_ref[:, cols] = mm(n_ref[...], w)
            if t != 1:
                ph_ref[:, cols] = mm(nh_ref[...], w)
        edge_ref[...] = ph_ref[:, :part] * ph_ref[:, 2 * part :]
        for k in range(shards):
            r = slice(k * rows, (k + 1) * rows)
            ext_ref[:edge] = edge_ref[k * edge : (k + 1) * edge]
            ext_ref[edge:] = proj_ref[r, :part] * proj_ref[r, 2 * part :]
            conv = taps_ref[rim : rim + 1] * ext_ref[edge:]
            for t in range(rim):
                conv = conv + taps_ref[t : t + 1] * ext_ref[edge - rim + t : edge - rim + t + rows]
            gated_ref[r] = (proj_ref[r, part : 2 * part] * conv).astype(bf16)
        for t in range(width // 512):
            cols = slice(t * 512, (t + 1) * 512)
            o = mm(gated_ref[...], o_ref[:, cols]).astype(bf16)
            for k in range(shards):
                p_refs[k][:, cols] = o[k * rows : (k + 1) * rows]

    projected, edge_product, gated, *mix_parts = run(
        mixer_body,
        [
            shape((group, 3 * part), f32),
            shape((shards * edge, part), f32),
            shape((group, part)),
        ]
        + [shape((rows, width))] * shards,
        [normed_one, normed_edge, taps_own, w_in, out_proj],
        scratch=[pltpu.VMEM((shards * edge, 3 * part), f32), pltpu.VMEM((edge + rows, part), f32)],
        after=(cot_held,),
        us=5.5,
        limit=6,
    )

    def cot_body(place_ref, *refs):
        blocks_, (down_ref, dh_ref, keep_ref, send_ref, all_ref) = refs[:shards], refs[shards:]

        @pl.when(pl.program_id(0) == 0)
        def _():
            for k in range(shards):
                all_ref[k * rows : (k + 1) * rows] = blocks_[k][...]
            turn(all_ref, place_ref[1], keep_ref, send_ref)

        dh_ref[...] = mm_t(all_ref[...], down_ref[...])

    d_hidden, cot_keep, cot_send = run(
        cot_body,
        [shape((group, hidden), f32), far((half, group)), far((half, group))],
        [place, *cot_blocks, in_far(down_proj)],
        grid=(h_steps,),
        in_specs=[SMEM] + [whole(b) for b in cot_blocks] + [tiles((tile, width), 0)],
        out_specs=[tiles((group, tile), 1), whole(shape((half, group))), whole(shape((half, group)))],
        scratch=[pltpu.VMEM((group, width), bf16)],
        after=(gated,),
        us=5,
        limit=14,
    )

    cot_come = swap(cot_send, "dp", 1)
    mix_got = [swap(mix_parts[k], "fsdp", k) for k in others]

    def second_body(*refs):
        parts, x_ref, gain_ref, s_ref, n_ref = refs[:shards], *refs[shards:]
        total = x_ref[...].astype(f32)
        for p in parts:
            total = total + p[...].astype(f32)
        s_ref[...] = total
        r = lax.rsqrt(jnp.mean(total * total, axis=-1, keepdims=True) + epsilon)
        n_ref[...] = (total * r * gain_ref[1:2]).astype(bf16)

    second, normed_two = run(
        second_body,
        [shape((rows, width), f32), shape((rows, width))],
        [mix_parts[0], *mix_got, x_local, gains],
        after=(d_hidden,),
    )
    two_blocks = [normed_two] + send_tokens(normed_two)

    both_next = wait_for(both_next, normed_two)
    w_both = assemble(
        both_piece(f, 0, part),
        [
            (both_mine, c * half_part + here),
            (both_next, c * half_part + there),
            (swap(both_mine, "dp", 1), (1 - c) * half_part + here),
            (swap(both_next, "dp", 1), (1 - c) * half_part + there),
        ],
        (normed_two,),
        limit=16,
    )
    turned = shape((half, group))

    def turn_two_body(place_ref, *refs):
        blocks_, (all_ref, keep_ref, send_ref) = refs[:shards], refs[shards:]
        for k in range(shards):
            all_ref[k * rows : (k + 1) * rows] = blocks_[k][...]
        turn(all_ref, place_ref[1], keep_ref, send_ref)

    two_all, two_keep, two_send = run(
        turn_two_body,
        [shape((group, width)), turned, turned],
        [place, *two_blocks],
        in_specs=[SMEM] + [whole(b) for b in two_blocks],
        after=(w_both,),
    )
    two_come = swap(two_send, "dp", 1)

    def feed_body(all_ref, w_ref, dh_ref, du_ref, dg_ref, h_ref):
        gate = mm(all_ref[...], w_ref[0])
        upward = mm(all_ref[...], w_ref[1])
        s = jax.nn.sigmoid(gate)
        dh = dh_ref[...]
        du_ref[...] = (dh * (gate * s)).astype(bf16).reshape(du_ref.shape)
        dg_ref[...] = (dh * upward * s * (1.0 + gate * (1.0 - s))).astype(bf16).reshape(du_ref.shape)
        h_ref[...] = (gate * s * upward).astype(bf16).reshape(du_ref.shape)

    bundle = 32
    units = (group // bundle, bundle, hidden)
    unit_tiles = tiles((group // bundle, bundle, tile), 2)
    d_up, d_gate, hidden_all = run(
        feed_body,
        [far(units)] * 3,
        [two_all, w_both, d_hidden],
        grid=(h_steps,),
        in_specs=[whole(two_all), tiles((2, width, tile), 2), tiles((group, tile), 1)],
        out_specs=[unit_tiles] * 3,
        after=(two_come,),
        us=10,
        limit=24,
    )
    d_up_come = swap(d_up, "dp", 1)
    d_gate_come = swap(d_gate, "dp", 1)
    hidden_come = swap(hidden_all, "dp", 1)

    def flat(ref):
        return ref[...].reshape(group, ref.shape[2])

    def up_sum_body(own_ref, come_ref, du_ref, duc_ref, out_ref):
        total = mm(own_ref[...], flat(du_ref)) + mm(come_ref[...], flat(duc_ref))
        out_ref[...] = total.astype(bf16).reshape(blocks, chunk, tile)

    (up_both,) = run(
        up_sum_body,
        [shape((blocks, chunk, hidden))],
        [two_keep, two_come, d_up, d_up_come],
        grid=(h_steps,),
        in_specs=[whole(turned), whole(turned), unit_tiles, unit_tiles],
        out_specs=[tiles((blocks, chunk, tile), 2)],
        us=5,
        limit=14,
        hbm=True,
        near=(0, 1, 3),
    )
    up_sum = lax.psum_scatter(up_both, "seq", scatter_dimension=0, tiled=True).reshape(chunk, hidden)

    def back_two_body(dg_ref, du_ref, wg_ref, wu_ref, *p_refs):
        d = (mm_t(flat(dg_ref), wg_ref[...]) + mm_t(flat(du_ref), wu_ref[...])).astype(bf16)
        for k in range(shards):
            p_refs[k][...] = d[k * rows : (k + 1) * rows]

    back_two = run(
        back_two_body,
        [shape((rows, width))] * shards,
        [d_gate, d_up, w_both, w_both],
        grid=(d_steps,),
        in_specs=[
            whole(d_gate),
            whole(d_up),
            pl.BlockSpec((None, tile, hidden), lambda step: (0, step, 0)),
            pl.BlockSpec((None, tile, hidden), lambda step: (1, step, 0)),
        ],
        out_specs=[tiles((rows, tile), 1)] * shards,
        us=7,
        limit=16,
        hbm=True,
    )
    back_two_got = [swap(back_two[k], "fsdp", k) for k in others]

    def two_sum_body(own_ref, come_ref, cot_own_ref, cot_come_ref, dg_ref, dgc_ref, h_ref, hc_ref, out_ref):
        total = mm(own_ref[...], flat(dg_ref)) + mm(come_ref[...], flat(dgc_ref))
        out_ref[:, 0] = total.astype(bf16).reshape(blocks, chunk, tile)
        total = mm(cot_own_ref[...], flat(h_ref)) + mm(cot_come_ref[...], flat(hc_ref))
        out_ref[:, 1] = total.astype(bf16).reshape(blocks, chunk, tile)

    (two_both,) = run(
        two_sum_body,
        [shape((blocks, 2, chunk, hidden))],
        [two_keep, two_come, cot_keep, cot_come, d_gate, d_gate_come, hidden_all, hidden_come],
        grid=(h_steps,),
        in_specs=[whole(turned)] * 4 + [unit_tiles] * 4,
        out_specs=[tiles((blocks, 2, chunk, tile), 3)],
        after=(back_two[0],),
        us=10,
        limit=20,
        hbm=True,
        near=(0, 1, 2, 3, 5, 7),
    )

    def second_grad_body(*refs):
        parts, (s_ref, cot_ref, gain_ref, d_ref, mix_ref, term_ref) = refs[:shards], refs[shards:]
        dn = parts[0][...].astype(f32)
        for p in parts[1:]:
            dn = dn + p[...].astype(f32)
        s = s_ref[...]
        r = lax.rsqrt(jnp.mean(s * s, axis=-1, keepdims=True) + epsilon)
        term_ref[...] = jnp.sum(dn * s * r, axis=0, keepdims=True)
        a = dn * gain_ref[1:2]
        d = cot_ref[...].astype(f32) + r * a - s * (r * r * r) * jnp.mean(a * s, axis=-1, keepdims=True)
        d_ref[...] = d
        mix_ref[...] = d.astype(bf16)

    d_second, d_mix, two_term = run(
        second_grad_body,
        [shape((rows, width), f32), shape((rows, width)), shape((1, width), f32)],
        [back_two[0], *back_two_got, second, cot_local, gains],
        after=(two_both,),
    )
    mix_blocks = [d_mix] + send_tokens(d_mix)

    two_both = wait_for(two_both, up_sum, d_mix, keep=True)
    two_sum = lax.psum_scatter(two_both, "seq", scatter_dimension=0, tiled=True)
    two_sum = two_sum.reshape(2, chunk, hidden)

    runs = part // (shards * slab)
    channels = part // shards

    def owner_body(place_ref, g_ref, *out_refs):
        row = lax.broadcasted_iota(jnp.int32, (part, channels), 0)
        col = lax.broadcasted_iota(jnp.int32, (part, channels), 1)
        for k in range(shards):
            source = (col // slab) * (shards * slab) + (place_ref[0] ^ k) * slab + col % slab
            out_refs[k][...] = mm(g_ref[...], (row == source).astype(bf16)).astype(bf16)

    owner = run(
        owner_body,
        [shape((group, channels))] * shards,
        [place, gated],
        in_specs=[SMEM, whole(gated)],
        after=(two_both,),
    )
    owner_got = [owner[0]] + [swap(owner[k], "fsdp", k) for k in others]

    def gated_grad_body(*refs):
        blocks_, (o_ref, proj_ref, edge_ref, taps_ref) = refs[:shards], refs[shards : shards + 4]
        all_ref, dc_ref, dconv_ref, head_ref, term_ref, ext_ref = refs[shards + 4 :]
        for k in range(shards):
            all_ref[k * rows : (k + 1) * rows] = blocks_[k][...]
        dg = mm_t(all_ref[...], o_ref[...])
        dconv_ref[...] = dg * proj_ref[:, part : 2 * part]
        terms = [jnp.zeros((1, part), f32)] * taps
        for k in range(shards):
            r = slice(k * rows, (k + 1) * rows)
            d = dconv_ref[r]
            head_ref[k * 8 : (k + 1) * 8] = d[:8]
            ext_ref[:edge] = edge_ref[k * edge : (k + 1) * edge]
            ext_ref[edge:] = proj_ref[r, :part] * proj_ref[r, 2 * part :]
            conv = jnp.zeros((rows, part), f32)
            for t in range(taps):
                e = ext_ref[edge - rim + t : edge - rim + t + rows]
                conv = conv + taps_ref[t : t + 1] * e
                terms[t] = terms[t] + jnp.sum(d * e, axis=0, keepdims=True)
            dc_ref[r] = (dg[k * rows : (k + 1) * rows] * conv).astype(bf16)
        for t in range(taps):
            term_ref[t : t + 1] = terms[t]

    mix_all, d_c, d_conv, heads, tap_terms = run(
        gated_grad_body,
        [
            shape((group, width)),
            shape((group, part)),
            shape((group, part), f32),
            shape((shards * 8, part), f32),
            shape((taps, part), f32),
        ],
        [*mix_blocks, out_proj, projected, edge_product, taps_own],
        scratch=[pltpu.VMEM((edge + rows, part), f32)],
    )
    behind = shifted(heads, "seq", -1)

    def turn_body(place_ref, n_ref, *refs):
        got, (nt_ref, ot_ref) = refs[:shards], refs[shards:]
        for h in range(2):
            nt_ref[h] = n_ref[:, h * half : (h + 1) * half].T
        row = lax.broadcasted_iota(jnp.int32, (channels, part), 0)
        col = lax.broadcasted_iota(jnp.int32, (channels, part), 1)
        for b in range(shards):
            both = jnp.zeros((rows, part), f32)
            for k in range(shards):
                spread = (col == row + (place_ref[0] ^ k) * channels).astype(bf16)
                both = both + mm(got[k][(b ^ k) * rows : ((b ^ k) + 1) * rows], spread)
            both = both.astype(bf16)
            for h in range(2):
                wide = both[:, h * (part // 2) : (h + 1) * (part // 2)]
                ot_ref[h, :, b * rows : (b + 1) * rows] = wide.astype(f32).T.astype(bf16)

    one_turned, own_turned = run(
        turn_body,
        [shape((2, half, group)), shape((2, part // 2, group))],
        [place, normed_one, *owner_got],
        in_specs=[SMEM, whole(normed_one)] + [whole(o) for o in owner_got],
        after=(mix_blocks[0],),
    )

    def projected_grad_body(
        place_ref, dconv_ref, behind_ref, taps_ref, proj_ref, dc_ref, nt_ref, ot_ref, mix_ref,
        dp_ref, in_ref, out_ref, ext_ref,
    ):
        other = 1 - place_ref[1]
        for k in range(shards):
            r = slice(k * rows, (k + 1) * rows)
            ext_ref[:rows] = dconv_ref[r]
            ext_ref[rows:] = behind_ref[k * 8 : (k + 1) * 8]
            d = taps_ref[rim : rim + 1] * ext_ref[:rows]
            for t in range(rim):
                d = d + taps_ref[t : t + 1] * ext_ref[rim - t : rim - t + rows]
            dp_ref[r, :part] = (d * proj_ref[r, 2 * part :]).astype(bf16)
            dp_ref[r, part : 2 * part] = dc_ref[r]
            dp_ref[r, 2 * part :] = (d * proj_ref[r, :part]).astype(bf16)
        for t in range(3):
            cols = slice(t * part, (t + 1) * part)
            in_ref[:, :, cols] = mm(nt_ref[other], dp_ref[:, cols]).astype(bf16).reshape(blocks, chunk, part)
        for t in range(width // 512):
            cols = slice(t * 512, (t + 1) * 512)
            out_ref[:, cols] = mm(ot_ref[other], mix_ref[:, cols]).astype(bf16)

    d_projected, in_there, out_there = run(
        projected_grad_body,
        [shape((group, 3 * part)), shape((blocks, chunk, 3 * part)), shape((part // 2, width))],
        [place, d_conv, behind, taps_own, projected, d_c, one_turned, own_turned, mix_all],
        in_specs=[SMEM] + [whole(a) for a in (d_conv, behind, taps_own, projected, d_c, one_turned, own_turned, mix_all)],
        scratch=[pltpu.VMEM((rows + 8, part), f32)],
        us=3,
    )
    in_come = swap(in_there, "dp", 1)
    out_come = swap(out_there, "dp", 1)

    def back_one_body(dp_ref, w_ref, *p_refs):
        d = mm_t(dp_ref[...], w_ref[...]).astype(bf16)
        for k in range(shards):
            p_refs[k][...] = d[k * rows : (k + 1) * rows]

    back_one = run(
        back_one_body,
        [shape((rows, width))] * shards,
        [d_projected, w_in],
        grid=(d_steps,),
        in_specs=[whole(d_projected), tiles((tile, 3 * part), 0)],
        out_specs=[tiles((rows, tile), 1)] * shards,
        us=4,
        limit=14,
        hbm=True,
    )
    back_one_got = [swap(back_one[k], "fsdp", k) for k in others]

    def mixer_sum_body(place_ref, nt_ref, dp_ref, in_come_ref, ot_ref, mix_ref, out_come_ref, in_ref, out_ref):
        own = place_ref[1]
        for t in range(3):
            cols = slice(t * part, (t + 1) * part)
            here = mm(nt_ref[own], dp_ref[:, cols]).reshape(blocks, chunk, part)
            in_ref[:, :, cols] = (here + in_come_ref[:, :, cols].astype(f32)).astype(bf16)
        for t in range(width // 512):
            cols = slice(t * 512, (t + 1) * 512)
            here = mm(ot_ref[own], mix_ref[:, cols])
            out_ref[:, cols] = (here + out_come_ref[:, cols].astype(f32)).astype(bf16)

    in_both, out_both = run(
        mixer_sum_body,
        [shape((blocks, chunk, 3 * part)), shape((part // 2, width))],
        [place, one_turned, d_projected, in_come, own_turned, mix_all, out_come],
        in_specs=[SMEM]
        + [whole(a) for a in (one_turned, d_projected, in_come, own_turned, mix_all, out_come)],
        after=(back_one[0],),
    )

    def final_body(h_ref, w_ref, *p_refs):
        d = mm(flat(h_ref), w_ref[...]).astype(bf16)
        for k in range(shards):
            p_refs[k][...] = d[k * rows : (k + 1) * rows]

    final_parts = run(
        final_body,
        [shape((rows, width))] * shards,
        [hidden_all, in_far(down_proj)],
        grid=(d_steps,),
        in_specs=[whole(hidden_all), tiles((hidden, tile), 1)],
        out_specs=[tiles((rows, tile), 1)] * shards,
        after=(in_both,),
        us=4,
        limit=14,
        hbm=True,
    )

    final_got = [swap(final_parts[k], "fsdp", k) for k in others]
    total = second + final_parts[0].astype(f32)
    for piece in final_got:
        total = total + piece.astype(f32)
    block_output = total.astype(bf16).reshape(seqs, length, width)

    def own_rows(k):
        return lax.dynamic_slice_in_dim(out_both, (z ^ k) * slab, slab, 0)

    out_got = [own_rows(0)] + [swap(own_rows(k), "seq", k) for k in range(1, blocks)]

    def out_sum_body(*refs):
        total = refs[0][...].astype(f32)
        for ref in refs[1:-1]:
            total = total + ref[...].astype(f32)
        refs[-1][...] = total

    (out_grad,) = run(out_sum_body, [shape((slab, width), f32)], out_got)

    def input_grad_body(*refs):
        parts, (x_ref, d_ref, gain_ref, out_ref, term_ref) = refs[:shards], refs[shards:]
        dn = parts[0][...].astype(f32)
        for p in parts[1:]:
            dn = dn + p[...].astype(f32)
        x = x_ref[...].astype(f32)
        r = lax.rsqrt(jnp.mean(x * x, axis=-1, keepdims=True) + epsilon)
        term_ref[...] = jnp.sum(dn * x * r, axis=0, keepdims=True)
        a = dn * gain_ref[0:1]
        out_ref[...] = d_ref[...] + r * a - x * (r * r * r) * jnp.mean(a * x, axis=-1, keepdims=True)

    input_grad, one_term = run(
        input_grad_body,
        [shape((rows, width), f32), shape((1, width), f32)],
        [back_one[0], *back_one_got, x_local, d_second, gains],
        after=(in_both,),
    )
    input_grad = input_grad.reshape(seqs, length, width)

    spread_taps = [jnp.where(f == s, tap_terms, 0.0) for s in range(shards)]
    terms = jnp.concatenate([one_term, two_term, jnp.concatenate(spread_taps, axis=1)], axis=0)
    terms = sum_everywhere(terms)
    own = lax.dynamic_slice_in_dim(terms, ((c * blocks + z) * shards + f) * slab, slab, 1)

    def spread_rows(reduced, dims, put):
        parts = [lax.dynamic_slice_in_dim(reduced, f * slab, slab, 0)]
        parts += [swap(lax.dynamic_slice_in_dim(reduced, (f ^ k) * slab, slab, 0), "fsdp", k) for k in others]

        def body(place_ref, *refs):
            got, out_ref = refs[:shards], refs[shards]
            for s in range(shards):
                pick = got[0][...].astype(f32)
                for k in others:
                    pick = jnp.where((place_ref[0] ^ k) == s, got[k][...].astype(f32), pick)
                put(out_ref, s, pick)

        return run(body, [shape(dims, f32)], [place, *parts], in_specs=[SMEM] + [whole(p) for p in parts])[0]

    def put_columns(out_ref, s, value):
        out_ref[:, s * hidden : (s + 1) * hidden] = value

    def put_streams(out_ref, s, value):
        for t in range(3):
            out_ref[:, t * width + s * part : t * width + (s + 1) * part] = value[:, t * part : (t + 1) * part]

    up_grad = spread_rows(up_sum, (slab, shards * hidden), put_columns)
    in_both = wait_for(in_both, two_sum, input_grad, block_output, up_grad, out_grad, keep=True)
    in_sum = lax.psum_scatter(in_both, "seq", scatter_dimension=0, tiled=True)
    in_sum = in_sum.reshape(chunk, 3 * part)

    gate_grad = spread_rows(two_sum[0], (slab, shards * hidden), put_columns)
    down_rows = spread_rows(two_sum[1], (slab, shards * hidden), put_columns)
    down_grad = jnp.transpose(down_rows)
    in_sum = wait_for(in_sum, gate_grad, down_rows, terms, keep=True)
    in_grad = spread_rows(in_sum, (slab, 3 * width), put_streams)
    return (
        block_output,
        input_grad,
        in_grad,
        out_grad,
        gate_grad,
        up_grad,
        down_grad,
        own[0],
        own[1],
        own[2:],
    )


def solution(mesh):
    placed = (
        P(("dp", "fsdp"), "seq", None),
        P("fsdp", None),
        P("fsdp", None),
        P("fsdp", None),
        P("fsdp", None),
        P("fsdp", None),
        P("fsdp"),
        P("fsdp"),
        P(None, "fsdp"),
        P(("dp", "fsdp"), "seq", None),
    )
    return jax.shard_map(
        on_device,
        mesh=mesh,
        in_specs=placed,
        out_specs=(
            P(("dp", "fsdp"), "seq", None),
            P(("dp", "fsdp"), "seq", None),
            P(("dp", "seq", "fsdp"), None),
            P(("dp", "seq", "fsdp"), None),
            P(("dp", "seq", "fsdp"), None),
            P(("dp", "seq", "fsdp"), None),
            P(None, ("dp", "seq", "fsdp")),
            P(("dp", "seq", "fsdp")),
            P(("dp", "seq", "fsdp")),
            P(None, ("dp", "seq", "fsdp")),
        ),
        check_vma=False,
    )
```

```python
import math

import jax
import jax.numpy as jnp
from jax import lax
from jax.experimental import pallas as pl
from jax.experimental.pallas import tpu as pltpu
from jax.sharding import PartitionSpec as P

epsilon = 1e-05
f32 = jnp.float32
bf16 = jnp.bfloat16
MIB = 1 << 20
SCALE = 1e8
ANY = pl.BlockSpec(memory_space=pl.ANY)


def shape(dims, dtype=bf16):
    return jax.ShapeDtypeStruct(dims, dtype)


def far(dims, dtype=bf16):
    return pltpu.HBM(dims, dtype)


def in_far(value):
    return pltpu.with_memory_space_constraint(value, pltpu.HBM)


def whole(array):
    dims = array.shape
    return pl.BlockSpec(dims, lambda *steps: (0,) * len(dims), pipeline_mode=pl.Buffered(1))


def tiles(dims, axis):
    return pl.BlockSpec(dims, lambda step: tuple(step if i == axis else 0 for i in range(len(dims))))


def run(body, outs, ins, grid=(1,), in_specs=None, out_specs=None, scratch=(), after=(), limit=6, us=1.0, aliases=None, hbm=False, near=()):
    in_specs = [whole(a) for a in ins] if in_specs is None else in_specs
    out_specs = [whole(o) for o in outs] if out_specs is None else out_specs
    n, m = len(ins), len(after)
    if hbm:
        ins = [in_far(a) if a.size > 1024 and i not in near else a for i, a in enumerate(ins)]
        outs = [far(o.shape, o.dtype) if math.prod(o.shape) > 1024 else o for o in outs]

    def kernel(*refs):
        body(*refs[:n], *refs[n + m :])

    return pl.pallas_call(
        kernel,
        out_shape=tuple(outs),
        grid=grid,
        in_specs=list(in_specs) + [ANY] * m,
        out_specs=tuple(out_specs),
        scratch_shapes=list(scratch),
        compiler_params=pltpu.CompilerParams(vmem_limit_bytes=limit * MIB),
        cost_estimate=pl.CostEstimate(flops=int(us * SCALE), bytes_accessed=1000, transcendentals=0),
        input_output_aliases=aliases or {},
    )(*ins, *after)


def mm(a, b):
    return lax.dot_general(a, b, (((1,), (0,)), ((), ())), preferred_element_type=f32)


def mm_t(a, b):
    return lax.dot_general(a, b, (((1,), (1,)), ((), ())), preferred_element_type=f32)


def swap(value, axis, k):
    return lax.ppermute(value, axis, [(i, i ^ k) for i in range(lax.axis_size(axis))])


def shifted(block, axis, distance):
    devices = range(lax.axis_size(axis))
    route = [(i - distance, i) for i in devices if i - distance in devices]
    return lax.ppermute(block, axis, route)


def sum_over(value, axis, after=()):
    size = lax.axis_size(axis)
    if after:
        value = wait_for(value, *after)
    if size <= 4:
        return sum((swap(value, axis, k) for k in range(1, size)), value)
    k = 1
    while k < size:
        value = value + swap(value, axis, k)
        k *= 2
    return value


def wait_body(value_ref, out_ref):
    pass


def wait_for(value, *after, keep=False):
    return run(
        wait_body,
        [far(value.shape, value.dtype) if keep else shape(value.shape, value.dtype)],
        [in_far(value) if keep else value],
        in_specs=[ANY],
        out_specs=[ANY],
        after=after,
        limit=4,
        us=0.3,
        aliases={0: 0},
    )[0]


def wait_all_body(*refs):
    pass


def wait_all(values, *after):
    count = len(values)
    return run(
        wait_all_body,
        [shape(v.shape, v.dtype) for v in values],
        values,
        in_specs=[ANY] * count,
        out_specs=[ANY] * count,
        after=after,
        limit=4,
        us=0.3,
        aliases={i: i for i in range(count)},
    )


def hold_body(value_ref, out_ref, sem):
    copy = pltpu.make_async_copy(value_ref, out_ref, sem)
    copy.start()
    copy.wait()


def hold(value, *after):
    return run(
        hold_body,
        [shape(value.shape, value.dtype)],
        [value],
        in_specs=[ANY],
        out_specs=[ANY],
        scratch=[pltpu.SemaphoreType.DMA(())],
        after=after,
        limit=4,
    )[0]


def on_device(
    block_input,
    in_proj,
    out_proj,
    gate_proj,
    up_proj,
    down_proj,
    norm_one,
    norm_two,
    conv_kernel,
    out_cotangent,
):
    shards = lax.axis_size("fsdp")
    blocks = lax.axis_size("seq")
    f = lax.axis_index("fsdp")
    c = lax.axis_index("dp")
    z = lax.axis_index("seq")
    others = range(1, shards)
    seqs, length, width = block_input.shape
    rows = seqs * length
    group = shards * rows
    part = in_proj.shape[0]
    hidden = down_proj.shape[0]
    taps = conv_kernel.shape[0]
    rim = taps - 1
    edge = 16
    half_part = part // 2
    half = width // 2
    slab = width // (blocks * 2 * shards)
    tile = 512
    h_steps = pl.cdiv(hidden, tile)
    d_steps = width // tile
    chunk = half // blocks
    place = jnp.stack([f, c, z % 2]).astype(jnp.int32)
    SMEM = pl.BlockSpec(memory_space=pltpu.SMEM)
    VMEM = pl.BlockSpec(memory_space=pltpu.VMEM)

    def send_tokens(local):
        return [swap(local, "fsdp", k) for k in others]

    def turn(all_ref, own, keep_ref, send_ref):
        for h in range(2):
            value = all_ref[:, h * half : (h + 1) * half].T

            @pl.when(own == h)
            def _():
                keep_ref[...] = value

            @pl.when(own != h)
            def _():
                send_ref[...] = value

    def pack(pieces, after=()):
        count = len(pieces)

        def body(*refs):
            got, out_ref, sems = refs[:count], refs[count], refs[count + 1]
            copies = [pltpu.make_async_copy(got[i], out_ref.at[i], sems.at[i]) for i in range(count)]
            for copy in copies:
                copy.start()
            for copy in copies:
                copy.wait()

        return run(
            body,
            [shape((count, *pieces[0].shape))],
            pieces,
            in_specs=[ANY] * count,
            out_specs=[VMEM],
            scratch=[pltpu.SemaphoreType.DMA((count,))],
            after=after,
            limit=6,
        )[0]

    def assemble(own, parts, after=(), out=shape, out_spec=VMEM, limit=14):
        planes, columns = parts[0][0].shape[1], parts[0][0].shape[3]
        count = len(others)
        arrays = [p for p, _ in parts]
        starts = jnp.stack([f] + [h for _, h in parts]).astype(jnp.int32)

        def body(place_ref, own_ref, *refs):
            got, out_ref, sems = refs[: len(arrays)], refs[-2], refs[-1]
            f_ = place_ref[0]
            copies = []
            for p in range(planes):
                row = pl.ds(pl.multiple_of(f_ * part, part), part)
                if own.ndim == 3:
                    copies.append(pltpu.make_async_copy(own_ref.at[p], out_ref.at[p, row], sems.at[len(copies)]))
                else:
                    for t in range(columns // part):
                        source = own_ref.at[:, pl.ds(pl.multiple_of(t * width + f_ * part, part), part)]
                        target = out_ref.at[p, row, pl.ds(t * part, part)]
                        copies.append(pltpu.make_async_copy(source, target, sems.at[len(copies)]))
                for j, ref in enumerate(got):
                    size = ref.shape[2]
                    for i, k in enumerate(others):
                        start = pl.multiple_of((f_ ^ k) * part + place_ref[1 + j], size)
                        target = out_ref.at[p, pl.ds(start, size)]
                        copies.append(pltpu.make_async_copy(ref.at[i, p], target, sems.at[len(copies)]))
            for copy in copies:
                copy.start()
            for copy in copies:
                copy.wait()

        return run(
            body,
            [out((planes, width, columns))],
            [starts, own, *arrays],
            in_specs=[SMEM] + [ANY] * (1 + len(arrays)),
            out_specs=[out_spec],
            scratch=[pltpu.SemaphoreType.DMA((planes * (4 + len(arrays) * count),))],
            after=after,
            limit=limit,
        )[0]

    quarter = half_part // 2
    here, there = (z % 2) * quarter, (1 - z % 2) * quarter

    def in_body(place_ref, w_ref, *refs):
        outs, sems = refs[: len(others)], refs[-1]
        copies = []
        first = pl.multiple_of(place_ref[1] * half_part + place_ref[2] * quarter, quarter)
        for i, k in enumerate(others):
            for t in range(3):
                start = pl.multiple_of(t * width + (place_ref[0] ^ k) * part, part)
                source = w_ref.at[pl.ds(first, quarter), pl.ds(start, part)]
                target = outs[i].at[:, pl.ds(t * part, part)]
                copies.append(pltpu.make_async_copy(source, target, sems.at[i * 3 + t]))
        for copy in copies:
            copy.start()
        for copy in copies:
            copy.wait()

    in_sent = run(
        in_body,
        [shape((quarter, 3 * part))] * len(others),
        [place, in_far(in_proj)],
        in_specs=[SMEM, ANY],
        out_specs=[VMEM] * len(others),
        scratch=[pltpu.SemaphoreType.DMA((3 * len(others),))],
    )
    in_got = [swap(m, "fsdp", k) for m, k in zip(in_sent, others)]

    x_local = block_input.reshape(rows, width)
    cot_local = out_cotangent.reshape(rows, width)
    tail = shifted(x_local[rows - edge :], "seq", 1)
    small = jnp.concatenate([norm_one[None], norm_two[None], conv_kernel], axis=0)
    small = jnp.pad(small, ((0, edge - taps - 2), (0, 0)))

    def join_body(x_ref, t_ref, small_ref, out_ref):
        out_ref[:rows] = x_ref[...]
        out_ref[rows:] = t_ref[...]
        row = lax.broadcasted_iota(jnp.int32, (edge, part), 0)
        out_ref[rows:, :part] = jnp.where(row < taps + 2, small_ref[...], t_ref[:, :part])

    (message,) = run(join_body, [shape((rows + edge, width))], [x_local, tail, small])
    messages = [message] + send_tokens(message)
    taps_own = conv_kernel.astype(f32)

    in_mine = pack(in_got, (message,))
    in_next = swap(in_mine, "seq", 1)

    def both_piece(j, start, size):
        return jnp.stack(
            [lax.dynamic_slice(weight, (start, j * hidden), (size, hidden)) for weight in (gate_proj, up_proj)]
        )

    both_sent = [both_piece(f ^ k, c * half_part + here, quarter) for k in others]
    both_sent = wait_all(both_sent, *in_got)
    both_got = [swap(piece, "fsdp", k) for piece, k in zip(both_sent, others)]

    def norm_body(place_ref, *refs):
        xs, (n_ref, nh_ref, gain_ref) = refs[:shards], refs[shards:]
        for s in range(shards):
            pick = xs[0][rows:, :part]
            for k in others:
                pick = jnp.where((place_ref[0] ^ k) == s, xs[k][rows:, :part], pick)
            gain_ref[:, s * part : (s + 1) * part] = pick[:8].astype(f32)
        gain = gain_ref[0:1]

        def normed(v):
            v = v.astype(f32)
            r = lax.rsqrt(jnp.mean(v * v, axis=-1, keepdims=True) + epsilon)
            return (v * r * gain).astype(bf16)

        for k in range(shards):
            n_ref[k * rows : (k + 1) * rows] = normed(xs[k][:rows])
            nh_ref[k * edge : (k + 1) * edge] = normed(xs[k][rows:])

    normed_one, normed_edge, gains = run(
        norm_body,
        [shape((group, width)), shape((shards * edge, width)), shape((8, width), f32)],
        [place, *[in_far(m) for m in messages]],
        in_specs=[SMEM] + [whole(m) for m in messages],
        after=(in_mine,),
        us=2,
    )

    both_mine = pack(both_got, (normed_one, in_next))
    both_next = swap(both_mine, "seq", 1)
    w_in = assemble(
        in_far(in_proj),
        [
            (in_mine[:, None], c * half_part + here),
            (in_next[:, None], c * half_part + there),
            (swap(in_mine, "dp", 1)[:, None], (1 - c) * half_part + here),
            (swap(in_next, "dp", 1)[:, None], (1 - c) * half_part + there),
        ],
        (both_mine,),
    )[0]

    cot_held = hold(cot_local, both_mine)
    cot_blocks = [cot_held] + send_tokens(cot_held)

    def mixer_body(n_ref, nh_ref, taps_ref, w_ref, o_ref, proj_ref, edge_ref, gated_ref, *refs):
        p_refs, (ph_ref, ext_ref) = refs[:shards], refs[shards:]
        for t in range(3):
            cols = slice(t * part, (t + 1) * part)
            w = w_ref[:, cols]
            proj_ref[:, cols] = mm(n_ref[...], w)
            if t != 1:
                ph_ref[:, cols] = mm(nh_ref[...], w)
        edge_ref[...] = ph_ref[:, :part] * ph_ref[:, 2 * part :]
        for k in range(shards):
            r = slice(k * rows, (k + 1) * rows)
            ext_ref[:edge] = edge_ref[k * edge : (k + 1) * edge]
            ext_ref[edge:] = proj_ref[r, :part] * proj_ref[r, 2 * part :]
            conv = taps_ref[rim : rim + 1] * ext_ref[edge:]
            for t in range(rim):
                conv = conv + taps_ref[t : t + 1] * ext_ref[edge - rim + t : edge - rim + t + rows]
            gated_ref[r] = (proj_ref[r, part : 2 * part] * conv).astype(bf16)
        for t in range(width // 512):
            cols = slice(t * 512, (t + 1) * 512)
            o = mm(gated_ref[...], o_ref[:, cols]).astype(bf16)
            for k in range(shards):
                p_refs[k][:, cols] = o[k * rows : (k + 1) * rows]

    projected, edge_product, gated, *mix_parts = run(
        mixer_body,
        [
            shape((group, 3 * part), f32),
            shape((shards * edge, part), f32),
            shape((group, part)),
        ]
        + [shape((rows, width))] * shards,
        [normed_one, normed_edge, taps_own, w_in, out_proj],
        scratch=[pltpu.VMEM((shards * edge, 3 * part), f32), pltpu.VMEM((edge + rows, part), f32)],
        after=(cot_held,),
        us=5.5,
        limit=6,
    )

    def cot_body(place_ref, *refs):
        blocks_, (down_ref, dh_ref, keep_ref, send_ref, all_ref) = refs[:shards], refs[shards:]

        @pl.when(pl.program_id(0) == 0)
        def _():
            for k in range(shards):
                all_ref[k * rows : (k + 1) * rows] = blocks_[k][...]
            turn(all_ref, place_ref[1], keep_ref, send_ref)

        dh_ref[...] = mm_t(all_ref[...], down_ref[...])

    d_hidden, cot_keep, cot_send = run(
        cot_body,
        [shape((group, hidden), f32), far((half, group)), far((half, group))],
        [place, *cot_blocks, in_far(down_proj)],
        grid=(h_steps,),
        in_specs=[SMEM] + [whole(b) for b in cot_blocks] + [tiles((tile, width), 0)],
        out_specs=[tiles((group, tile), 1), whole(shape((half, group))), whole(shape((half, group)))],
        scratch=[pltpu.VMEM((group, width), bf16)],
        after=(gated,),
        us=5,
        limit=14,
    )

    cot_come = swap(cot_send, "dp", 1)
    mix_got = [swap(mix_parts[k], "fsdp", k) for k in others]

    def second_body(*refs):
        parts, x_ref, gain_ref, s_ref, n_ref = refs[:shards], *refs[shards:]
        total = x_ref[...].astype(f32)
        for p in parts:
            total = total + p[...].astype(f32)
        s_ref[...] = total
        r = lax.rsqrt(jnp.mean(total * total, axis=-1, keepdims=True) + epsilon)
        n_ref[...] = (total * r * gain_ref[1:2]).astype(bf16)

    second, normed_two = run(
        second_body,
        [shape((rows, width), f32), shape((rows, width))],
        [mix_parts[0], *mix_got, x_local, gains],
        after=(d_hidden,),
    )
    two_blocks = [normed_two] + send_tokens(normed_two)

    both_next = wait_for(both_next, normed_two)
    w_both = assemble(
        both_piece(f, 0, part),
        [
            (both_mine, c * half_part + here),
            (both_next, c * half_part + there),
            (swap(both_mine, "dp", 1), (1 - c) * half_part + here),
            (swap(both_next, "dp", 1), (1 - c) * half_part + there),
        ],
        (normed_two,),
        limit=16,
    )
    turned = shape((half, group))

    def turn_two_body(place_ref, *refs):
        blocks_, (all_ref, keep_ref, send_ref) = refs[:shards], refs[shards:]
        for k in range(shards):
            all_ref[k * rows : (k + 1) * rows] = blocks_[k][...]
        turn(all_ref, place_ref[1], keep_ref, send_ref)

    two_all, two_keep, two_send = run(
        turn_two_body,
        [shape((group, width)), turned, turned],
        [place, *two_blocks],
        in_specs=[SMEM] + [whole(b) for b in two_blocks],
        after=(w_both,),
    )
    two_come = swap(two_send, "dp", 1)

    def feed_body(all_ref, w_ref, dh_ref, du_ref, dg_ref, h_ref):
        gate = mm(all_ref[...], w_ref[0])
        upward = mm(all_ref[...], w_ref[1])
        s = jax.nn.sigmoid(gate)
        dh = dh_ref[...]
        du_ref[...] = (dh * (gate * s)).astype(bf16).reshape(du_ref.shape)
        dg_ref[...] = (dh * upward * s * (1.0 + gate * (1.0 - s))).astype(bf16).reshape(du_ref.shape)
        h_ref[...] = (gate * s * upward).astype(bf16).reshape(du_ref.shape)

    bundle = 32
    units = (group // bundle, bundle, hidden)
    unit_tiles = tiles((group // bundle, bundle, tile), 2)
    d_up, d_gate, hidden_all = run(
        feed_body,
        [far(units)] * 3,
        [two_all, w_both, d_hidden],
        grid=(h_steps,),
        in_specs=[whole(two_all), tiles((2, width, tile), 2), tiles((group, tile), 1)],
        out_specs=[unit_tiles] * 3,
        after=(two_come,),
        us=10,
        limit=24,
    )
    d_up_come = swap(d_up, "dp", 1)
    d_gate_come = swap(d_gate, "dp", 1)
    hidden_come = swap(hidden_all, "dp", 1)

    def flat(ref):
        return ref[...].reshape(group, ref.shape[2])

    def up_sum_body(own_ref, come_ref, du_ref, duc_ref, out_ref):
        total = mm(own_ref[...], flat(du_ref)) + mm(come_ref[...], flat(duc_ref))
        out_ref[...] = total.astype(bf16).reshape(blocks, chunk, tile)

    (up_both,) = run(
        up_sum_body,
        [shape((blocks, chunk, hidden))],
        [two_keep, two_come, d_up, d_up_come],
        grid=(h_steps,),
        in_specs=[whole(turned), whole(turned), unit_tiles, unit_tiles],
        out_specs=[tiles((blocks, chunk, tile), 2)],
        us=5,
        limit=14,
        hbm=True,
        near=(0, 1, 3),
    )
    up_sum = lax.psum_scatter(up_both, "seq", scatter_dimension=0, tiled=True).reshape(chunk, hidden)

    def two_sum_body(own_ref, come_ref, cot_own_ref, cot_come_ref, dg_ref, dgc_ref, h_ref, hc_ref, out_ref):
        total = mm(own_ref[...], flat(dg_ref)) + mm(come_ref[...], flat(dgc_ref))
        out_ref[:, 0] = total.astype(bf16).reshape(blocks, chunk, tile)
        total = mm(cot_own_ref[...], flat(h_ref)) + mm(cot_come_ref[...], flat(hc_ref))
        out_ref[:, 1] = total.astype(bf16).reshape(blocks, chunk, tile)

    (two_both,) = run(
        two_sum_body,
        [shape((blocks, 2, chunk, hidden))],
        [two_keep, two_come, cot_keep, cot_come, d_gate, d_gate_come, hidden_all, hidden_come],
        grid=(h_steps,),
        in_specs=[whole(turned)] * 4 + [unit_tiles] * 4,
        out_specs=[tiles((blocks, 2, chunk, tile), 3)],
        after=(up_both,),
        us=10,
        limit=20,
        hbm=True,
        near=(0, 1, 2, 3, 5, 7),
    )
    two_sum = lax.psum_scatter(two_both, "seq", scatter_dimension=0, tiled=True)
    two_sum = two_sum.reshape(2, chunk, hidden)

    def back_two_body(dg_ref, du_ref, wg_ref, wu_ref, *p_refs):
        d = (mm_t(flat(dg_ref), wg_ref[...]) + mm_t(flat(du_ref), wu_ref[...])).astype(bf16)
        for k in range(shards):
            p_refs[k][...] = d[k * rows : (k + 1) * rows]

    back_two = run(
        back_two_body,
        [shape((rows, width))] * shards,
        [d_gate, d_up, w_both, w_both],
        grid=(d_steps,),
        in_specs=[
            whole(d_gate),
            whole(d_up),
            pl.BlockSpec((None, tile, hidden), lambda step: (0, step, 0)),
            pl.BlockSpec((None, tile, hidden), lambda step: (1, step, 0)),
        ],
        out_specs=[tiles((rows, tile), 1)] * shards,
        after=(two_both,),
        us=7,
        limit=16,
        hbm=True,
    )
    back_two_got = [swap(back_two[k], "fsdp", k) for k in others]

    def second_grad_body(*refs):
        parts, (s_ref, cot_ref, gain_ref, d_ref, mix_ref, term_ref) = refs[:shards], refs[shards:]
        dn = parts[0][...].astype(f32)
        for p in parts[1:]:
            dn = dn + p[...].astype(f32)
        s = s_ref[...]
        r = lax.rsqrt(jnp.mean(s * s, axis=-1, keepdims=True) + epsilon)
        term_ref[...] = jnp.sum(dn * s * r, axis=0, keepdims=True)
        a = dn * gain_ref[1:2]
        d = cot_ref[...].astype(f32) + r * a - s * (r * r * r) * jnp.mean(a * s, axis=-1, keepdims=True)
        d_ref[...] = d
        mix_ref[...] = d.astype(bf16)

    d_second, d_mix, two_term = run(
        second_grad_body,
        [shape((rows, width), f32), shape((rows, width)), shape((1, width), f32)],
        [back_two[0], *back_two_got, second, cot_local, gains],
    )
    mix_blocks = [d_mix] + send_tokens(d_mix)

    runs = part // (shards * slab)
    channels = part // shards

    def owner_body(place_ref, g_ref, *out_refs):
        row = lax.broadcasted_iota(jnp.int32, (part, channels), 0)
        col = lax.broadcasted_iota(jnp.int32, (part, channels), 1)
        for k in range(shards):
            source = (col // slab) * (shards * slab) + (place_ref[0] ^ k) * slab + col % slab
            out_refs[k][...] = mm(g_ref[...], (row == source).astype(bf16)).astype(bf16)

    owner = run(
        owner_body,
        [shape((group, channels))] * shards,
        [place, gated],
        in_specs=[SMEM, whole(gated)],
        after=(two_both,),
    )
    owner_got = [owner[0]] + [swap(owner[k], "fsdp", k) for k in others]

    def gated_grad_body(*refs):
        blocks_, (o_ref, proj_ref, edge_ref, taps_ref) = refs[:shards], refs[shards : shards + 4]
        all_ref, dc_ref, dconv_ref, head_ref, term_ref, ext_ref = refs[shards + 4 :]
        for k in range(shards):
            all_ref[k * rows : (k + 1) * rows] = blocks_[k][...]
        dg = mm_t(all_ref[...], o_ref[...])
        dconv_ref[...] = dg * proj_ref[:, part : 2 * part]
        terms = [jnp.zeros((1, part), f32)] * taps
        for k in range(shards):
            r = slice(k * rows, (k + 1) * rows)
            d = dconv_ref[r]
            head_ref[k * 8 : (k + 1) * 8] = d[:8]
            ext_ref[:edge] = edge_ref[k * edge : (k + 1) * edge]
            ext_ref[edge:] = proj_ref[r, :part] * proj_ref[r, 2 * part :]
            conv = jnp.zeros((rows, part), f32)
            for t in range(taps):
                e = ext_ref[edge - rim + t : edge - rim + t + rows]
                conv = conv + taps_ref[t : t + 1] * e
                terms[t] = terms[t] + jnp.sum(d * e, axis=0, keepdims=True)
            dc_ref[r] = (dg[k * rows : (k + 1) * rows] * conv).astype(bf16)
        for t in range(taps):
            term_ref[t : t + 1] = terms[t]

    mix_all, d_c, d_conv, heads, tap_terms = run(
        gated_grad_body,
        [
            shape((group, width)),
            shape((group, part)),
            shape((group, part), f32),
            shape((shards * 8, part), f32),
            shape((taps, part), f32),
        ],
        [*mix_blocks, out_proj, projected, edge_product, taps_own],
        scratch=[pltpu.VMEM((edge + rows, part), f32)],
    )
    behind = shifted(heads, "seq", -1)

    def turn_body(place_ref, n_ref, *refs):
        got, (nt_ref, ot_ref) = refs[:shards], refs[shards:]
        for h in range(2):
            nt_ref[h] = n_ref[:, h * half : (h + 1) * half].T
        row = lax.broadcasted_iota(jnp.int32, (channels, part), 0)
        col = lax.broadcasted_iota(jnp.int32, (channels, part), 1)
        for b in range(shards):
            both = jnp.zeros((rows, part), f32)
            for k in range(shards):
                spread = (col == row + (place_ref[0] ^ k) * channels).astype(bf16)
                both = both + mm(got[k][(b ^ k) * rows : ((b ^ k) + 1) * rows], spread)
            both = both.astype(bf16)
            for h in range(2):
                wide = both[:, h * (part // 2) : (h + 1) * (part // 2)]
                ot_ref[h, :, b * rows : (b + 1) * rows] = wide.astype(f32).T.astype(bf16)

    one_turned, own_turned = run(
        turn_body,
        [shape((2, half, group)), shape((2, part // 2, group))],
        [place, normed_one, *owner_got],
        in_specs=[SMEM, whole(normed_one)] + [whole(o) for o in owner_got],
        after=(mix_blocks[0],),
    )

    def projected_grad_body(
        place_ref, dconv_ref, behind_ref, taps_ref, proj_ref, dc_ref, nt_ref, ot_ref, mix_ref,
        dp_ref, in_ref, out_ref, ext_ref,
    ):
        other = 1 - place_ref[1]
        for k in range(shards):
            r = slice(k * rows, (k + 1) * rows)
            ext_ref[:rows] = dconv_ref[r]
            ext_ref[rows:] = behind_ref[k * 8 : (k + 1) * 8]
            d = taps_ref[rim : rim + 1] * ext_ref[:rows]
            for t in range(rim):
                d = d + taps_ref[t : t + 1] * ext_ref[rim - t : rim - t + rows]
            dp_ref[r, :part] = (d * proj_ref[r, 2 * part :]).astype(bf16)
            dp_ref[r, part : 2 * part] = dc_ref[r]
            dp_ref[r, 2 * part :] = (d * proj_ref[r, :part]).astype(bf16)
        for t in range(3):
            cols = slice(t * part, (t + 1) * part)
            in_ref[:, :, cols] = mm(nt_ref[other], dp_ref[:, cols]).astype(bf16).reshape(blocks, chunk, part)
        for t in range(width // 512):
            cols = slice(t * 512, (t + 1) * 512)
            out_ref[:, cols] = mm(ot_ref[other], mix_ref[:, cols]).astype(bf16)

    d_projected, in_there, out_there = run(
        projected_grad_body,
        [shape((group, 3 * part)), shape((blocks, chunk, 3 * part)), shape((part // 2, width))],
        [place, d_conv, behind, taps_own, projected, d_c, one_turned, own_turned, mix_all],
        in_specs=[SMEM] + [whole(a) for a in (d_conv, behind, taps_own, projected, d_c, one_turned, own_turned, mix_all)],
        scratch=[pltpu.VMEM((rows + 8, part), f32)],
        us=3,
    )
    in_come = swap(in_there, "dp", 1)
    out_come = swap(out_there, "dp", 1)

    def back_one_body(dp_ref, w_ref, *p_refs):
        d = mm_t(dp_ref[...], w_ref[...]).astype(bf16)
        for k in range(shards):
            p_refs[k][...] = d[k * rows : (k + 1) * rows]

    back_one = run(
        back_one_body,
        [shape((rows, width))] * shards,
        [d_projected, w_in],
        grid=(d_steps,),
        in_specs=[whole(d_projected), tiles((tile, 3 * part), 0)],
        out_specs=[tiles((rows, tile), 1)] * shards,
        us=4,
        limit=14,
        hbm=True,
    )
    back_one_got = [swap(back_one[k], "fsdp", k) for k in others]

    def mixer_sum_body(place_ref, nt_ref, dp_ref, in_come_ref, ot_ref, mix_ref, out_come_ref, in_ref, out_ref):
        own = place_ref[1]
        for t in range(3):
            cols = slice(t * part, (t + 1) * part)
            here = mm(nt_ref[own], dp_ref[:, cols]).reshape(blocks, chunk, part)
            in_ref[:, :, cols] = (here + in_come_ref[:, :, cols].astype(f32)).astype(bf16)
        for t in range(width // 512):
            cols = slice(t * 512, (t + 1) * 512)
            here = mm(ot_ref[own], mix_ref[:, cols])
            out_ref[:, cols] = (here + out_come_ref[:, cols].astype(f32)).astype(bf16)

    in_both, out_both = run(
        mixer_sum_body,
        [shape((blocks, chunk, 3 * part)), shape((blocks * slab, width))],
        [place, one_turned, d_projected, in_come, own_turned, mix_all, out_come],
        in_specs=[SMEM]
        + [whole(a) for a in (one_turned, d_projected, in_come, own_turned, mix_all, out_come)],
        after=(back_one[0],),
    )

    def final_body(h_ref, w_ref, *p_refs):
        d = mm(flat(h_ref), w_ref[...]).astype(bf16)
        for k in range(shards):
            p_refs[k][...] = d[k * rows : (k + 1) * rows]

    final_parts = run(
        final_body,
        [shape((rows, width))] * shards,
        [hidden_all, in_far(down_proj)],
        grid=(d_steps,),
        in_specs=[whole(hidden_all), tiles((hidden, tile), 1)],
        out_specs=[tiles((rows, tile), 1)] * shards,
        after=(in_both,),
        us=4,
        limit=14,
        hbm=True,
    )

    in_rows = in_both.reshape(blocks, shards, slab, 3 * part)

    def rows_for(k):
        return lax.dynamic_index_in_dim(in_rows, f ^ k, 1, keepdims=False)

    in_pieces = [rows_for(0)] + [swap(rows_for(k), "fsdp", k) for k in others]

    def place_body(place_ref, *refs):
        got, (o_ref, out_ref) = refs[:shards], refs[shards:]
        for s in range(shards):
            pick = got[0][...]
            for k in others:
                pick = jnp.where((place_ref[0] ^ k) == s, got[k][...], pick)
            for t in range(3):
                start = t * width + s * part
                out_ref[:, :, start : start + part] = pick[:, :, t * part : (t + 1) * part]
        out_ref[:, :, 3 * width :] = o_ref[...]

    (mix_both,) = run(
        place_body,
        [far((blocks, slab, 4 * width))],
        [place, *in_pieces, out_both.reshape(blocks, slab, width)],
        in_specs=[SMEM] + [VMEM] * (shards + 1),
        after=(final_parts[0],),
        limit=12,
    )
    mix_sum = lax.psum_scatter(mix_both, "seq", scatter_dimension=0, tiled=True).reshape(slab, 4 * width)

    def input_grad_body(*refs):
        parts, (x_ref, d_ref, gain_ref, out_ref, term_ref) = refs[:shards], refs[shards:]
        dn = parts[0][...].astype(f32)
        for p in parts[1:]:
            dn = dn + p[...].astype(f32)
        x = x_ref[...].astype(f32)
        r = lax.rsqrt(jnp.mean(x * x, axis=-1, keepdims=True) + epsilon)
        term_ref[...] = jnp.sum(dn * x * r, axis=0, keepdims=True)
        a = dn * gain_ref[0:1]
        out_ref[...] = d_ref[...] + r * a - x * (r * r * r) * jnp.mean(a * x, axis=-1, keepdims=True)

    input_grad, one_term = run(
        input_grad_body,
        [shape((rows, width), f32), shape((1, width), f32)],
        [back_one[0], *back_one_got, x_local, d_second, gains],
        after=(mix_both,),
    )
    input_grad = input_grad.reshape(seqs, length, width)


    two_sum = wait_for(two_sum, input_grad)
    up_rows = up_sum.reshape(1, shards, slab, hidden)
    two_rows = two_sum.reshape(2, shards, slab, hidden)

    def feed_rows(k):
        parts = [lax.dynamic_index_in_dim(r, f ^ k, 1, keepdims=False) for r in (up_rows, two_rows)]
        return jnp.concatenate(parts, axis=0)

    feed_pieces = [feed_rows(0)] + [swap(feed_rows(k), "fsdp", k) for k in others]

    final_got = [swap(final_parts[k], "fsdp", k) for k in others]
    final_got = wait_all(final_got, feed_pieces[0])
    total = second + final_parts[0].astype(f32)
    for piece in final_got:
        total = total + piece.astype(f32)
    block_output = total.astype(bf16).reshape(seqs, length, width)

    spread_taps = [jnp.where(f == s, tap_terms, 0.0) for s in range(shards)]
    terms = jnp.concatenate([one_term, two_term, jnp.concatenate(spread_taps, axis=1)], axis=0)
    terms = sum_over(sum_over(sum_over(terms, "dp"), "seq"), "fsdp", feed_pieces[1:])
    own = lax.dynamic_slice_in_dim(terms, ((c * blocks + z) * shards + f) * slab, slab, 1)

    def spread_body(place_ref, *refs):
        got, outs = refs[:shards], refs[shards:]
        for n in range(3):
            for s in range(shards):
                pick = got[0][n]
                for k in others:
                    pick = jnp.where((place_ref[0] ^ k) == s, got[k][n], pick)
                outs[n][:, s * hidden : (s + 1) * hidden] = pick.astype(f32)

    up_grad, gate_grad, down_rows = run(
        spread_body,
        [far((slab, shards * hidden), f32)] * 3,
        [place, *feed_pieces],
        in_specs=[SMEM] + [whole(p) for p in feed_pieces],
        limit=12,
    )
    down_grad = jnp.transpose(down_rows)

    def last_body(sum_ref, in_ref, out_ref):
        in_ref[...] = sum_ref[:, : 3 * width].astype(f32)
        out_ref[...] = sum_ref[:, 3 * width :].astype(f32)

    in_grad, out_grad = run(
        last_body, [far((slab, 3 * width), f32), far((slab, width), f32)], [mix_sum], after=(gate_grad, block_output, terms)
    )
    return (
        block_output,
        input_grad,
        in_grad,
        out_grad,
        gate_grad,
        up_grad,
        down_grad,
        own[0],
        own[1],
        own[2:],
    )


def solution(mesh):
    placed = (
        P(("dp", "fsdp"), "seq", None),
        P("fsdp", None),
        P("fsdp", None),
        P("fsdp", None),
        P("fsdp", None),
        P("fsdp", None),
        P("fsdp"),
        P("fsdp"),
        P(None, "fsdp"),
        P(("dp", "fsdp"), "seq", None),
    )
    return jax.shard_map(
        on_device,
        mesh=mesh,
        in_specs=placed,
        out_specs=(
            P(("dp", "fsdp"), "seq", None),
            P(("dp", "fsdp"), "seq", None),
            P(("dp", "seq", "fsdp"), None),
            P(("dp", "seq", "fsdp"), None),
            P(("dp", "seq", "fsdp"), None),
            P(("dp", "seq", "fsdp"), None),
            P(None, ("dp", "seq", "fsdp")),
            P(("dp", "seq", "fsdp")),
            P(("dp", "seq", "fsdp")),
            P(None, ("dp", "seq", "fsdp")),
        ),
        check_vma=False,
    )
```

```python
import math

import jax
import jax.numpy as jnp
from jax import lax
from jax.experimental import pallas as pl
from jax.experimental.pallas import tpu as pltpu
from jax.sharding import PartitionSpec as P

epsilon = 1e-05
f32 = jnp.float32
bf16 = jnp.bfloat16
MIB = 1 << 20
SCALE = 1e8
ANY = pl.BlockSpec(memory_space=pl.ANY)


def shape(dims, dtype=bf16):
    return jax.ShapeDtypeStruct(dims, dtype)


def far(dims, dtype=bf16):
    return pltpu.HBM(dims, dtype)


def in_far(value):
    return pltpu.with_memory_space_constraint(value, pltpu.HBM)


def whole(array):
    dims = array.shape
    return pl.BlockSpec(dims, lambda *steps: (0,) * len(dims), pipeline_mode=pl.Buffered(1))


def tiles(dims, axis):
    return pl.BlockSpec(dims, lambda step: tuple(step if i == axis else 0 for i in range(len(dims))))


def run(body, outs, ins, grid=(1,), in_specs=None, out_specs=None, scratch=(), after=(), limit=6, us=1.0, aliases=None, hbm=False, near=()):
    in_specs = [whole(a) for a in ins] if in_specs is None else in_specs
    out_specs = [whole(o) for o in outs] if out_specs is None else out_specs
    n, m = len(ins), len(after)
    if hbm:
        ins = [in_far(a) if a.size > 1024 and i not in near else a for i, a in enumerate(ins)]
        outs = [far(o.shape, o.dtype) if math.prod(o.shape) > 1024 else o for o in outs]

    def kernel(*refs):
        body(*refs[:n], *refs[n + m :])

    return pl.pallas_call(
        kernel,
        out_shape=tuple(outs),
        grid=grid,
        in_specs=list(in_specs) + [ANY] * m,
        out_specs=tuple(out_specs),
        scratch_shapes=list(scratch),
        compiler_params=pltpu.CompilerParams(vmem_limit_bytes=limit * MIB),
        cost_estimate=pl.CostEstimate(flops=int(us * SCALE), bytes_accessed=1000, transcendentals=0),
        input_output_aliases=aliases or {},
    )(*ins, *after)


def mm(a, b):
    return lax.dot_general(a, b, (((1,), (0,)), ((), ())), preferred_element_type=f32)


def mm_t(a, b):
    return lax.dot_general(a, b, (((1,), (1,)), ((), ())), preferred_element_type=f32)


def swap(value, axis, k):
    return lax.ppermute(value, axis, [(i, i ^ k) for i in range(lax.axis_size(axis))])


def shifted(block, axis, distance):
    devices = range(lax.axis_size(axis))
    route = [(i - distance, i) for i in devices if i - distance in devices]
    return lax.ppermute(block, axis, route)


def sum_over(value, axis, after=()):
    size = lax.axis_size(axis)
    if after:
        value = wait_for(value, *after)
    if size <= 4:
        return sum((swap(value, axis, k) for k in range(1, size)), value)
    k = 1
    while k < size:
        value = value + swap(value, axis, k)
        k *= 2
    return value


def wait_body(value_ref, out_ref):
    pass


def wait_for(value, *after, keep=False):
    return run(
        wait_body,
        [far(value.shape, value.dtype) if keep else shape(value.shape, value.dtype)],
        [in_far(value) if keep else value],
        in_specs=[ANY],
        out_specs=[ANY],
        after=after,
        limit=4,
        us=0.3,
        aliases={0: 0},
    )[0]


def wait_all_body(*refs):
    pass


def wait_all(values, *after):
    count = len(values)
    return run(
        wait_all_body,
        [shape(v.shape, v.dtype) for v in values],
        values,
        in_specs=[ANY] * count,
        out_specs=[ANY] * count,
        after=after,
        limit=4,
        us=0.3,
        aliases={i: i for i in range(count)},
    )


def hold_body(value_ref, out_ref, sem):
    copy = pltpu.make_async_copy(value_ref, out_ref, sem)
    copy.start()
    copy.wait()


def hold(value, *after):
    return run(
        hold_body,
        [shape(value.shape, value.dtype)],
        [value],
        in_specs=[ANY],
        out_specs=[ANY],
        scratch=[pltpu.SemaphoreType.DMA(())],
        after=after,
        limit=4,
    )[0]


def on_device(
    block_input,
    in_proj,
    out_proj,
    gate_proj,
    up_proj,
    down_proj,
    norm_one,
    norm_two,
    conv_kernel,
    out_cotangent,
):
    shards = lax.axis_size("fsdp")
    blocks = lax.axis_size("seq")
    f = lax.axis_index("fsdp")
    c = lax.axis_index("dp")
    z = lax.axis_index("seq")
    others = range(1, shards)
    seqs, length, width = block_input.shape
    rows = seqs * length
    group = shards * rows
    part = in_proj.shape[0]
    hidden = down_proj.shape[0]
    taps = conv_kernel.shape[0]
    rim = taps - 1
    edge = 16
    half_part = part // 2
    half = width // 2
    slab = width // (blocks * 2 * shards)
    tile = 512
    h_steps = pl.cdiv(hidden, tile)
    d_steps = width // tile
    chunk = half // blocks
    place = jnp.stack([f, c, z % 2]).astype(jnp.int32)
    SMEM = pl.BlockSpec(memory_space=pltpu.SMEM)
    VMEM = pl.BlockSpec(memory_space=pltpu.VMEM)

    def send_tokens(local):
        return [swap(local, "fsdp", k) for k in others]

    def turn(all_ref, own, keep_ref, send_ref):
        for h in range(2):
            value = all_ref[:, h * half : (h + 1) * half].T

            @pl.when(own == h)
            def _():
                keep_ref[...] = value

            @pl.when(own != h)
            def _():
                send_ref[...] = value

    def pack(pieces, after=()):
        count = len(pieces)

        def body(*refs):
            got, out_ref, sems = refs[:count], refs[count], refs[count + 1]
            copies = [pltpu.make_async_copy(got[i], out_ref.at[i], sems.at[i]) for i in range(count)]
            for copy in copies:
                copy.start()
            for copy in copies:
                copy.wait()

        return run(
            body,
            [shape((count, *pieces[0].shape))],
            pieces,
            in_specs=[ANY] * count,
            out_specs=[VMEM],
            scratch=[pltpu.SemaphoreType.DMA((count,))],
            after=after,
            limit=6,
        )[0]

    def assemble(own, parts, after=(), out=shape, out_spec=VMEM, limit=14):
        planes, columns = parts[0][0].shape[1], parts[0][0].shape[3]
        count = len(others)
        arrays = [p for p, _ in parts]
        starts = jnp.stack([f] + [h for _, h in parts]).astype(jnp.int32)

        def body(place_ref, own_ref, *refs):
            got, out_ref, sems = refs[: len(arrays)], refs[-2], refs[-1]
            f_ = place_ref[0]
            copies = []
            for p in range(planes):
                row = pl.ds(pl.multiple_of(f_ * part, part), part)
                if own.ndim == 3:
                    copies.append(pltpu.make_async_copy(own_ref.at[p], out_ref.at[p, row], sems.at[len(copies)]))
                else:
                    for t in range(columns // part):
                        source = own_ref.at[:, pl.ds(pl.multiple_of(t * width + f_ * part, part), part)]
                        target = out_ref.at[p, row, pl.ds(t * part, part)]
                        copies.append(pltpu.make_async_copy(source, target, sems.at[len(copies)]))
                for j, ref in enumerate(got):
                    size = ref.shape[2]
                    for i, k in enumerate(others):
                        start = pl.multiple_of((f_ ^ k) * part + place_ref[1 + j], size)
                        target = out_ref.at[p, pl.ds(start, size)]
                        copies.append(pltpu.make_async_copy(ref.at[i, p], target, sems.at[len(copies)]))
            for copy in copies:
                copy.start()
            for copy in copies:
                copy.wait()

        return run(
            body,
            [out((planes, width, columns))],
            [starts, own, *arrays],
            in_specs=[SMEM] + [ANY] * (1 + len(arrays)),
            out_specs=[out_spec],
            scratch=[pltpu.SemaphoreType.DMA((planes * (4 + len(arrays) * count),))],
            after=after,
            limit=limit,
        )[0]

    quarter = half_part // 2
    here, there = (z % 2) * quarter, (1 - z % 2) * quarter

    def in_body(place_ref, w_ref, *refs):
        outs, sems = refs[: len(others)], refs[-1]
        copies = []
        first = pl.multiple_of(place_ref[1] * half_part + place_ref[2] * quarter, quarter)
        for i, k in enumerate(others):
            for t in range(3):
                start = pl.multiple_of(t * width + (place_ref[0] ^ k) * part, part)
                source = w_ref.at[pl.ds(first, quarter), pl.ds(start, part)]
                target = outs[i].at[:, pl.ds(t * part, part)]
                copies.append(pltpu.make_async_copy(source, target, sems.at[i * 3 + t]))
        for copy in copies:
            copy.start()
        for copy in copies:
            copy.wait()

    in_sent = run(
        in_body,
        [shape((quarter, 3 * part))] * len(others),
        [place, in_far(in_proj)],
        in_specs=[SMEM, ANY],
        out_specs=[VMEM] * len(others),
        scratch=[pltpu.SemaphoreType.DMA((3 * len(others),))],
    )
    in_got = [swap(m, "fsdp", k) for m, k in zip(in_sent, others)]

    x_local = block_input.reshape(rows, width)
    cot_local = out_cotangent.reshape(rows, width)
    tail = shifted(x_local[rows - edge :], "seq", 1)
    small = jnp.concatenate([norm_one[None], norm_two[None], conv_kernel], axis=0)
    small = jnp.pad(small, ((0, edge - taps - 2), (0, 0)))

    def join_body(x_ref, t_ref, small_ref, out_ref):
        out_ref[:rows] = x_ref[...]
        out_ref[rows:] = t_ref[...]
        row = lax.broadcasted_iota(jnp.int32, (edge, part), 0)
        out_ref[rows:, :part] = jnp.where(row < taps + 2, small_ref[...], t_ref[:, :part])

    (message,) = run(join_body, [shape((rows + edge, width))], [x_local, tail, small])
    messages = [message] + send_tokens(message)
    taps_own = conv_kernel.astype(f32)

    in_mine = pack(in_got, (message,))
    in_next = swap(in_mine, "seq", 1)

    def both_piece(j, start, size):
        return jnp.stack(
            [lax.dynamic_slice(weight, (start, j * hidden), (size, hidden)) for weight in (gate_proj, up_proj)]
        )

    both_sent = [both_piece(f ^ k, c * half_part + here, quarter) for k in others]
    both_sent = wait_all(both_sent, *in_got)
    both_got = [swap(piece, "fsdp", k) for piece, k in zip(both_sent, others)]

    both_mine = pack(both_got, (in_next,))
    both_next = swap(both_mine, "seq", 1)

    def norm_body(place_ref, *refs):
        xs, (n_ref, nh_ref, gain_ref) = refs[:shards], refs[shards:]
        for s in range(shards):
            pick = xs[0][rows:, :part]
            for k in others:
                pick = jnp.where((place_ref[0] ^ k) == s, xs[k][rows:, :part], pick)
            gain_ref[:, s * part : (s + 1) * part] = pick[:8].astype(f32)
        gain = gain_ref[0:1]

        def normed(v):
            v = v.astype(f32)
            r = lax.rsqrt(jnp.mean(v * v, axis=-1, keepdims=True) + epsilon)
            return (v * r * gain).astype(bf16)

        for k in range(shards):
            n_ref[k * rows : (k + 1) * rows] = normed(xs[k][:rows])
            nh_ref[k * edge : (k + 1) * edge] = normed(xs[k][rows:])

    normed_one, normed_edge, gains = run(
        norm_body,
        [shape((group, width)), shape((shards * edge, width)), shape((8, width), f32)],
        [place, *[in_far(m) for m in messages]],
        in_specs=[SMEM] + [whole(m) for m in messages],
        after=(both_mine,),
        us=2,
    )

    w_in = assemble(
        in_far(in_proj),
        [
            (in_mine[:, None], c * half_part + here),
            (in_next[:, None], c * half_part + there),
            (swap(in_mine, "dp", 1)[:, None], (1 - c) * half_part + here),
            (swap(in_next, "dp", 1)[:, None], (1 - c) * half_part + there),
        ],
        (both_mine,),
    )[0]

    cot_held = hold(cot_local, both_mine)
    cot_blocks = [cot_held] + send_tokens(cot_held)

    def mixer_body(n_ref, nh_ref, taps_ref, w_ref, o_ref, proj_ref, edge_ref, gated_ref, *refs):
        p_refs, (ph_ref, ext_ref) = refs[:shards], refs[shards:]
        for t in range(3):
            cols = slice(t * part, (t + 1) * part)
            w = w_ref[:, cols]
            proj_ref[:, cols] = mm(n_ref[...], w)
            if t != 1:
                ph_ref[:, cols] = mm(nh_ref[...], w)
        edge_ref[...] = ph_ref[:, :part] * ph_ref[:, 2 * part :]
        for k in range(shards):
            r = slice(k * rows, (k + 1) * rows)
            ext_ref[:edge] = edge_ref[k * edge : (k + 1) * edge]
            ext_ref[edge:] = proj_ref[r, :part] * proj_ref[r, 2 * part :]
            conv = taps_ref[rim : rim + 1] * ext_ref[edge:]
            for t in range(rim):
                conv = conv + taps_ref[t : t + 1] * ext_ref[edge - rim + t : edge - rim + t + rows]
            gated_ref[r] = (proj_ref[r, part : 2 * part] * conv).astype(bf16)
        for t in range(width // 512):
            cols = slice(t * 512, (t + 1) * 512)
            o = mm(gated_ref[...], o_ref[:, cols]).astype(bf16)
            for k in range(shards):
                p_refs[k][:, cols] = o[k * rows : (k + 1) * rows]

    projected, edge_product, gated, *mix_parts = run(
        mixer_body,
        [
            shape((group, 3 * part), f32),
            shape((shards * edge, part), f32),
            shape((group, part)),
        ]
        + [shape((rows, width))] * shards,
        [normed_one, normed_edge, taps_own, w_in, out_proj],
        scratch=[pltpu.VMEM((shards * edge, 3 * part), f32), pltpu.VMEM((edge + rows, part), f32)],
        after=(cot_held,),
        us=5.5,
        limit=6,
    )

    def cot_body(place_ref, *refs):
        blocks_, (down_ref, dh_ref, keep_ref, send_ref, all_ref) = refs[:shards], refs[shards:]

        @pl.when(pl.program_id(0) == 0)
        def _():
            for k in range(shards):
                all_ref[k * rows : (k + 1) * rows] = blocks_[k][...]
            turn(all_ref, place_ref[1], keep_ref, send_ref)

        dh_ref[...] = mm_t(all_ref[...], down_ref[...])

    d_hidden, cot_keep, cot_send = run(
        cot_body,
        [shape((group, hidden), f32), far((half, group)), far((half, group))],
        [place, *cot_blocks, in_far(down_proj)],
        grid=(h_steps,),
        in_specs=[SMEM] + [whole(b) for b in cot_blocks] + [tiles((tile, width), 0)],
        out_specs=[tiles((group, tile), 1), whole(shape((half, group))), whole(shape((half, group)))],
        scratch=[pltpu.VMEM((group, width), bf16)],
        after=(gated,),
        us=5,
        limit=14,
    )

    cot_come = swap(cot_send, "dp", 1)
    mix_got = [swap(mix_parts[k], "fsdp", k) for k in others]

    def second_body(*refs):
        parts, x_ref, gain_ref, s_ref, n_ref = refs[:shards], *refs[shards:]
        total = x_ref[...].astype(f32)
        for p in parts:
            total = total + p[...].astype(f32)
        s_ref[...] = total
        r = lax.rsqrt(jnp.mean(total * total, axis=-1, keepdims=True) + epsilon)
        n_ref[...] = (total * r * gain_ref[1:2]).astype(bf16)

    second, normed_two = run(
        second_body,
        [shape((rows, width), f32), shape((rows, width))],
        [mix_parts[0], *mix_got, x_local, gains],
        after=(d_hidden,),
    )
    two_blocks = [normed_two] + send_tokens(normed_two)

    both_next = wait_for(both_next, normed_two)
    w_both = assemble(
        both_piece(f, 0, part),
        [
            (both_mine, c * half_part + here),
            (both_next, c * half_part + there),
            (swap(both_mine, "dp", 1), (1 - c) * half_part + here),
            (swap(both_next, "dp", 1), (1 - c) * half_part + there),
        ],
        (normed_two,),
        limit=16,
    )
    turned = shape((half, group))

    def turn_two_body(place_ref, *refs):
        blocks_, (all_ref, keep_ref, send_ref) = refs[:shards], refs[shards:]
        for k in range(shards):
            all_ref[k * rows : (k + 1) * rows] = blocks_[k][...]
        turn(all_ref, place_ref[1], keep_ref, send_ref)

    two_all, two_keep, two_send = run(
        turn_two_body,
        [shape((group, width)), turned, turned],
        [place, *two_blocks],
        in_specs=[SMEM] + [whole(b) for b in two_blocks],
        after=(w_both,),
    )
    two_come = swap(two_send, "dp", 1)

    def feed_body(all_ref, w_ref, dh_ref, du_ref, dg_ref, h_ref):
        gate = mm(all_ref[...], w_ref[0])
        upward = mm(all_ref[...], w_ref[1])
        s = jax.nn.sigmoid(gate)
        dh = dh_ref[...]
        du_ref[...] = (dh * (gate * s)).astype(bf16).reshape(du_ref.shape)
        dg_ref[...] = (dh * upward * s * (1.0 + gate * (1.0 - s))).astype(bf16).reshape(du_ref.shape)
        h_ref[...] = (gate * s * upward).astype(bf16).reshape(du_ref.shape)

    bundle = 32
    units = (group // bundle, bundle, hidden)
    unit_tiles = tiles((group // bundle, bundle, tile), 2)
    d_up, d_gate, hidden_all = run(
        feed_body,
        [far(units)] * 3,
        [two_all, w_both, d_hidden],
        grid=(h_steps,),
        in_specs=[whole(two_all), tiles((2, width, tile), 2), tiles((group, tile), 1)],
        out_specs=[unit_tiles] * 3,
        us=10,
        limit=24,
    )
    d_up = wait_for(d_up, two_come, keep=True)
    d_up_come = swap(d_up, "dp", 1)
    d_gate_come = swap(d_gate, "dp", 1)
    hidden_come = swap(hidden_all, "dp", 1)

    def flat(ref):
        return ref[...].reshape(group, ref.shape[2])

    def up_sum_body(own_ref, come_ref, du_ref, duc_ref, out_ref):
        total = mm(own_ref[...], flat(du_ref)) + mm(come_ref[...], flat(duc_ref))
        out_ref[...] = total.astype(bf16).reshape(blocks, chunk, tile)

    (up_both,) = run(
        up_sum_body,
        [shape((blocks, chunk, hidden))],
        [two_keep, two_come, d_up, d_up_come],
        grid=(h_steps,),
        in_specs=[whole(turned), whole(turned), unit_tiles, unit_tiles],
        out_specs=[tiles((blocks, chunk, tile), 2)],
        us=5,
        limit=14,
        hbm=True,
        near=(0, 1, 3),
    )
    up_sum = lax.psum_scatter(up_both, "seq", scatter_dimension=0, tiled=True).reshape(chunk, hidden)

    def two_sum_body(own_ref, come_ref, cot_own_ref, cot_come_ref, dg_ref, dgc_ref, h_ref, hc_ref, out_ref):
        total = mm(own_ref[...], flat(dg_ref)) + mm(come_ref[...], flat(dgc_ref))
        out_ref[:, 0] = total.astype(bf16).reshape(blocks, chunk, tile)
        total = mm(cot_own_ref[...], flat(h_ref)) + mm(cot_come_ref[...], flat(hc_ref))
        out_ref[:, 1] = total.astype(bf16).reshape(blocks, chunk, tile)

    (two_both,) = run(
        two_sum_body,
        [shape((blocks, 2, chunk, hidden))],
        [two_keep, two_come, cot_keep, cot_come, d_gate, d_gate_come, hidden_all, hidden_come],
        grid=(h_steps,),
        in_specs=[whole(turned)] * 4 + [unit_tiles] * 4,
        out_specs=[tiles((blocks, 2, chunk, tile), 3)],
        after=(up_both,),
        us=10,
        limit=20,
        hbm=True,
        near=(0, 1, 2, 3, 5, 7),
    )
    two_sum = lax.psum_scatter(two_both, "seq", scatter_dimension=0, tiled=True)
    two_sum = two_sum.reshape(2, chunk, hidden)

    def back_two_body(dg_ref, du_ref, wg_ref, wu_ref, *p_refs):
        d = (mm_t(flat(dg_ref), wg_ref[...]) + mm_t(flat(du_ref), wu_ref[...])).astype(bf16)
        for k in range(shards):
            p_refs[k][...] = d[k * rows : (k + 1) * rows]

    back_two = run(
        back_two_body,
        [shape((rows, width))] * shards,
        [d_gate, d_up, w_both, w_both],
        grid=(d_steps,),
        in_specs=[
            whole(d_gate),
            whole(d_up),
            pl.BlockSpec((None, tile, hidden), lambda step: (0, step, 0)),
            pl.BlockSpec((None, tile, hidden), lambda step: (1, step, 0)),
        ],
        out_specs=[tiles((rows, tile), 1)] * shards,
        after=(two_both,),
        us=7,
        limit=16,
        hbm=True,
    )
    back_two_got = [swap(back_two[k], "fsdp", k) for k in others]

    def second_grad_body(*refs):
        parts, (s_ref, cot_ref, gain_ref, d_ref, mix_ref, term_ref) = refs[:shards], refs[shards:]
        dn = parts[0][...].astype(f32)
        for p in parts[1:]:
            dn = dn + p[...].astype(f32)
        s = s_ref[...]
        r = lax.rsqrt(jnp.mean(s * s, axis=-1, keepdims=True) + epsilon)
        term_ref[...] = jnp.sum(dn * s * r, axis=0, keepdims=True)
        a = dn * gain_ref[1:2]
        d = cot_ref[...].astype(f32) + r * a - s * (r * r * r) * jnp.mean(a * s, axis=-1, keepdims=True)
        d_ref[...] = d
        mix_ref[...] = d.astype(bf16)

    d_second, d_mix, two_term = run(
        second_grad_body,
        [shape((rows, width), f32), shape((rows, width)), shape((1, width), f32)],
        [back_two[0], *back_two_got, second, cot_local, gains],
    )
    mix_blocks = [d_mix] + send_tokens(d_mix)

    runs = part // (shards * slab)
    channels = part // shards

    def owner_body(place_ref, g_ref, *out_refs):
        row = lax.broadcasted_iota(jnp.int32, (part, channels), 0)
        col = lax.broadcasted_iota(jnp.int32, (part, channels), 1)
        for k in range(shards):
            source = (col // slab) * (shards * slab) + (place_ref[0] ^ k) * slab + col % slab
            out_refs[k][...] = mm(g_ref[...], (row == source).astype(bf16)).astype(bf16)

    owner = run(
        owner_body,
        [shape((group, channels))] * shards,
        [place, gated],
        in_specs=[SMEM, whole(gated)],
        after=(two_both,),
    )
    owner_got = [owner[0]] + [swap(owner[k], "fsdp", k) for k in others]

    def gated_grad_body(*refs):
        blocks_, (o_ref, proj_ref, edge_ref, taps_ref) = refs[:shards], refs[shards : shards + 4]
        all_ref, dc_ref, dconv_ref, head_ref, term_ref, ext_ref = refs[shards + 4 :]
        for k in range(shards):
            all_ref[k * rows : (k + 1) * rows] = blocks_[k][...]
        dg = mm_t(all_ref[...], o_ref[...])
        dconv_ref[...] = dg * proj_ref[:, part : 2 * part]
        terms = [jnp.zeros((1, part), f32)] * taps
        for k in range(shards):
            r = slice(k * rows, (k + 1) * rows)
            d = dconv_ref[r]
            head_ref[k * 8 : (k + 1) * 8] = d[:8]
            ext_ref[:edge] = edge_ref[k * edge : (k + 1) * edge]
            ext_ref[edge:] = proj_ref[r, :part] * proj_ref[r, 2 * part :]
            conv = jnp.zeros((rows, part), f32)
            for t in range(taps):
                e = ext_ref[edge - rim + t : edge - rim + t + rows]
                conv = conv + taps_ref[t : t + 1] * e
                terms[t] = terms[t] + jnp.sum(d * e, axis=0, keepdims=True)
            dc_ref[r] = (dg[k * rows : (k + 1) * rows] * conv).astype(bf16)
        for t in range(taps):
            term_ref[t : t + 1] = terms[t]

    mix_all, d_c, d_conv, heads, tap_terms = run(
        gated_grad_body,
        [
            shape((group, width)),
            shape((group, part)),
            shape((group, part), f32),
            shape((shards * 8, part), f32),
            shape((taps, part), f32),
        ],
        [*mix_blocks, out_proj, projected, edge_product, taps_own],
        scratch=[pltpu.VMEM((edge + rows, part), f32)],
    )
    behind = shifted(heads, "seq", -1)

    def turn_body(place_ref, n_ref, *refs):
        got, (nt_ref, ot_ref) = refs[:shards], refs[shards:]
        for h in range(2):
            nt_ref[h] = n_ref[:, h * half : (h + 1) * half].T
        row = lax.broadcasted_iota(jnp.int32, (channels, part), 0)
        col = lax.broadcasted_iota(jnp.int32, (channels, part), 1)
        for b in range(shards):
            both = jnp.zeros((rows, part), f32)
            for k in range(shards):
                spread = (col == row + (place_ref[0] ^ k) * channels).astype(bf16)
                both = both + mm(got[k][(b ^ k) * rows : ((b ^ k) + 1) * rows], spread)
            both = both.astype(bf16)
            for h in range(2):
                wide = both[:, h * (part // 2) : (h + 1) * (part // 2)]
                ot_ref[h, :, b * rows : (b + 1) * rows] = wide.astype(f32).T.astype(bf16)

    one_turned, own_turned = run(
        turn_body,
        [shape((2, half, group)), shape((2, part // 2, group))],
        [place, normed_one, *owner_got],
        in_specs=[SMEM, whole(normed_one)] + [whole(o) for o in owner_got],
        after=(mix_blocks[0],),
    )

    def projected_grad_body(
        place_ref, dconv_ref, behind_ref, taps_ref, proj_ref, dc_ref, nt_ref, ot_ref, mix_ref,
        dp_ref, in_ref, out_ref, ext_ref,
    ):
        other = 1 - place_ref[1]
        for k in range(shards):
            r = slice(k * rows, (k + 1) * rows)
            ext_ref[:rows] = dconv_ref[r]
            ext_ref[rows:] = behind_ref[k * 8 : (k + 1) * 8]
            d = taps_ref[rim : rim + 1] * ext_ref[:rows]
            for t in range(rim):
                d = d + taps_ref[t : t + 1] * ext_ref[rim - t : rim - t + rows]
            dp_ref[r, :part] = (d * proj_ref[r, 2 * part :]).astype(bf16)
            dp_ref[r, part : 2 * part] = dc_ref[r]
            dp_ref[r, 2 * part :] = (d * proj_ref[r, :part]).astype(bf16)
        for t in range(3):
            cols = slice(t * part, (t + 1) * part)
            in_ref[:, :, cols] = mm(nt_ref[other], dp_ref[:, cols]).astype(bf16).reshape(blocks, chunk, part)
        for t in range(width // 512):
            cols = slice(t * 512, (t + 1) * 512)
            out_ref[:, cols] = mm(ot_ref[other], mix_ref[:, cols]).astype(bf16)

    d_projected, in_there, out_there = run(
        projected_grad_body,
        [shape((group, 3 * part)), shape((blocks, chunk, 3 * part)), shape((part // 2, width))],
        [place, d_conv, behind, taps_own, projected, d_c, one_turned, own_turned, mix_all],
        in_specs=[SMEM] + [whole(a) for a in (d_conv, behind, taps_own, projected, d_c, one_turned, own_turned, mix_all)],
        scratch=[pltpu.VMEM((rows + 8, part), f32)],
        us=3,
    )
    in_come = swap(in_there, "dp", 1)
    out_come = swap(out_there, "dp", 1)

    def back_one_body(dp_ref, w_ref, *p_refs):
        d = mm_t(dp_ref[...], w_ref[...]).astype(bf16)
        for k in range(shards):
            p_refs[k][...] = d[k * rows : (k + 1) * rows]

    back_one = run(
        back_one_body,
        [shape((rows, width))] * shards,
        [d_projected, w_in],
        grid=(d_steps,),
        in_specs=[whole(d_projected), tiles((tile, 3 * part), 0)],
        out_specs=[tiles((rows, tile), 1)] * shards,
        us=4,
        limit=14,
        hbm=True,
    )
    back_one_got = [swap(back_one[k], "fsdp", k) for k in others]

    def mixer_sum_body(place_ref, nt_ref, dp_ref, in_come_ref, ot_ref, mix_ref, out_come_ref, in_ref, out_ref):
        own = place_ref[1]
        for t in range(3):
            cols = slice(t * part, (t + 1) * part)
            here = mm(nt_ref[own], dp_ref[:, cols]).reshape(blocks, chunk, part)
            in_ref[:, :, cols] = (here + in_come_ref[:, :, cols].astype(f32)).astype(bf16)
        for t in range(width // 512):
            cols = slice(t * 512, (t + 1) * 512)
            here = mm(ot_ref[own], mix_ref[:, cols])
            out_ref[:, cols] = (here + out_come_ref[:, cols].astype(f32)).astype(bf16)

    in_both, out_both = run(
        mixer_sum_body,
        [shape((blocks, chunk, 3 * part)), shape((blocks * slab, width))],
        [place, one_turned, d_projected, in_come, own_turned, mix_all, out_come],
        in_specs=[SMEM]
        + [whole(a) for a in (one_turned, d_projected, in_come, own_turned, mix_all, out_come)],
        after=(back_one[0],),
    )

    def final_body(h_ref, w_ref, *p_refs):
        d = mm(flat(h_ref), w_ref[...]).astype(bf16)
        for k in range(shards):
            p_refs[k][...] = d[k * rows : (k + 1) * rows]

    final_parts = run(
        final_body,
        [shape((rows, width))] * shards,
        [hidden_all, in_far(down_proj)],
        grid=(d_steps,),
        in_specs=[whole(hidden_all), tiles((hidden, tile), 1)],
        out_specs=[tiles((rows, tile), 1)] * shards,
        after=(in_both,),
        us=4,
        limit=14,
        hbm=True,
    )

    in_rows = in_both.reshape(blocks, shards, slab, 3 * part)

    def rows_for(k):
        return lax.dynamic_index_in_dim(in_rows, f ^ k, 1, keepdims=False)

    in_pieces = [rows_for(0)] + [swap(rows_for(k), "fsdp", k) for k in others]

    def place_body(place_ref, *refs):
        got, (o_ref, out_ref) = refs[:shards], refs[shards:]
        for s in range(shards):
            pick = got[0][...]
            for k in others:
                pick = jnp.where((place_ref[0] ^ k) == s, got[k][...], pick)
            for t in range(3):
                start = t * width + s * part
                out_ref[:, :, start : start + part] = pick[:, :, t * part : (t + 1) * part]
        out_ref[:, :, 3 * width :] = o_ref[...]

    (mix_both,) = run(
        place_body,
        [far((blocks, slab, 4 * width))],
        [place, *in_pieces, out_both.reshape(blocks, slab, width)],
        in_specs=[SMEM] + [VMEM] * (shards + 1),
        after=(final_parts[0],),
        limit=12,
    )
    mix_sum = lax.psum_scatter(mix_both, "seq", scatter_dimension=0, tiled=True).reshape(slab, 4 * width)

    def input_grad_body(*refs):
        parts, (x_ref, d_ref, gain_ref, out_ref, term_ref) = refs[:shards], refs[shards:]
        dn = parts[0][...].astype(f32)
        for p in parts[1:]:
            dn = dn + p[...].astype(f32)
        x = x_ref[...].astype(f32)
        r = lax.rsqrt(jnp.mean(x * x, axis=-1, keepdims=True) + epsilon)
        term_ref[...] = jnp.sum(dn * x * r, axis=0, keepdims=True)
        a = dn * gain_ref[0:1]
        out_ref[...] = d_ref[...] + r * a - x * (r * r * r) * jnp.mean(a * x, axis=-1, keepdims=True)

    input_grad, one_term = run(
        input_grad_body,
        [shape((rows, width), f32), shape((1, width), f32)],
        [back_one[0], *back_one_got, x_local, d_second, gains],
        after=(mix_both,),
    )
    input_grad = input_grad.reshape(seqs, length, width)


    two_sum = wait_for(two_sum, input_grad)
    up_rows = up_sum.reshape(1, shards, slab, hidden)
    two_rows = two_sum.reshape(2, shards, slab, hidden)

    def feed_rows(k):
        parts = [lax.dynamic_index_in_dim(r, f ^ k, 1, keepdims=False) for r in (up_rows, two_rows)]
        return jnp.concatenate(parts, axis=0)

    feed_pieces = [feed_rows(0)] + [swap(feed_rows(k), "fsdp", k) for k in others]

    final_got = [swap(final_parts[k], "fsdp", k) for k in others]
    final_got = wait_all(final_got, feed_pieces[0])
    total = second + final_parts[0].astype(f32)
    for piece in final_got:
        total = total + piece.astype(f32)
    block_output = total.astype(bf16).reshape(seqs, length, width)

    spread_taps = [jnp.where(f == s, tap_terms, 0.0) for s in range(shards)]
    terms = jnp.concatenate([one_term, two_term, jnp.concatenate(spread_taps, axis=1)], axis=0)
    terms = sum_over(sum_over(sum_over(terms, "dp"), "seq"), "fsdp", feed_pieces[1:])
    own = lax.dynamic_slice_in_dim(terms, ((c * blocks + z) * shards + f) * slab, slab, 1)

    def spread_body(place_ref, *refs):
        got, outs = refs[:shards], refs[shards:]
        for n in range(3):
            for s in range(shards):
                pick = got[0][n]
                for k in others:
                    pick = jnp.where((place_ref[0] ^ k) == s, got[k][n], pick)
                outs[n][:, s * hidden : (s + 1) * hidden] = pick.astype(f32)

    up_grad, gate_grad, down_rows = run(
        spread_body,
        [far((slab, shards * hidden), f32)] * 3,
        [place, *feed_pieces],
        in_specs=[SMEM] + [whole(p) for p in feed_pieces],
        limit=12,
    )
    down_grad = jnp.transpose(down_rows)

    def last_body(sum_ref, in_ref, out_ref):
        in_ref[...] = sum_ref[:, : 3 * width].astype(f32)
        out_ref[...] = sum_ref[:, 3 * width :].astype(f32)

    in_grad, out_grad = run(
        last_body, [far((slab, 3 * width), f32), far((slab, width), f32)], [in_far(mix_sum)], after=(gate_grad, block_output, terms)
    )
    return (
        block_output,
        input_grad,
        in_grad,
        out_grad,
        gate_grad,
        up_grad,
        down_grad,
        own[0],
        own[1],
        own[2:],
    )


def solution(mesh):
    placed = (
        P(("dp", "fsdp"), "seq", None),
        P("fsdp", None),
        P("fsdp", None),
        P("fsdp", None),
        P("fsdp", None),
        P("fsdp", None),
        P("fsdp"),
        P("fsdp"),
        P(None, "fsdp"),
        P(("dp", "fsdp"), "seq", None),
    )
    return jax.shard_map(
        on_device,
        mesh=mesh,
        in_specs=placed,
        out_specs=(
            P(("dp", "fsdp"), "seq", None),
            P(("dp", "fsdp"), "seq", None),
            P(("dp", "seq", "fsdp"), None),
            P(("dp", "seq", "fsdp"), None),
            P(("dp", "seq", "fsdp"), None),
            P(("dp", "seq", "fsdp"), None),
            P(None, ("dp", "seq", "fsdp")),
            P(("dp", "seq", "fsdp")),
            P(("dp", "seq", "fsdp")),
            P(None, ("dp", "seq", "fsdp")),
        ),
        check_vma=False,
    )
```

```python
import math

import jax
import jax.numpy as jnp
from jax import lax
from jax.experimental import pallas as pl
from jax.experimental.pallas import tpu as pltpu
from jax.sharding import PartitionSpec as P

epsilon = 1e-05
f32 = jnp.float32
bf16 = jnp.bfloat16
MIB = 1 << 20
SCALE = 1e8
ANY = pl.BlockSpec(memory_space=pl.ANY)


def shape(dims, dtype=bf16):
    return jax.ShapeDtypeStruct(dims, dtype)


def far(dims, dtype=bf16):
    return pltpu.HBM(dims, dtype)


def in_far(value):
    return pltpu.with_memory_space_constraint(value, pltpu.HBM)


def whole(array):
    dims = array.shape
    return pl.BlockSpec(dims, lambda *steps: (0,) * len(dims), pipeline_mode=pl.Buffered(1))


def tiles(dims, axis):
    return pl.BlockSpec(dims, lambda step: tuple(step if i == axis else 0 for i in range(len(dims))))


def run(body, outs, ins, grid=(1,), in_specs=None, out_specs=None, scratch=(), after=(), limit=6, us=1.0, aliases=None, hbm=False, near=()):
    in_specs = [whole(a) for a in ins] if in_specs is None else in_specs
    out_specs = [whole(o) for o in outs] if out_specs is None else out_specs
    n, m = len(ins), len(after)
    if hbm:
        ins = [in_far(a) if a.size > 1024 and i not in near else a for i, a in enumerate(ins)]
        outs = [far(o.shape, o.dtype) if math.prod(o.shape) > 1024 else o for o in outs]

    def kernel(*refs):
        body(*refs[:n], *refs[n + m :])

    return pl.pallas_call(
        kernel,
        out_shape=tuple(outs),
        grid=grid,
        in_specs=list(in_specs) + [ANY] * m,
        out_specs=tuple(out_specs),
        scratch_shapes=list(scratch),
        compiler_params=pltpu.CompilerParams(vmem_limit_bytes=limit * MIB),
        cost_estimate=pl.CostEstimate(flops=int(us * SCALE), bytes_accessed=1000, transcendentals=0),
        input_output_aliases=aliases or {},
    )(*ins, *after)


def mm(a, b):
    return lax.dot_general(a, b, (((1,), (0,)), ((), ())), preferred_element_type=f32)


def mm_t(a, b):
    return lax.dot_general(a, b, (((1,), (1,)), ((), ())), preferred_element_type=f32)


def swap(value, axis, k):
    return lax.ppermute(value, axis, [(i, i ^ k) for i in range(lax.axis_size(axis))])


def shifted(block, axis, distance):
    devices = range(lax.axis_size(axis))
    route = [(i - distance, i) for i in devices if i - distance in devices]
    return lax.ppermute(block, axis, route)


def sum_over(value, axis, after=()):
    size = lax.axis_size(axis)
    if after:
        value = wait_for(value, *after)
    if size <= 4:
        return sum((swap(value, axis, k) for k in range(1, size)), value)
    k = 1
    while k < size:
        value = value + swap(value, axis, k)
        k *= 2
    return value


def wait_body(value_ref, out_ref):
    pass


def wait_for(value, *after, keep=False):
    return run(
        wait_body,
        [far(value.shape, value.dtype) if keep else shape(value.shape, value.dtype)],
        [in_far(value) if keep else value],
        in_specs=[ANY],
        out_specs=[ANY],
        after=after,
        limit=4,
        us=0.3,
        aliases={0: 0},
    )[0]


def wait_all_body(*refs):
    pass


def wait_all(values, *after):
    count = len(values)
    return run(
        wait_all_body,
        [shape(v.shape, v.dtype) for v in values],
        values,
        in_specs=[ANY] * count,
        out_specs=[ANY] * count,
        after=after,
        limit=4,
        us=0.3,
        aliases={i: i for i in range(count)},
    )


def hold_body(value_ref, out_ref, sem):
    copy = pltpu.make_async_copy(value_ref, out_ref, sem)
    copy.start()
    copy.wait()


def hold(value, *after):
    return run(
        hold_body,
        [shape(value.shape, value.dtype)],
        [value],
        in_specs=[ANY],
        out_specs=[ANY],
        scratch=[pltpu.SemaphoreType.DMA(())],
        after=after,
        limit=4,
    )[0]


def on_device(
    block_input,
    in_proj,
    out_proj,
    gate_proj,
    up_proj,
    down_proj,
    norm_one,
    norm_two,
    conv_kernel,
    out_cotangent,
):
    shards = lax.axis_size("fsdp")
    blocks = lax.axis_size("seq")
    f = lax.axis_index("fsdp")
    c = lax.axis_index("dp")
    z = lax.axis_index("seq")
    others = range(1, shards)
    seqs, length, width = block_input.shape
    rows = seqs * length
    group = shards * rows
    part = in_proj.shape[0]
    hidden = down_proj.shape[0]
    taps = conv_kernel.shape[0]
    rim = taps - 1
    edge = 16
    half_part = part // 2
    half = width // 2
    slab = width // (blocks * 2 * shards)
    tile = 512
    h_steps = pl.cdiv(hidden, tile)
    d_steps = width // tile
    chunk = half // blocks
    place = jnp.stack([f, c, z % 2]).astype(jnp.int32)
    SMEM = pl.BlockSpec(memory_space=pltpu.SMEM)
    VMEM = pl.BlockSpec(memory_space=pltpu.VMEM)

    def send_tokens(local):
        return [swap(local, "fsdp", k) for k in others]

    def turn(all_ref, own, keep_ref, send_ref):
        for h in range(2):
            value = all_ref[:, h * half : (h + 1) * half].T

            @pl.when(own == h)
            def _():
                keep_ref[...] = value

            @pl.when(own != h)
            def _():
                send_ref[...] = value

    def pack(pieces, after=()):
        count = len(pieces)

        def body(*refs):
            got, out_ref, sems = refs[:count], refs[count], refs[count + 1]
            copies = [pltpu.make_async_copy(got[i], out_ref.at[i], sems.at[i]) for i in range(count)]
            for copy in copies:
                copy.start()
            for copy in copies:
                copy.wait()

        return run(
            body,
            [shape((count, *pieces[0].shape))],
            pieces,
            in_specs=[ANY] * count,
            out_specs=[VMEM],
            scratch=[pltpu.SemaphoreType.DMA((count,))],
            after=after,
            limit=6,
        )[0]

    def assemble(own, parts, after=(), out=shape, out_spec=VMEM, limit=14):
        planes, columns = parts[0][0].shape[1], parts[0][0].shape[3]
        count = len(others)
        arrays = [p for p, _ in parts]
        starts = jnp.stack([f] + [h for _, h in parts]).astype(jnp.int32)

        def body(place_ref, own_ref, *refs):
            got, out_ref, sems = refs[: len(arrays)], refs[-2], refs[-1]
            f_ = place_ref[0]
            copies = []
            for p in range(planes):
                row = pl.ds(pl.multiple_of(f_ * part, part), part)
                if own.ndim == 3:
                    copies.append(pltpu.make_async_copy(own_ref.at[p], out_ref.at[p, row], sems.at[len(copies)]))
                else:
                    for t in range(columns // part):
                        source = own_ref.at[:, pl.ds(pl.multiple_of(t * width + f_ * part, part), part)]
                        target = out_ref.at[p, row, pl.ds(t * part, part)]
                        copies.append(pltpu.make_async_copy(source, target, sems.at[len(copies)]))
                for j, ref in enumerate(got):
                    size = ref.shape[2]
                    for i, k in enumerate(others):
                        start = pl.multiple_of((f_ ^ k) * part + place_ref[1 + j], size)
                        target = out_ref.at[p, pl.ds(start, size)]
                        copies.append(pltpu.make_async_copy(ref.at[i, p], target, sems.at[len(copies)]))
            for copy in copies:
                copy.start()
            for copy in copies:
                copy.wait()

        return run(
            body,
            [out((planes, width, columns))],
            [starts, own, *arrays],
            in_specs=[SMEM] + [VMEM] * (1 + len(arrays)),
            out_specs=[out_spec],
            scratch=[pltpu.SemaphoreType.DMA((planes * (4 + len(arrays) * count),))],
            after=after,
            limit=limit,
        )[0]

    quarter = half_part // 2
    here, there = (z % 2) * quarter, (1 - z % 2) * quarter

    def in_body(place_ref, w_ref, *refs):
        outs, sems = refs[: len(others)], refs[-1]
        copies = []
        first = pl.multiple_of(place_ref[1] * half_part + place_ref[2] * quarter, quarter)
        for i, k in enumerate(others):
            for t in range(3):
                start = pl.multiple_of(t * width + (place_ref[0] ^ k) * part, part)
                source = w_ref.at[pl.ds(first, quarter), pl.ds(start, part)]
                target = outs[i].at[:, pl.ds(t * part, part)]
                copies.append(pltpu.make_async_copy(source, target, sems.at[i * 3 + t]))
        for copy in copies:
            copy.start()
        for copy in copies:
            copy.wait()

    in_sent = run(
        in_body,
        [shape((quarter, 3 * part))] * len(others),
        [place, in_far(in_proj)],
        in_specs=[SMEM, ANY],
        out_specs=[VMEM] * len(others),
        scratch=[pltpu.SemaphoreType.DMA((3 * len(others),))],
    )
    in_got = [swap(m, "fsdp", k) for m, k in zip(in_sent, others)]

    x_local = block_input.reshape(rows, width)
    cot_local = out_cotangent.reshape(rows, width)
    tail = shifted(x_local[rows - edge :], "seq", 1)
    small = jnp.concatenate([norm_one[None], norm_two[None], conv_kernel], axis=0)
    small = jnp.pad(small, ((0, edge - taps - 2), (0, 0)))

    def join_body(x_ref, t_ref, small_ref, out_ref):
        out_ref[:rows] = x_ref[...]
        out_ref[rows:] = t_ref[...]
        row = lax.broadcasted_iota(jnp.int32, (edge, part), 0)
        out_ref[rows:, :part] = jnp.where(row < taps + 2, small_ref[...], t_ref[:, :part])

    (message,) = run(join_body, [shape((rows + edge, width))], [x_local, tail, small])
    messages = [message] + send_tokens(message)
    taps_own = conv_kernel.astype(f32)

    in_mine = pack(in_got, (message,))
    in_next = swap(in_mine, "seq", 1)

    def both_piece(j, start, size):
        return jnp.stack(
            [lax.dynamic_slice(weight, (start, j * hidden), (size, hidden)) for weight in (gate_proj, up_proj)]
        )

    both_sent = [both_piece(f ^ k, c * half_part + here, quarter) for k in others]
    both_sent = wait_all(both_sent, *in_got)
    both_got = [swap(piece, "fsdp", k) for piece, k in zip(both_sent, others)]

    both_mine = pack(both_got, (in_next,))
    both_next = swap(both_mine, "seq", 1)

    def norm_body(place_ref, *refs):
        xs, (n_ref, nh_ref, gain_ref) = refs[:shards], refs[shards:]
        for s in range(shards):
            pick = xs[0][rows:, :part]
            for k in others:
                pick = jnp.where((place_ref[0] ^ k) == s, xs[k][rows:, :part], pick)
            gain_ref[:, s * part : (s + 1) * part] = pick[:8].astype(f32)
        gain = gain_ref[0:1]

        def normed(v):
            v = v.astype(f32)
            r = lax.rsqrt(jnp.mean(v * v, axis=-1, keepdims=True) + epsilon)
            return (v * r * gain).astype(bf16)

        for k in range(shards):
            n_ref[k * rows : (k + 1) * rows] = normed(xs[k][:rows])
            nh_ref[k * edge : (k + 1) * edge] = normed(xs[k][rows:])

    normed_one, normed_edge, gains = run(
        norm_body,
        [shape((group, width)), shape((shards * edge, width)), shape((8, width), f32)],
        [place, *[in_far(m) for m in messages]],
        in_specs=[SMEM] + [whole(m) for m in messages],
        after=(both_mine,),
        us=2,
    )

    w_in = assemble(
        in_far(in_proj),
        [
            (in_mine[:, None], c * half_part + here),
            (in_next[:, None], c * half_part + there),
            (swap(in_mine, "dp", 1)[:, None], (1 - c) * half_part + here),
            (swap(in_next, "dp", 1)[:, None], (1 - c) * half_part + there),
        ],
        (both_mine,),
    )[0]

    cot_held = hold(cot_local, both_mine)
    cot_blocks = [cot_held] + send_tokens(cot_held)

    def mixer_body(n_ref, nh_ref, taps_ref, w_ref, o_ref, far_ref, edge_ref, gated_ref, *refs):
        p_refs, (ph_ref, ext_ref, proj_ref, sem) = refs[:shards], refs[shards:]
        for t in range(3):
            cols = slice(t * part, (t + 1) * part)
            w = w_ref[:, cols]
            proj_ref[:, cols] = mm(n_ref[...], w)
            if t != 1:
                ph_ref[:, cols] = mm(nh_ref[...], w)
        leave = pltpu.make_async_copy(proj_ref, far_ref, sem)
        leave.start()
        edge_ref[...] = ph_ref[:, :part] * ph_ref[:, 2 * part :]
        for k in range(shards):
            r = slice(k * rows, (k + 1) * rows)
            ext_ref[:edge] = edge_ref[k * edge : (k + 1) * edge]
            ext_ref[edge:] = proj_ref[r, :part] * proj_ref[r, 2 * part :]
            conv = taps_ref[rim : rim + 1] * ext_ref[edge:]
            for t in range(rim):
                conv = conv + taps_ref[t : t + 1] * ext_ref[edge - rim + t : edge - rim + t + rows]
            gated_ref[r] = (proj_ref[r, part : 2 * part] * conv).astype(bf16)
        for t in range(width // 512):
            cols = slice(t * 512, (t + 1) * 512)
            o = mm(gated_ref[...], o_ref[:, cols]).astype(bf16)
            for k in range(shards):
                p_refs[k][:, cols] = o[k * rows : (k + 1) * rows]
        leave.wait()

    projected, edge_product, gated, *mix_parts = run(
        mixer_body,
        [
            far((group, 3 * part), f32),
            shape((shards * edge, part), f32),
            shape((group, part)),
        ]
        + [shape((rows, width))] * shards,
        [normed_one, normed_edge, taps_own, w_in, out_proj],
        out_specs=[ANY, whole(shape((shards * edge, part))), whole(shape((group, part)))]
        + [whole(shape((rows, width)))] * shards,
        scratch=[
            pltpu.VMEM((shards * edge, 3 * part), f32),
            pltpu.VMEM((edge + rows, part), f32),
            pltpu.VMEM((group, 3 * part), f32),
            pltpu.SemaphoreType.DMA(()),
        ],
        after=(cot_held,),
        us=5.5,
        limit=10,
    )

    def cot_body(place_ref, *refs):
        blocks_, (down_ref, dh_ref, keep_ref, send_ref, all_ref) = refs[:shards], refs[shards:]

        @pl.when(pl.program_id(0) == 0)
        def _():
            for k in range(shards):
                all_ref[k * rows : (k + 1) * rows] = blocks_[k][...]
            turn(all_ref, place_ref[1], keep_ref, send_ref)

        dh_ref[...] = mm_t(all_ref[...], down_ref[...])

    d_hidden, cot_keep, cot_send = run(
        cot_body,
        [shape((group, hidden), f32), far((half, group)), far((half, group))],
        [place, *cot_blocks, in_far(down_proj)],
        grid=(h_steps,),
        in_specs=[SMEM] + [whole(b) for b in cot_blocks] + [tiles((tile, width), 0)],
        out_specs=[tiles((group, tile), 1), whole(shape((half, group))), whole(shape((half, group)))],
        scratch=[pltpu.VMEM((group, width), bf16)],
        after=(gated,),
        us=5,
        limit=14,
    )

    cot_come = swap(cot_send, "dp", 1)
    mix_got = [swap(mix_parts[k], "fsdp", k) for k in others]

    def second_body(*refs):
        parts, x_ref, gain_ref, s_ref, n_ref = refs[:shards], *refs[shards:]
        total = x_ref[...].astype(f32)
        for p in parts:
            total = total + p[...].astype(f32)
        s_ref[...] = total
        r = lax.rsqrt(jnp.mean(total * total, axis=-1, keepdims=True) + epsilon)
        n_ref[...] = (total * r * gain_ref[1:2]).astype(bf16)

    second, normed_two = run(
        second_body,
        [shape((rows, width), f32), shape((rows, width))],
        [mix_parts[0], *mix_got, x_local, gains],
        after=(d_hidden,),
    )
    two_blocks = [normed_two] + send_tokens(normed_two)

    both_next = wait_for(both_next, normed_two)
    w_both = assemble(
        both_piece(f, 0, part),
        [
            (both_mine, c * half_part + here),
            (both_next, c * half_part + there),
            (swap(both_mine, "dp", 1), (1 - c) * half_part + here),
            (swap(both_next, "dp", 1), (1 - c) * half_part + there),
        ],
        (normed_two,),
        out=far,
        out_spec=ANY,
        limit=20,
    )
    w_both = in_far(w_both)
    turned = shape((half, group))

    def turn_two_body(place_ref, *refs):
        blocks_, (all_ref, keep_ref, send_ref) = refs[:shards], refs[shards:]
        for k in range(shards):
            all_ref[k * rows : (k + 1) * rows] = blocks_[k][...]
        turn(all_ref, place_ref[1], keep_ref, send_ref)

    two_all, two_keep, two_send = run(
        turn_two_body,
        [shape((group, width)), turned, turned],
        [place, *two_blocks],
        in_specs=[SMEM] + [whole(b) for b in two_blocks],
        after=(w_both,),
    )
    two_come = swap(two_send, "dp", 1)

    bundle = 32
    units = (group // bundle, bundle, hidden)
    unit_tiles = tiles((group // bundle, bundle, tile), 2)
    def gate_body(all_ref, w_ref, dh_ref, g_ref, du_ref):
        gate_ = mm(all_ref[...], w_ref[...])
        g_ref[...] = gate_
        du = dh_ref[...] * (gate_ * jax.nn.sigmoid(gate_))
        du_ref[...] = du.astype(bf16).reshape(du_ref.shape)

    gate, d_up = run(
        gate_body,
        [far((group, hidden), f32), far(units)],
        [two_all, w_both, d_hidden],
        grid=(h_steps,),
        in_specs=[
            whole(two_all),
            pl.BlockSpec((None, width, tile), lambda step: (0, 0, step)),
            tiles((group, tile), 1),
        ],
        out_specs=[tiles((group, tile), 1), unit_tiles],
        us=6,
        limit=16,
    )
    gate = in_far(gate)
    d_up = wait_for(d_up, two_come, keep=True)
    d_up_come = swap(d_up, "dp", 1)

    def flat(ref):
        return ref[...].reshape(group, ref.shape[2])

    def up_sum_body(own_ref, come_ref, du_ref, duc_ref, out_ref):
        total = mm(own_ref[...], flat(du_ref)) + mm(come_ref[...], flat(duc_ref))
        out_ref[...] = total.astype(bf16).reshape(blocks, chunk, tile)

    (up_both,) = run(
        up_sum_body,
        [shape((blocks, chunk, hidden))],
        [two_keep, two_come, d_up, d_up_come],
        grid=(h_steps,),
        in_specs=[whole(turned), whole(turned), unit_tiles, unit_tiles],
        out_specs=[tiles((blocks, chunk, tile), 2)],
        us=5,
        limit=14,
        hbm=True,
        near=(0, 1, 3),
    )
    up_sum = lax.psum_scatter(up_both, "seq", scatter_dimension=0, tiled=True).reshape(chunk, hidden)

    def up_body(all_ref, w_ref, g_ref, dh_ref, dg_ref, h_ref):
        upward = mm(all_ref[...], w_ref[...])
        gate_ = g_ref[...]
        s = jax.nn.sigmoid(gate_)
        dg = dh_ref[...] * upward * s * (1.0 + gate_ * (1.0 - s))
        dg_ref[...] = dg.astype(bf16).reshape(dg_ref.shape)
        h_ref[...] = (gate_ * s * upward).astype(bf16).reshape(h_ref.shape)

    d_gate, hidden_all = run(
        up_body,
        [far(units)] * 2,
        [two_all, w_both, gate, d_hidden],
        grid=(h_steps,),
        in_specs=[
            whole(two_all),
            pl.BlockSpec((None, width, tile), lambda step: (1, 0, step)),
            tiles((group, tile), 1),
            tiles((group, tile), 1),
        ],
        out_specs=[unit_tiles] * 2,
        after=(in_far(up_both),),
        us=7,
        limit=18,
    )
    d_gate_come = swap(d_gate, "dp", 1)
    hidden_come = swap(hidden_all, "dp", 1)

    def back_two_body(dg_ref, du_ref, wg_ref, wu_ref, *p_refs):
        d = (mm_t(flat(dg_ref), wg_ref[...]) + mm_t(flat(du_ref), wu_ref[...])).astype(bf16)
        for k in range(shards):
            p_refs[k][...] = d[k * rows : (k + 1) * rows]

    back_two = run(
        back_two_body,
        [shape((rows, width))] * shards,
        [d_gate, d_up, w_both, w_both],
        grid=(d_steps,),
        in_specs=[
            whole(d_gate),
            whole(d_up),
            pl.BlockSpec((None, tile, hidden), lambda step: (0, step, 0)),
            pl.BlockSpec((None, tile, hidden), lambda step: (1, step, 0)),
        ],
        out_specs=[tiles((rows, tile), 1)] * shards,
        us=7,
        limit=16,
        hbm=True,
    )
    back_two_got = [swap(back_two[k], "fsdp", k) for k in others]

    main = hidden // 128 * 128
    rest = hidden - main
    last_main = main - (h_steps - 1) * tile

    def two_sum_body(own_ref, come_ref, cot_own_ref, cot_come_ref, dg_ref, dgc_ref, h_ref, hc_ref, out_ref):
        step = pl.program_id(0)
        gate_ = mm(own_ref[...], flat(dg_ref)) + mm(come_ref[...], flat(dgc_ref))
        gate_ = gate_.reshape(blocks, chunk, tile)
        down_ = mm(cot_own_ref[...], flat(h_ref)) + mm(cot_come_ref[...], flat(hc_ref))
        down_ = down_.reshape(blocks, chunk, tile)

        @pl.when(step < h_steps - 1)
        def _():
            at = pl.multiple_of(step * tile, 128)
            out_ref[:, :, pl.ds(at, tile)] = gate_.astype(bf16)
            out_ref[:, :, pl.ds(main + at, tile)] = down_.astype(bf16)

        @pl.when(step == h_steps - 1)
        def _():
            out_ref[:, :, main - last_main : main] = gate_[:, :, :last_main].astype(bf16)
            out_ref[:, :, 2 * main - last_main : 2 * main] = down_[:, :, :last_main].astype(bf16)
            rests = [v[:, :, last_main : last_main + rest] for v in (gate_, down_)]
            out_ref[:, :, 2 * main :] = jnp.concatenate(rests, axis=2).astype(bf16)

    (two_both,) = run(
        two_sum_body,
        [shape((blocks, chunk, 2 * hidden))],
        [two_keep, two_come, cot_keep, cot_come, d_gate, d_gate_come, hidden_all, hidden_come],
        grid=(h_steps,),
        in_specs=[whole(turned)] * 4 + [unit_tiles] * 4,
        out_specs=[whole(shape((blocks, chunk, 2 * hidden)))],
        after=(in_far(back_two[0]),),
        us=10,
        limit=24,
        hbm=True,
        near=(0, 1, 2, 3, 5, 7),
    )
    two_sum = lax.psum_scatter(two_both, "seq", scatter_dimension=0, tiled=True)
    two_sum = two_sum.reshape(chunk, 2 * hidden)

    def second_grad_body(*refs):
        parts, (s_ref, cot_ref, gain_ref, d_ref, mix_ref, term_ref) = refs[:shards], refs[shards:]
        dn = parts[0][...].astype(f32)
        for p in parts[1:]:
            dn = dn + p[...].astype(f32)
        s = s_ref[...]
        r = lax.rsqrt(jnp.mean(s * s, axis=-1, keepdims=True) + epsilon)
        term_ref[...] = jnp.sum(dn * s * r, axis=0, keepdims=True)
        a = dn * gain_ref[1:2]
        d = cot_ref[...].astype(f32) + r * a - s * (r * r * r) * jnp.mean(a * s, axis=-1, keepdims=True)
        d_ref[...] = d
        mix_ref[...] = d.astype(bf16)

    d_second, d_mix, two_term = run(
        second_grad_body,
        [shape((rows, width), f32), shape((rows, width)), shape((1, width), f32)],
        [back_two[0], *back_two_got, second, cot_local, gains],
    )
    mix_blocks = [d_mix] + send_tokens(d_mix)

    runs = part // (shards * slab)
    channels = part // shards

    def owner_body(place_ref, g_ref, *out_refs):
        row = lax.broadcasted_iota(jnp.int32, (part, channels), 0)
        col = lax.broadcasted_iota(jnp.int32, (part, channels), 1)
        for k in range(shards):
            source = (col // slab) * (shards * slab) + (place_ref[0] ^ k) * slab + col % slab
            out_refs[k][...] = mm(g_ref[...], (row == source).astype(bf16)).astype(bf16)

    owner = run(
        owner_body,
        [shape((group, channels))] * shards,
        [place, gated],
        in_specs=[SMEM, whole(gated)],
        after=(in_far(two_both),),
    )
    owner_got = [owner[0]] + [swap(owner[k], "fsdp", k) for k in others]

    def gated_grad_body(*refs):
        blocks_, (o_ref, proj_ref, edge_ref, taps_ref) = refs[:shards], refs[shards : shards + 4]
        all_ref, dc_ref, dconv_ref, head_ref, term_ref, ext_ref = refs[shards + 4 :]
        for k in range(shards):
            all_ref[k * rows : (k + 1) * rows] = blocks_[k][...]
        dg = mm_t(all_ref[...], o_ref[...])
        dconv_ref[...] = dg * proj_ref[:, part : 2 * part]
        terms = [jnp.zeros((1, part), f32)] * taps
        for k in range(shards):
            r = slice(k * rows, (k + 1) * rows)
            d = dconv_ref[r]
            head_ref[k * 8 : (k + 1) * 8] = d[:8]
            ext_ref[:edge] = edge_ref[k * edge : (k + 1) * edge]
            ext_ref[edge:] = proj_ref[r, :part] * proj_ref[r, 2 * part :]
            conv = jnp.zeros((rows, part), f32)
            for t in range(taps):
                e = ext_ref[edge - rim + t : edge - rim + t + rows]
                conv = conv + taps_ref[t : t + 1] * e
                terms[t] = terms[t] + jnp.sum(d * e, axis=0, keepdims=True)
            dc_ref[r] = (dg[k * rows : (k + 1) * rows] * conv).astype(bf16)
        for t in range(taps):
            term_ref[t : t + 1] = terms[t]

    mix_all, d_c, d_conv, heads, tap_terms = run(
        gated_grad_body,
        [
            shape((group, width)),
            shape((group, part)),
            shape((group, part), f32),
            shape((shards * 8, part), f32),
            shape((taps, part), f32),
        ],
        [*mix_blocks, out_proj, projected, edge_product, taps_own],
        scratch=[pltpu.VMEM((edge + rows, part), f32)],
    )
    behind = shifted(heads, "seq", -1)

    def turn_body(place_ref, n_ref, *refs):
        got, (nt_ref, ot_ref) = refs[:shards], refs[shards:]
        for h in range(2):
            nt_ref[h] = n_ref[:, h * half : (h + 1) * half].T
        row = lax.broadcasted_iota(jnp.int32, (channels, part), 0)
        col = lax.broadcasted_iota(jnp.int32, (channels, part), 1)
        for b in range(shards):
            both = jnp.zeros((rows, part), f32)
            for k in range(shards):
                spread = (col == row + (place_ref[0] ^ k) * channels).astype(bf16)
                both = both + mm(got[k][(b ^ k) * rows : ((b ^ k) + 1) * rows], spread)
            both = both.astype(bf16)
            for h in range(2):
                wide = both[:, h * (part // 2) : (h + 1) * (part // 2)]
                ot_ref[h, :, b * rows : (b + 1) * rows] = wide.astype(f32).T.astype(bf16)

    one_turned, own_turned = run(
        turn_body,
        [shape((2, half, group)), shape((2, part // 2, group))],
        [place, normed_one, *owner_got],
        in_specs=[SMEM, whole(normed_one)] + [whole(o) for o in owner_got],
        after=(mix_blocks[0],),
    )

    def projected_grad_body(
        place_ref, dconv_ref, behind_ref, taps_ref, proj_ref, dc_ref, nt_ref, ot_ref, mix_ref,
        dp_ref, in_ref, out_ref, ext_ref,
    ):
        other = 1 - place_ref[1]
        for k in range(shards):
            r = slice(k * rows, (k + 1) * rows)
            ext_ref[:rows] = dconv_ref[r]
            ext_ref[rows:] = behind_ref[k * 8 : (k + 1) * 8]
            d = taps_ref[rim : rim + 1] * ext_ref[:rows]
            for t in range(rim):
                d = d + taps_ref[t : t + 1] * ext_ref[rim - t : rim - t + rows]
            dp_ref[r, :part] = (d * proj_ref[r, 2 * part :]).astype(bf16)
            dp_ref[r, part : 2 * part] = dc_ref[r]
            dp_ref[r, 2 * part :] = (d * proj_ref[r, :part]).astype(bf16)
        for t in range(3):
            cols = slice(t * part, (t + 1) * part)
            in_ref[:, :, cols] = mm(nt_ref[other], dp_ref[:, cols]).astype(bf16).reshape(blocks, chunk, part)
        for t in range(width // 512):
            cols = slice(t * 512, (t + 1) * 512)
            out_ref[:, cols] = mm(ot_ref[other], mix_ref[:, cols]).astype(bf16)

    d_projected, in_there, out_there = run(
        projected_grad_body,
        [shape((group, 3 * part)), shape((blocks, chunk, 3 * part)), shape((part // 2, width))],
        [place, d_conv, behind, taps_own, projected, d_c, one_turned, own_turned, mix_all],
        in_specs=[SMEM] + [whole(a) for a in (d_conv, behind, taps_own, projected, d_c, one_turned, own_turned, mix_all)],
        scratch=[pltpu.VMEM((rows + 8, part), f32)],
        us=3,
    )
    in_come = swap(in_there, "dp", 1)
    out_come = swap(out_there, "dp", 1)

    def back_one_body(dp_ref, w_ref, *p_refs):
        d = mm_t(dp_ref[...], w_ref[...]).astype(bf16)
        for k in range(shards):
            p_refs[k][...] = d[k * rows : (k + 1) * rows]

    back_one = run(
        back_one_body,
        [shape((rows, width))] * shards,
        [d_projected, w_in],
        grid=(d_steps,),
        in_specs=[whole(d_projected), tiles((tile, 3 * part), 0)],
        out_specs=[tiles((rows, tile), 1)] * shards,
        us=4,
        limit=14,
        hbm=True,
    )
    back_one_got = [swap(back_one[k], "fsdp", k) for k in others]

    def mixer_sum_body(place_ref, nt_ref, dp_ref, in_come_ref, ot_ref, mix_ref, out_come_ref, in_ref, out_ref):
        own = place_ref[1]
        for t in range(3):
            cols = slice(t * part, (t + 1) * part)
            here = mm(nt_ref[own], dp_ref[:, cols]).reshape(blocks, chunk, part)
            in_ref[:, :, cols] = (here + in_come_ref[:, :, cols].astype(f32)).astype(bf16)
        for t in range(width // 512):
            cols = slice(t * 512, (t + 1) * 512)
            here = mm(ot_ref[own], mix_ref[:, cols])
            out_ref[:, cols] = (here + out_come_ref[:, cols].astype(f32)).astype(bf16)

    in_both, out_both = run(
        mixer_sum_body,
        [shape((blocks, chunk, 3 * part)), shape((blocks * slab, width))],
        [place, one_turned, d_projected, in_come, own_turned, mix_all, out_come],
        in_specs=[SMEM]
        + [whole(a) for a in (one_turned, d_projected, in_come, own_turned, mix_all, out_come)],
        after=(in_far(back_one[0]),),
    )

    def final_body(h_ref, w_ref, *p_refs):
        d = mm(flat(h_ref), w_ref[...]).astype(bf16)
        for k in range(shards):
            p_refs[k][...] = d[k * rows : (k + 1) * rows]

    final_parts = run(
        final_body,
        [shape((rows, width))] * shards,
        [hidden_all, in_far(down_proj)],
        grid=(d_steps,),
        in_specs=[whole(hidden_all), tiles((hidden, tile), 1)],
        out_specs=[tiles((rows, tile), 1)] * shards,
        after=(in_both,),
        us=4,
        limit=14,
        hbm=True,
    )

    in_rows = in_both.reshape(blocks, shards, slab, 3 * part)

    def rows_for(k):
        return lax.dynamic_index_in_dim(in_rows, f ^ k, 1, keepdims=False)

    in_pieces = [rows_for(0)] + [swap(rows_for(k), "fsdp", k) for k in others]

    def place_body(place_ref, *refs):
        got, (o_ref, out_ref) = refs[:shards], refs[shards:]
        for s in range(shards):
            pick = got[0][...]
            for k in others:
                pick = jnp.where((place_ref[0] ^ k) == s, got[k][...], pick)
            for t in range(3):
                start = t * width + s * part
                out_ref[:, :, start : start + part] = pick[:, :, t * part : (t + 1) * part]
        out_ref[:, :, 3 * width :] = o_ref[...]

    (mix_both,) = run(
        place_body,
        [far((blocks, slab, 4 * width))],
        [place, *in_pieces, out_both.reshape(blocks, slab, width)],
        in_specs=[SMEM] + [VMEM] * (shards + 1),
        after=(in_far(final_parts[0]),),
        limit=12,
    )
    mix_sum = lax.psum_scatter(mix_both, "seq", scatter_dimension=0, tiled=True).reshape(slab, 4 * width)

    def input_grad_body(*refs):
        parts, (x_ref, d_ref, gain_ref, out_ref, term_ref) = refs[:shards], refs[shards:]
        dn = parts[0][...].astype(f32)
        for p in parts[1:]:
            dn = dn + p[...].astype(f32)
        x = x_ref[...].astype(f32)
        r = lax.rsqrt(jnp.mean(x * x, axis=-1, keepdims=True) + epsilon)
        term_ref[...] = jnp.sum(dn * x * r, axis=0, keepdims=True)
        a = dn * gain_ref[0:1]
        out_ref[...] = d_ref[...] + r * a - x * (r * r * r) * jnp.mean(a * x, axis=-1, keepdims=True)

    input_grad, one_term = run(
        input_grad_body,
        [shape((rows, width), f32), shape((1, width), f32)],
        [back_one[0], *back_one_got, x_local, d_second, gains],
        after=(in_far(mix_both),),
    )
    input_grad = input_grad.reshape(seqs, length, width)


    two_sum = wait_for(two_sum, one_term)
    up_rows = up_sum.reshape(shards, slab, hidden)
    two_rows = two_sum.reshape(shards, slab, 2 * hidden)

    def feed_rows(k):
        parts = [lax.dynamic_index_in_dim(r, f ^ k, 0, keepdims=False) for r in (two_rows, up_rows)]
        return jnp.concatenate(parts, axis=1)

    feed_pieces = [feed_rows(0)] + [swap(feed_rows(k), "fsdp", k) for k in others]

    final_got = [swap(final_parts[k], "fsdp", k) for k in others]
    final_got = wait_all(final_got, feed_pieces[0])
    total = second + final_parts[0].astype(f32)
    for piece in final_got:
        total = total + piece.astype(f32)
    block_output = total.astype(bf16).reshape(seqs, length, width)

    spread_taps = [jnp.where(f == s, tap_terms, 0.0) for s in range(shards)]
    terms = jnp.concatenate([one_term, two_term, jnp.concatenate(spread_taps, axis=1)], axis=0)
    terms = sum_over(sum_over(sum_over(terms, "dp", feed_pieces[:1]), "seq"), "fsdp", feed_pieces[1:])
    own = lax.dynamic_slice_in_dim(terms, ((c * blocks + z) * shards + f) * slab, slab, 1)

    def spread_body(place_ref, *refs):
        got, (up_ref, gate_ref, down_ref) = refs[:shards], refs[shards:]

        def pick(s, start, size):
            value = got[0][:, start : start + size]
            for k in others:
                value = jnp.where((place_ref[0] ^ k) == s, got[k][:, start : start + size], value)
            return value.astype(f32)

        for s in range(shards):
            at = s * hidden
            up_ref[:, at : at + hidden] = pick(s, 2 * hidden, hidden)
            gate_ref[:, at : at + main] = pick(s, 0, main)
            down_ref[:, at : at + main] = pick(s, main, main)
            gate_ref[:, at + main : at + hidden] = pick(s, 2 * main, rest)
            down_ref[:, at + main : at + hidden] = pick(s, 2 * main + rest, rest)

    up_grad, gate_grad, down_rows = run(
        spread_body,
        [far((slab, shards * hidden), f32)] * 3,
        [place, *feed_pieces],
        in_specs=[SMEM] + [whole(p) for p in feed_pieces],
        limit=12,
    )
    down_grad = jnp.transpose(down_rows)

    def last_body(sum_ref, in_ref, out_ref):
        in_ref[...] = sum_ref[:, : 3 * width].astype(f32)
        out_ref[...] = sum_ref[:, 3 * width :].astype(f32)

    in_grad, out_grad = run(
        last_body, [far((slab, 3 * width), f32), far((slab, width), f32)], [in_far(mix_sum)], after=(in_far(gate_grad), in_far(block_output), own)
    )
    return (
        block_output,
        input_grad,
        in_grad,
        out_grad,
        gate_grad,
        up_grad,
        down_grad,
        own[0],
        own[1],
        own[2:],
    )


def solution(mesh):
    placed = (
        P(("dp", "fsdp"), "seq", None),
        P("fsdp", None),
        P("fsdp", None),
        P("fsdp", None),
        P("fsdp", None),
        P("fsdp", None),
        P("fsdp"),
        P("fsdp"),
        P(None, "fsdp"),
        P(("dp", "fsdp"), "seq", None),
    )
    return jax.shard_map(
        on_device,
        mesh=mesh,
        in_specs=placed,
        out_specs=(
            P(("dp", "fsdp"), "seq", None),
            P(("dp", "fsdp"), "seq", None),
            P(("dp", "seq", "fsdp"), None),
            P(("dp", "seq", "fsdp"), None),
            P(("dp", "seq", "fsdp"), None),
            P(("dp", "seq", "fsdp"), None),
            P(None, ("dp", "seq", "fsdp")),
            P(("dp", "seq", "fsdp")),
            P(("dp", "seq", "fsdp")),
            P(None, ("dp", "seq", "fsdp")),
        ),
        check_vma=False,
    )
```

```python
import math

import jax
import jax.numpy as jnp
from jax import lax
from jax.experimental import pallas as pl
from jax.experimental.pallas import tpu as pltpu
from jax.sharding import PartitionSpec as P

epsilon = 1e-05
f32 = jnp.float32
bf16 = jnp.bfloat16
MIB = 1 << 20
SCALE = 1e8
ANY = pl.BlockSpec(memory_space=pl.ANY)


def shape(dims, dtype=bf16):
    return jax.ShapeDtypeStruct(dims, dtype)


def far(dims, dtype=bf16):
    return pltpu.HBM(dims, dtype)


def in_far(value):
    return pltpu.with_memory_space_constraint(value, pltpu.HBM)


def whole(array):
    dims = array.shape
    return pl.BlockSpec(dims, lambda *steps: (0,) * len(dims), pipeline_mode=pl.Buffered(1))


def tiles(dims, axis):
    return pl.BlockSpec(dims, lambda step: tuple(step if i == axis else 0 for i in range(len(dims))))


def run(body, outs, ins, grid=(1,), in_specs=None, out_specs=None, scratch=(), after=(), limit=6, us=1.0, aliases=None, hbm=False, near=()):
    in_specs = [whole(a) for a in ins] if in_specs is None else in_specs
    out_specs = [whole(o) for o in outs] if out_specs is None else out_specs
    n, m = len(ins), len(after)
    if hbm:
        ins = [in_far(a) if a.size > 1024 and i not in near else a for i, a in enumerate(ins)]
        outs = [far(o.shape, o.dtype) if math.prod(o.shape) > 1024 else o for o in outs]

    def kernel(*refs):
        body(*refs[:n], *refs[n + m :])

    return pl.pallas_call(
        kernel,
        out_shape=tuple(outs),
        grid=grid,
        in_specs=list(in_specs) + [ANY] * m,
        out_specs=tuple(out_specs),
        scratch_shapes=list(scratch),
        compiler_params=pltpu.CompilerParams(vmem_limit_bytes=limit * MIB),
        cost_estimate=pl.CostEstimate(flops=int(us * SCALE), bytes_accessed=1000, transcendentals=0),
        input_output_aliases=aliases or {},
    )(*ins, *after)


def mm(a, b):
    return lax.dot_general(a, b, (((1,), (0,)), ((), ())), preferred_element_type=f32)


def mm_t(a, b):
    return lax.dot_general(a, b, (((1,), (1,)), ((), ())), preferred_element_type=f32)


def swap(value, axis, k):
    return lax.ppermute(value, axis, [(i, i ^ k) for i in range(lax.axis_size(axis))])


def shifted(block, axis, distance):
    devices = range(lax.axis_size(axis))
    route = [(i - distance, i) for i in devices if i - distance in devices]
    return lax.ppermute(block, axis, route)


def sum_over(value, axis, after=()):
    size = lax.axis_size(axis)
    if after:
        value = wait_for(value, *after)
    if size <= 4:
        return sum((swap(value, axis, k) for k in range(1, size)), value)
    k = 1
    while k < size:
        value = value + swap(value, axis, k)
        k *= 2
    return value


def wait_body(value_ref, out_ref):
    pass


def wait_for(value, *after, keep=False):
    return run(
        wait_body,
        [far(value.shape, value.dtype) if keep else shape(value.shape, value.dtype)],
        [in_far(value) if keep else value],
        in_specs=[ANY],
        out_specs=[ANY],
        after=after,
        limit=4,
        us=0.3,
        aliases={0: 0},
    )[0]


def wait_all_body(*refs):
    pass


def wait_all(values, *after):
    count = len(values)
    return run(
        wait_all_body,
        [shape(v.shape, v.dtype) for v in values],
        values,
        in_specs=[ANY] * count,
        out_specs=[ANY] * count,
        after=after,
        limit=4,
        us=0.3,
        aliases={i: i for i in range(count)},
    )


def hold_body(value_ref, out_ref, sem):
    copy = pltpu.make_async_copy(value_ref, out_ref, sem)
    copy.start()
    copy.wait()


def hold(value, *after):
    return run(
        hold_body,
        [shape(value.shape, value.dtype)],
        [value],
        in_specs=[ANY],
        out_specs=[ANY],
        scratch=[pltpu.SemaphoreType.DMA(())],
        after=after,
        limit=4,
    )[0]


def on_device(
    block_input,
    in_proj,
    out_proj,
    gate_proj,
    up_proj,
    down_proj,
    norm_one,
    norm_two,
    conv_kernel,
    out_cotangent,
):
    shards = lax.axis_size("fsdp")
    blocks = lax.axis_size("seq")
    f = lax.axis_index("fsdp")
    c = lax.axis_index("dp")
    z = lax.axis_index("seq")
    others = range(1, shards)
    seqs, length, width = block_input.shape
    rows = seqs * length
    group = shards * rows
    part = in_proj.shape[0]
    hidden = down_proj.shape[0]
    taps = conv_kernel.shape[0]
    rim = taps - 1
    edge = 16
    half_part = part // 2
    half = width // 2
    slab = width // (blocks * 2 * shards)
    tile = 512
    h_steps = pl.cdiv(hidden, tile)
    d_steps = width // tile
    chunk = half // blocks
    place = jnp.stack([f, c, z % 2]).astype(jnp.int32)
    SMEM = pl.BlockSpec(memory_space=pltpu.SMEM)
    VMEM = pl.BlockSpec(memory_space=pltpu.VMEM)

    def send_tokens(local):
        return [swap(local, "fsdp", k) for k in others]

    def turn(all_ref, own, keep_ref, send_ref):
        for h in range(2):
            value = all_ref[:, h * half : (h + 1) * half].T

            @pl.when(own == h)
            def _():
                keep_ref[...] = value

            @pl.when(own != h)
            def _():
                send_ref[...] = value

    def pack(pieces, after=()):
        count = len(pieces)

        def body(*refs):
            got, out_ref, sems = refs[:count], refs[count], refs[count + 1]
            copies = [pltpu.make_async_copy(got[i], out_ref.at[i], sems.at[i]) for i in range(count)]
            for copy in copies:
                copy.start()
            for copy in copies:
                copy.wait()

        return run(
            body,
            [shape((count, *pieces[0].shape))],
            pieces,
            in_specs=[ANY] * count,
            out_specs=[VMEM],
            scratch=[pltpu.SemaphoreType.DMA((count,))],
            after=after,
            limit=6,
        )[0]

    def assemble(own, parts, after=(), out=shape, out_spec=VMEM, in_spec=ANY, limit=14):
        planes, columns = parts[0][0].shape[1], parts[0][0].shape[3]
        count = len(others)
        arrays = [p for p, _ in parts]
        starts = jnp.stack([f] + [h for _, h in parts]).astype(jnp.int32)

        def body(place_ref, own_ref, *refs):
            got, out_ref, sems = refs[: len(arrays)], refs[-2], refs[-1]
            f_ = place_ref[0]
            copies = []
            for p in range(planes):
                row = pl.ds(pl.multiple_of(f_ * part, part), part)
                if own.ndim == 3:
                    copies.append(pltpu.make_async_copy(own_ref.at[p], out_ref.at[p, row], sems.at[len(copies)]))
                else:
                    for t in range(columns // part):
                        source = own_ref.at[:, pl.ds(pl.multiple_of(t * width + f_ * part, part), part)]
                        target = out_ref.at[p, row, pl.ds(t * part, part)]
                        copies.append(pltpu.make_async_copy(source, target, sems.at[len(copies)]))
                for j, ref in enumerate(got):
                    size = ref.shape[2]
                    for i, k in enumerate(others):
                        start = pl.multiple_of((f_ ^ k) * part + place_ref[1 + j], size)
                        target = out_ref.at[p, pl.ds(start, size)]
                        copies.append(pltpu.make_async_copy(ref.at[i, p], target, sems.at[len(copies)]))
            for copy in copies:
                copy.start()
            for copy in copies:
                copy.wait()

        return run(
            body,
            [out((planes, width, columns))],
            [starts, own, *arrays],
            in_specs=[SMEM] + [in_spec] * (1 + len(arrays)),
            out_specs=[out_spec],
            scratch=[pltpu.SemaphoreType.DMA((planes * (4 + len(arrays) * count),))],
            after=after,
            limit=limit,
        )[0]

    quarter = half_part // 2
    here, there = (z % 2) * quarter, (1 - z % 2) * quarter

    def in_body(place_ref, w_ref, *refs):
        outs, sems = refs[: len(others)], refs[-1]
        copies = []
        first = pl.multiple_of(place_ref[1] * half_part + place_ref[2] * quarter, quarter)
        for i, k in enumerate(others):
            for t in range(3):
                start = pl.multiple_of(t * width + (place_ref[0] ^ k) * part, part)
                source = w_ref.at[pl.ds(first, quarter), pl.ds(start, part)]
                target = outs[i].at[:, pl.ds(t * part, part)]
                copies.append(pltpu.make_async_copy(source, target, sems.at[i * 3 + t]))
        for copy in copies:
            copy.start()
        for copy in copies:
            copy.wait()

    in_sent = run(
        in_body,
        [shape((quarter, 3 * part))] * len(others),
        [place, in_far(in_proj)],
        in_specs=[SMEM, ANY],
        out_specs=[VMEM] * len(others),
        scratch=[pltpu.SemaphoreType.DMA((3 * len(others),))],
    )
    in_got = [swap(m, "fsdp", k) for m, k in zip(in_sent, others)]

    x_local = block_input.reshape(rows, width)
    cot_local = out_cotangent.reshape(rows, width)
    tail = shifted(x_local[rows - edge :], "seq", 1)
    small = jnp.concatenate([norm_one[None], norm_two[None], conv_kernel], axis=0)
    small = jnp.pad(small, ((0, edge - taps - 2), (0, 0)))

    def join_body(x_ref, t_ref, small_ref, out_ref):
        out_ref[:rows] = x_ref[...]
        out_ref[rows:] = t_ref[...]
        row = lax.broadcasted_iota(jnp.int32, (edge, part), 0)
        out_ref[rows:, :part] = jnp.where(row < taps + 2, small_ref[...], t_ref[:, :part])

    (message,) = run(join_body, [shape((rows + edge, width))], [x_local, tail, small])
    messages = [message] + send_tokens(message)
    taps_own = conv_kernel.astype(f32)

    in_mine = pack(in_got, (message,))
    in_next = swap(in_mine, "seq", 1)

    def both_piece(j, start, size):
        return jnp.stack(
            [lax.dynamic_slice(weight, (start, j * hidden), (size, hidden)) for weight in (gate_proj, up_proj)]
        )

    both_sent = [both_piece(f ^ k, c * half_part + here, quarter) for k in others]
    both_sent = wait_all(both_sent, *in_got)
    both_got = [swap(piece, "fsdp", k) for piece, k in zip(both_sent, others)]

    both_mine = pack(both_got, (in_next,))
    both_next = swap(both_mine, "seq", 1)

    def norm_body(place_ref, *refs):
        xs, (n_ref, nh_ref, gain_ref) = refs[:shards], refs[shards:]
        for s in range(shards):
            pick = xs[0][rows:, :part]
            for k in others:
                pick = jnp.where((place_ref[0] ^ k) == s, xs[k][rows:, :part], pick)
            gain_ref[:, s * part : (s + 1) * part] = pick[:8].astype(f32)
        gain = gain_ref[0:1]

        def normed(v):
            v = v.astype(f32)
            r = lax.rsqrt(jnp.mean(v * v, axis=-1, keepdims=True) + epsilon)
            return (v * r * gain).astype(bf16)

        for k in range(shards):
            n_ref[k * rows : (k + 1) * rows] = normed(xs[k][:rows])
            nh_ref[k * edge : (k + 1) * edge] = normed(xs[k][rows:])

    normed_one, normed_edge, gains = run(
        norm_body,
        [shape((group, width)), shape((shards * edge, width)), shape((8, width), f32)],
        [place, *[in_far(m) for m in messages]],
        in_specs=[SMEM] + [whole(m) for m in messages],
        after=(both_mine,),
        us=2,
    )

    w_in = assemble(
        in_far(in_proj),
        [
            (in_mine[:, None], c * half_part + here),
            (in_next[:, None], c * half_part + there),
            (swap(in_mine, "dp", 1)[:, None], (1 - c) * half_part + here),
            (swap(in_next, "dp", 1)[:, None], (1 - c) * half_part + there),
        ],
        (both_mine,),
    )[0]

    cot_held = hold(cot_local, both_mine)
    cot_blocks = [cot_held] + send_tokens(cot_held)

    def mixer_body(n_ref, nh_ref, taps_ref, w_ref, o_ref, far_ref, edge_ref, gated_ref, *refs):
        p_refs, (ph_ref, ext_ref, proj_ref, sem) = refs[:shards], refs[shards:]
        for t in range(3):
            cols = slice(t * part, (t + 1) * part)
            w = w_ref[:, cols]
            proj_ref[:, cols] = mm(n_ref[...], w)
            if t != 1:
                ph_ref[:, cols] = mm(nh_ref[...], w)
        leave = pltpu.make_async_copy(proj_ref, far_ref, sem)
        leave.start()
        edge_ref[...] = ph_ref[:, :part] * ph_ref[:, 2 * part :]
        for k in range(shards):
            r = slice(k * rows, (k + 1) * rows)
            ext_ref[:edge] = edge_ref[k * edge : (k + 1) * edge]
            ext_ref[edge:] = proj_ref[r, :part] * proj_ref[r, 2 * part :]
            conv = taps_ref[rim : rim + 1] * ext_ref[edge:]
            for t in range(rim):
                conv = conv + taps_ref[t : t + 1] * ext_ref[edge - rim + t : edge - rim + t + rows]
            gated_ref[r] = (proj_ref[r, part : 2 * part] * conv).astype(bf16)
        for t in range(width // 512):
            cols = slice(t * 512, (t + 1) * 512)
            o = mm(gated_ref[...], o_ref[:, cols]).astype(bf16)
            for k in range(shards):
                p_refs[k][:, cols] = o[k * rows : (k + 1) * rows]
        leave.wait()

    projected, edge_product, gated, *mix_parts = run(
        mixer_body,
        [
            far((group, 3 * part), f32),
            far((shards * edge, part), f32),
            shape((group, part)),
        ]
        + [shape((rows, width))] * shards,
        [normed_one, normed_edge, taps_own, w_in, out_proj],
        out_specs=[ANY, whole(shape((shards * edge, part))), whole(shape((group, part)))]
        + [whole(shape((rows, width)))] * shards,
        scratch=[
            pltpu.VMEM((shards * edge, 3 * part), f32),
            pltpu.VMEM((edge + rows, part), f32),
            pltpu.VMEM((group, 3 * part), f32),
            pltpu.SemaphoreType.DMA(()),
        ],
        after=(cot_held,),
        us=5.5,
        limit=10,
    )

    def cot_body(place_ref, *refs):
        blocks_, (down_ref, dh_ref, keep_ref, send_ref, all_ref) = refs[:shards], refs[shards:]

        @pl.when(pl.program_id(0) == 0)
        def _():
            for k in range(shards):
                all_ref[k * rows : (k + 1) * rows] = blocks_[k][...]
            turn(all_ref, place_ref[1], keep_ref, send_ref)

        dh_ref[...] = mm_t(all_ref[...], down_ref[...])

    d_hidden, cot_keep, cot_send = run(
        cot_body,
        [shape((group, hidden), f32), far((half, group)), far((half, group))],
        [place, *cot_blocks, in_far(down_proj)],
        grid=(h_steps,),
        in_specs=[SMEM] + [whole(b) for b in cot_blocks] + [tiles((tile, width), 0)],
        out_specs=[tiles((group, tile), 1), whole(shape((half, group))), whole(shape((half, group)))],
        scratch=[pltpu.VMEM((group, width), bf16)],
        after=(gated,),
        us=5,
        limit=14,
    )

    cot_come = swap(cot_send, "dp", 1)
    mix_got = [swap(mix_parts[k], "fsdp", k) for k in others]

    def second_body(*refs):
        parts, x_ref, gain_ref, s_ref, n_ref = refs[:shards], *refs[shards:]
        total = x_ref[...].astype(f32)
        for p in parts:
            total = total + p[...].astype(f32)
        s_ref[...] = total
        r = lax.rsqrt(jnp.mean(total * total, axis=-1, keepdims=True) + epsilon)
        n_ref[...] = (total * r * gain_ref[1:2]).astype(bf16)

    second, normed_two = run(
        second_body,
        [shape((rows, width), f32), shape((rows, width))],
        [mix_parts[0], *mix_got, x_local, gains],
        after=(d_hidden,),
    )
    two_blocks = [normed_two] + send_tokens(normed_two)

    both_next = wait_for(both_next, normed_two)
    w_both = assemble(
        both_piece(f, 0, part),
        [
            (both_mine, c * half_part + here),
            (both_next, c * half_part + there),
            (swap(both_mine, "dp", 1), (1 - c) * half_part + here),
            (swap(both_next, "dp", 1), (1 - c) * half_part + there),
        ],
        (normed_two,),
        out=far,
        out_spec=ANY,
        in_spec=VMEM,
        limit=20,
    )
    w_both = in_far(w_both)
    turned = shape((half, group))

    def turn_two_body(place_ref, *refs):
        blocks_, (all_ref, keep_ref, send_ref) = refs[:shards], refs[shards:]
        for k in range(shards):
            all_ref[k * rows : (k + 1) * rows] = blocks_[k][...]
        turn(all_ref, place_ref[1], keep_ref, send_ref)

    two_all, two_keep, two_send = run(
        turn_two_body,
        [shape((group, width)), turned, turned],
        [place, *two_blocks],
        in_specs=[SMEM] + [whole(b) for b in two_blocks],
        after=(w_both,),
    )
    two_come = swap(two_send, "dp", 1)

    bundle = 32
    units = (group // bundle, bundle, hidden)
    wide = 896
    wide_units = tiles((group // bundle, bundle, wide), 2)
    unit_tiles = tiles((group // bundle, bundle, tile), 2)
    def gate_body(all_ref, w_ref, dh_ref, g_ref, du_ref):
        gate_ = mm(all_ref[...], w_ref[...])
        g_ref[...] = gate_
        du = dh_ref[...] * (gate_ * jax.nn.sigmoid(gate_))
        du_ref[...] = du.astype(bf16).reshape(du_ref.shape)

    gate, d_up = run(
        gate_body,
        [far((group, hidden), f32), far(units)],
        [two_all, w_both, d_hidden],
        grid=(pl.cdiv(hidden, wide),),
        in_specs=[
            whole(two_all),
            pl.BlockSpec((None, width, wide), lambda step: (0, 0, step)),
            tiles((group, wide), 1),
        ],
        out_specs=[tiles((group, wide), 1), wide_units],
        us=6,
        limit=18,
    )
    gate = in_far(gate)
    d_up = wait_for(d_up, two_come, keep=True)
    d_up_come = swap(d_up, "dp", 1)

    def flat(ref):
        return ref[...].reshape(group, ref.shape[2])

    def up_own_body(own_ref, du_ref, out_ref):
        out_ref[...] = mm(own_ref[...], flat(du_ref)).astype(bf16)

    (up_own,) = run(
        up_own_body,
        [shape((half, hidden))],
        [two_keep, in_far(d_up)],
        grid=(pl.cdiv(hidden, wide),),
        in_specs=[whole(turned), wide_units],
        out_specs=[tiles((half, wide), 1)],
        us=3,
        limit=8,
    )

    def up_sum_body(term_ref, come_ref, duc_ref, out_ref):
        total = term_ref[...].astype(f32) + mm(come_ref[...], flat(duc_ref))
        out_ref[...] = total.astype(bf16).reshape(blocks, chunk, wide)

    (up_both,) = run(
        up_sum_body,
        [far((blocks, chunk, hidden))],
        [up_own, two_come, d_up_come],
        grid=(pl.cdiv(hidden, wide),),
        in_specs=[tiles((half, wide), 1), whole(turned), wide_units],
        out_specs=[tiles((blocks, chunk, wide), 2)],
        us=5,
        limit=11,
    )
    up_sum = lax.psum_scatter(up_both, "seq", scatter_dimension=0, tiled=True).reshape(chunk, hidden)

    def up_body(all_ref, w_ref, g_ref, dh_ref, dg_ref, h_ref):
        upward = mm(all_ref[...], w_ref[...])
        gate_ = g_ref[...]
        s = jax.nn.sigmoid(gate_)
        dg = dh_ref[...] * upward * s * (1.0 + gate_ * (1.0 - s))
        dg_ref[...] = dg.astype(bf16).reshape(dg_ref.shape)
        h_ref[...] = (gate_ * s * upward).astype(bf16).reshape(h_ref.shape)

    d_gate, hidden_all = run(
        up_body,
        [far(units)] * 2,
        [two_all, w_both, gate, d_hidden],
        grid=(h_steps,),
        in_specs=[
            whole(two_all),
            pl.BlockSpec((None, width, tile), lambda step: (1, 0, step)),
            tiles((group, tile), 1),
            tiles((group, tile), 1),
        ],
        out_specs=[unit_tiles] * 2,
        after=(in_far(up_both),),
        us=7,
        limit=18,
    )
    d_gate_come = swap(d_gate, "dp", 1)
    hidden_come = swap(hidden_all, "dp", 1)

    def back_two_body(dg_ref, du_ref, wg_ref, wu_ref, *p_refs):
        d = (mm_t(flat(dg_ref), wg_ref[...]) + mm_t(flat(du_ref), wu_ref[...])).astype(bf16)
        for k in range(shards):
            p_refs[k][...] = d[k * rows : (k + 1) * rows]

    back_two = run(
        back_two_body,
        [shape((rows, width))] * shards,
        [d_gate, d_up, w_both, w_both],
        grid=(d_steps,),
        in_specs=[
            whole(d_gate),
            whole(d_up),
            pl.BlockSpec((None, tile, hidden), lambda step: (0, step, 0)),
            pl.BlockSpec((None, tile, hidden), lambda step: (1, step, 0)),
        ],
        out_specs=[tiles((rows, tile), 1)] * shards,
        us=7,
        limit=16,
        hbm=True,
    )
    back_two_got = [swap(back_two[k], "fsdp", k) for k in others]

    main = hidden // 128 * 128
    rest = hidden - main
    last_main = main - (h_steps - 1) * tile

    def two_sum_body(own_ref, come_ref, cot_own_ref, cot_come_ref, dg_ref, dgc_ref, h_ref, hc_ref, out_ref):
        step = pl.program_id(0)
        gate_ = mm(own_ref[...], flat(dg_ref)) + mm(come_ref[...], flat(dgc_ref))
        gate_ = gate_.reshape(blocks, chunk, tile)
        down_ = mm(cot_own_ref[...], flat(h_ref)) + mm(cot_come_ref[...], flat(hc_ref))
        down_ = down_.reshape(blocks, chunk, tile)

        @pl.when(step < h_steps - 1)
        def _():
            at = pl.multiple_of(step * tile, 128)
            out_ref[:, :, pl.ds(at, tile)] = gate_.astype(bf16)
            out_ref[:, :, pl.ds(main + at, tile)] = down_.astype(bf16)

        @pl.when(step == h_steps - 1)
        def _():
            out_ref[:, :, main - last_main : main] = gate_[:, :, :last_main].astype(bf16)
            out_ref[:, :, 2 * main - last_main : 2 * main] = down_[:, :, :last_main].astype(bf16)
            rests = [v[:, :, last_main : last_main + rest] for v in (gate_, down_)]
            out_ref[:, :, 2 * main :] = jnp.concatenate(rests, axis=2).astype(bf16)

    (two_both,) = run(
        two_sum_body,
        [shape((blocks, chunk, 2 * hidden))],
        [two_keep, two_come, cot_keep, cot_come, d_gate, d_gate_come, hidden_all, hidden_come],
        grid=(h_steps,),
        in_specs=[whole(turned)] * 4 + [unit_tiles] * 4,
        out_specs=[whole(shape((blocks, chunk, 2 * hidden)))],
        after=(in_far(back_two[0]),),
        us=10,
        limit=24,
        hbm=True,
        near=(0, 1, 2, 3, 5, 7),
    )
    two_sum = lax.psum_scatter(two_both, "seq", scatter_dimension=0, tiled=True)
    two_sum = two_sum.reshape(chunk, 2 * hidden)

    def second_grad_body(*refs):
        parts, (s_ref, cot_ref, gain_ref, d_ref, mix_ref, term_ref) = refs[:shards], refs[shards:]
        dn = parts[0][...].astype(f32)
        for p in parts[1:]:
            dn = dn + p[...].astype(f32)
        s = s_ref[...]
        r = lax.rsqrt(jnp.mean(s * s, axis=-1, keepdims=True) + epsilon)
        term_ref[...] = jnp.sum(dn * s * r, axis=0, keepdims=True)
        a = dn * gain_ref[1:2]
        d = cot_ref[...].astype(f32) + r * a - s * (r * r * r) * jnp.mean(a * s, axis=-1, keepdims=True)
        d_ref[...] = d
        mix_ref[...] = d.astype(bf16)

    d_second, d_mix, two_term = run(
        second_grad_body,
        [shape((rows, width), f32), shape((rows, width)), shape((1, width), f32)],
        [back_two[0], *back_two_got, second, cot_local, gains],
    )
    mix_blocks = [d_mix] + send_tokens(d_mix)

    runs = part // (shards * slab)
    channels = part // shards

    def owner_body(place_ref, g_ref, *out_refs):
        row = lax.broadcasted_iota(jnp.int32, (part, channels), 0)
        col = lax.broadcasted_iota(jnp.int32, (part, channels), 1)
        for k in range(shards):
            source = (col // slab) * (shards * slab) + (place_ref[0] ^ k) * slab + col % slab
            out_refs[k][...] = mm(g_ref[...], (row == source).astype(bf16)).astype(bf16)

    owner = run(
        owner_body,
        [shape((group, channels))] * shards,
        [place, gated],
        in_specs=[SMEM, whole(gated)],
        after=(in_far(two_both),),
    )
    owner_got = [owner[0]] + [swap(owner[k], "fsdp", k) for k in others]

    def gated_grad_body(*refs):
        blocks_, (o_ref, proj_ref, edge_ref, taps_ref) = refs[:shards], refs[shards : shards + 4]
        all_ref, dc_ref, dconv_ref, head_ref, term_ref, ext_ref = refs[shards + 4 :]
        for k in range(shards):
            all_ref[k * rows : (k + 1) * rows] = blocks_[k][...]
        dg = mm_t(all_ref[...], o_ref[...])
        dconv_ref[...] = dg * proj_ref[:, part : 2 * part]
        terms = [jnp.zeros((1, part), f32)] * taps
        for k in range(shards):
            r = slice(k * rows, (k + 1) * rows)
            d = dconv_ref[r]
            head_ref[k * 8 : (k + 1) * 8] = d[:8]
            ext_ref[:edge] = edge_ref[k * edge : (k + 1) * edge]
            ext_ref[edge:] = proj_ref[r, :part] * proj_ref[r, 2 * part :]
            conv = jnp.zeros((rows, part), f32)
            for t in range(taps):
                e = ext_ref[edge - rim + t : edge - rim + t + rows]
                conv = conv + taps_ref[t : t + 1] * e
                terms[t] = terms[t] + jnp.sum(d * e, axis=0, keepdims=True)
            dc_ref[r] = (dg[k * rows : (k + 1) * rows] * conv).astype(bf16)
        for t in range(taps):
            term_ref[t : t + 1] = terms[t]

    mix_all, d_c, d_conv, heads, tap_terms = run(
        gated_grad_body,
        [
            shape((group, width)),
            shape((group, part)),
            shape((group, part), f32),
            shape((shards * 8, part), f32),
            shape((taps, part), f32),
        ],
        [*mix_blocks, out_proj, projected, edge_product, taps_own],
        scratch=[pltpu.VMEM((edge + rows, part), f32)],
    )
    behind = shifted(heads, "seq", -1)

    def turn_body(place_ref, n_ref, *refs):
        got, (nt_ref, ot_ref) = refs[:shards], refs[shards:]
        for h in range(2):
            nt_ref[h] = n_ref[:, h * half : (h + 1) * half].T
        row = lax.broadcasted_iota(jnp.int32, (channels, part), 0)
        col = lax.broadcasted_iota(jnp.int32, (channels, part), 1)
        for b in range(shards):
            both = jnp.zeros((rows, part), f32)
            for k in range(shards):
                spread = (col == row + (place_ref[0] ^ k) * channels).astype(bf16)
                both = both + mm(got[k][(b ^ k) * rows : ((b ^ k) + 1) * rows], spread)
            both = both.astype(bf16)
            for h in range(2):
                wide = both[:, h * (part // 2) : (h + 1) * (part // 2)]
                ot_ref[h, :, b * rows : (b + 1) * rows] = wide.astype(f32).T.astype(bf16)

    one_turned, own_turned = run(
        turn_body,
        [shape((2, half, group)), shape((2, part // 2, group))],
        [place, normed_one, *owner_got],
        in_specs=[SMEM, whole(normed_one)] + [whole(o) for o in owner_got],
        after=(mix_blocks[0],),
    )

    def projected_grad_body(
        place_ref, dconv_ref, behind_ref, taps_ref, proj_ref, dc_ref, nt_ref, ot_ref, mix_ref,
        dp_ref, in_ref, out_ref, ext_ref,
    ):
        other = 1 - place_ref[1]
        for k in range(shards):
            r = slice(k * rows, (k + 1) * rows)
            ext_ref[:rows] = dconv_ref[r]
            ext_ref[rows:] = behind_ref[k * 8 : (k + 1) * 8]
            d = taps_ref[rim : rim + 1] * ext_ref[:rows]
            for t in range(rim):
                d = d + taps_ref[t : t + 1] * ext_ref[rim - t : rim - t + rows]
            dp_ref[r, :part] = (d * proj_ref[r, 2 * part :]).astype(bf16)
            dp_ref[r, part : 2 * part] = dc_ref[r]
            dp_ref[r, 2 * part :] = (d * proj_ref[r, :part]).astype(bf16)
        for t in range(3):
            cols = slice(t * part, (t + 1) * part)
            in_ref[:, :, cols] = mm(nt_ref[other], dp_ref[:, cols]).astype(bf16).reshape(blocks, chunk, part)
        for t in range(width // 512):
            cols = slice(t * 512, (t + 1) * 512)
            out_ref[:, cols] = mm(ot_ref[other], mix_ref[:, cols]).astype(bf16)

    d_projected, in_there, out_there = run(
        projected_grad_body,
        [shape((group, 3 * part)), shape((blocks, chunk, 3 * part)), shape((part // 2, width))],
        [place, d_conv, behind, taps_own, projected, d_c, one_turned, own_turned, mix_all],
        in_specs=[SMEM] + [whole(a) for a in (d_conv, behind, taps_own, projected, d_c, one_turned, own_turned, mix_all)],
        scratch=[pltpu.VMEM((rows + 8, part), f32)],
        us=3,
    )
    in_come = swap(in_there, "dp", 1)
    out_come = swap(out_there, "dp", 1)

    def back_one_body(dp_ref, w_ref, *p_refs):
        d = mm_t(dp_ref[...], w_ref[...]).astype(bf16)
        for k in range(shards):
            p_refs[k][...] = d[k * rows : (k + 1) * rows]

    back_one = run(
        back_one_body,
        [shape((rows, width))] * shards,
        [d_projected, w_in],
        grid=(d_steps,),
        in_specs=[whole(d_projected), tiles((tile, 3 * part), 0)],
        out_specs=[tiles((rows, tile), 1)] * shards,
        us=4,
        limit=14,
        hbm=True,
    )
    back_one_got = [swap(back_one[k], "fsdp", k) for k in others]

    def mixer_sum_body(place_ref, nt_ref, dp_ref, in_come_ref, ot_ref, mix_ref, out_come_ref, in_ref, out_ref):
        own = place_ref[1]
        for t in range(3):
            cols = slice(t * part, (t + 1) * part)
            here = mm(nt_ref[own], dp_ref[:, cols]).reshape(blocks, chunk, part)
            in_ref[:, :, cols] = (here + in_come_ref[:, :, cols].astype(f32)).astype(bf16)
        for t in range(width // 512):
            cols = slice(t * 512, (t + 1) * 512)
            here = mm(ot_ref[own], mix_ref[:, cols])
            out_ref[:, cols] = (here + out_come_ref[:, cols].astype(f32)).astype(bf16)

    in_both, out_both = run(
        mixer_sum_body,
        [shape((blocks, chunk, 3 * part)), shape((blocks * slab, width))],
        [place, one_turned, d_projected, in_come, own_turned, mix_all, out_come],
        in_specs=[SMEM]
        + [whole(a) for a in (one_turned, d_projected, in_come, own_turned, mix_all, out_come)],
        after=(in_far(back_one[0]),),
    )

    def final_body(h_ref, w_ref, *p_refs):
        d = mm(flat(h_ref), w_ref[...]).astype(bf16)
        for k in range(shards):
            p_refs[k][...] = d[k * rows : (k + 1) * rows]

    final_parts = run(
        final_body,
        [shape((rows, width))] * shards,
        [hidden_all, in_far(down_proj)],
        grid=(d_steps,),
        in_specs=[whole(hidden_all), tiles((hidden, tile), 1)],
        out_specs=[tiles((rows, tile), 1)] * shards,
        after=(in_both,),
        us=4,
        limit=14,
        hbm=True,
    )

    in_rows = in_both.reshape(blocks, shards, slab, 3 * part)

    def rows_for(k):
        return lax.dynamic_index_in_dim(in_rows, f ^ k, 1, keepdims=False)

    in_pieces = [rows_for(0)] + [swap(rows_for(k), "fsdp", k) for k in others]

    def place_body(place_ref, *refs):
        got, (o_ref, out_ref) = refs[:shards], refs[shards:]
        for s in range(shards):
            pick = got[0][...]
            for k in others:
                pick = jnp.where((place_ref[0] ^ k) == s, got[k][...], pick)
            for t in range(3):
                start = t * width + s * part
                out_ref[:, :, start : start + part] = pick[:, :, t * part : (t + 1) * part]
        out_ref[:, :, 3 * width :] = o_ref[...]

    (mix_both,) = run(
        place_body,
        [far((blocks, slab, 4 * width))],
        [place, *in_pieces, out_both.reshape(blocks, slab, width)],
        in_specs=[SMEM] + [VMEM] * (shards + 1),
        after=(in_far(final_parts[0]),),
        limit=12,
    )
    mix_sum = lax.psum_scatter(mix_both, "seq", scatter_dimension=0, tiled=True).reshape(slab, 4 * width)

    def input_grad_body(*refs):
        parts, (x_ref, d_ref, gain_ref, out_ref, term_ref) = refs[:shards], refs[shards:]
        dn = parts[0][...].astype(f32)
        for p in parts[1:]:
            dn = dn + p[...].astype(f32)
        x = x_ref[...].astype(f32)
        r = lax.rsqrt(jnp.mean(x * x, axis=-1, keepdims=True) + epsilon)
        term_ref[...] = jnp.sum(dn * x * r, axis=0, keepdims=True)
        a = dn * gain_ref[0:1]
        out_ref[...] = d_ref[...] + r * a - x * (r * r * r) * jnp.mean(a * x, axis=-1, keepdims=True)

    input_grad, one_term = run(
        input_grad_body,
        [shape((rows, width), f32), shape((1, width), f32)],
        [back_one[0], *back_one_got, x_local, d_second, gains],
        after=(in_far(mix_both),),
    )
    input_grad = input_grad.reshape(seqs, length, width)


    two_sum = wait_for(two_sum, one_term)
    up_rows = up_sum.reshape(shards, slab, hidden)
    two_rows = two_sum.reshape(shards, slab, 2 * hidden)

    def feed_rows(k):
        parts = [lax.dynamic_index_in_dim(r, f ^ k, 0, keepdims=False) for r in (two_rows, up_rows)]
        return jnp.concatenate(parts, axis=1)

    feed_pieces = [feed_rows(0)] + [swap(feed_rows(k), "fsdp", k) for k in others]

    final_got = [swap(final_parts[k], "fsdp", k) for k in others]
    final_got = wait_all(final_got, feed_pieces[0])
    total = second + final_parts[0].astype(f32)
    for piece in final_got:
        total = total + piece.astype(f32)
    block_output = total.astype(bf16).reshape(seqs, length, width)

    spread_taps = [jnp.where(f == s, tap_terms, 0.0) for s in range(shards)]
    terms = jnp.concatenate([one_term, two_term, jnp.concatenate(spread_taps, axis=1)], axis=0)
    terms = sum_over(sum_over(sum_over(terms, "dp", feed_pieces[:1]), "seq"), "fsdp", feed_pieces[1:])
    own = lax.dynamic_slice_in_dim(terms, ((c * blocks + z) * shards + f) * slab, slab, 1)

    def spread_body(place_ref, *refs):
        got, (up_ref, gate_ref, down_ref) = refs[:shards], refs[shards:]

        def pick(s, start, size):
            value = got[0][:, start : start + size]
            for k in others:
                value = jnp.where((place_ref[0] ^ k) == s, got[k][:, start : start + size], value)
            return value.astype(f32)

        for s in range(shards):
            at = s * hidden
            up_ref[:, at : at + hidden] = pick(s, 2 * hidden, hidden)
            gate_ref[:, at : at + main] = pick(s, 0, main)
            down_ref[:, at : at + main] = pick(s, main, main)
            gate_ref[:, at + main : at + hidden] = pick(s, 2 * main, rest)
            down_ref[:, at + main : at + hidden] = pick(s, 2 * main + rest, rest)

    up_grad, gate_grad, down_rows = run(
        spread_body,
        [far((slab, shards * hidden), f32)] * 3,
        [place, *feed_pieces],
        in_specs=[SMEM] + [whole(p) for p in feed_pieces],
        limit=12,
    )
    down_grad = jnp.transpose(down_rows)

    def last_body(sum_ref, in_ref, out_ref):
        in_ref[...] = sum_ref[:, : 3 * width].astype(f32)
        out_ref[...] = sum_ref[:, 3 * width :].astype(f32)

    in_grad, out_grad = run(
        last_body, [far((slab, 3 * width), f32), far((slab, width), f32)], [in_far(mix_sum)], after=(in_far(gate_grad), in_far(block_output), own)
    )
    return (
        block_output,
        input_grad,
        in_grad,
        out_grad,
        gate_grad,
        up_grad,
        down_grad,
        own[0],
        own[1],
        own[2:],
    )


def solution(mesh):
    placed = (
        P(("dp", "fsdp"), "seq", None),
        P("fsdp", None),
        P("fsdp", None),
        P("fsdp", None),
        P("fsdp", None),
        P("fsdp", None),
        P("fsdp"),
        P("fsdp"),
        P(None, "fsdp"),
        P(("dp", "fsdp"), "seq", None),
    )
    return jax.shard_map(
        on_device,
        mesh=mesh,
        in_specs=placed,
        out_specs=(
            P(("dp", "fsdp"), "seq", None),
            P(("dp", "fsdp"), "seq", None),
            P(("dp", "seq", "fsdp"), None),
            P(("dp", "seq", "fsdp"), None),
            P(("dp", "seq", "fsdp"), None),
            P(("dp", "seq", "fsdp"), None),
            P(None, ("dp", "seq", "fsdp")),
            P(("dp", "seq", "fsdp")),
            P(("dp", "seq", "fsdp")),
            P(None, ("dp", "seq", "fsdp")),
        ),
        check_vma=False,
    )
```

```python
import math

import jax
import jax.numpy as jnp
from jax import lax
from jax.experimental import pallas as pl
from jax.experimental.pallas import tpu as pltpu
from jax.sharding import PartitionSpec as P

epsilon = 1e-05
f32 = jnp.float32
bf16 = jnp.bfloat16
MIB = 1 << 20
SCALE = 1e8
ANY = pl.BlockSpec(memory_space=pl.ANY)


def shape(dims, dtype=bf16):
    return jax.ShapeDtypeStruct(dims, dtype)


def far(dims, dtype=bf16):
    return pltpu.HBM(dims, dtype)


def in_far(value):
    return pltpu.with_memory_space_constraint(value, pltpu.HBM)


def whole(array):
    dims = array.shape
    return pl.BlockSpec(dims, lambda *steps: (0,) * len(dims), pipeline_mode=pl.Buffered(1))


def tiles(dims, axis):
    return pl.BlockSpec(dims, lambda step: tuple(step if i == axis else 0 for i in range(len(dims))))


def run(body, outs, ins, grid=(1,), in_specs=None, out_specs=None, scratch=(), after=(), limit=6, us=1.0, aliases=None, hbm=False, near=()):
    in_specs = [whole(a) for a in ins] if in_specs is None else in_specs
    out_specs = [whole(o) for o in outs] if out_specs is None else out_specs
    n, m = len(ins), len(after)
    if hbm:
        ins = [in_far(a) if a.size > 1024 and i not in near else a for i, a in enumerate(ins)]
        outs = [far(o.shape, o.dtype) if math.prod(o.shape) > 1024 else o for o in outs]

    def kernel(*refs):
        body(*refs[:n], *refs[n + m :])

    return pl.pallas_call(
        kernel,
        out_shape=tuple(outs),
        grid=grid,
        in_specs=list(in_specs) + [ANY] * m,
        out_specs=tuple(out_specs),
        scratch_shapes=list(scratch),
        compiler_params=pltpu.CompilerParams(vmem_limit_bytes=limit * MIB),
        cost_estimate=pl.CostEstimate(flops=int(us * SCALE), bytes_accessed=1000, transcendentals=0),
        input_output_aliases=aliases or {},
    )(*ins, *after)


def mm(a, b):
    return lax.dot_general(a, b, (((1,), (0,)), ((), ())), preferred_element_type=f32)


def mm_t(a, b):
    return lax.dot_general(a, b, (((1,), (1,)), ((), ())), preferred_element_type=f32)


def swap(value, axis, k):
    return lax.ppermute(value, axis, [(i, i ^ k) for i in range(lax.axis_size(axis))])


def shifted(block, axis, distance):
    devices = range(lax.axis_size(axis))
    route = [(i - distance, i) for i in devices if i - distance in devices]
    return lax.ppermute(block, axis, route)


def sum_over(value, axis, after=()):
    size = lax.axis_size(axis)
    if after:
        value = wait_for(value, *after)
    if size <= 4:
        return sum((swap(value, axis, k) for k in range(1, size)), value)
    k = 1
    while k < size:
        value = value + swap(value, axis, k)
        k *= 2
    return value


def wait_body(value_ref, out_ref):
    pass


def wait_for(value, *after, keep=False):
    return run(
        wait_body,
        [far(value.shape, value.dtype) if keep else shape(value.shape, value.dtype)],
        [in_far(value) if keep else value],
        in_specs=[ANY],
        out_specs=[ANY],
        after=after,
        limit=4,
        us=0.3,
        aliases={0: 0},
    )[0]


def wait_all_body(*refs):
    pass


def wait_all(values, *after):
    count = len(values)
    return run(
        wait_all_body,
        [shape(v.shape, v.dtype) for v in values],
        values,
        in_specs=[ANY] * count,
        out_specs=[ANY] * count,
        after=after,
        limit=4,
        us=0.3,
        aliases={i: i for i in range(count)},
    )


def hold_body(value_ref, out_ref, sem):
    copy = pltpu.make_async_copy(value_ref, out_ref, sem)
    copy.start()
    copy.wait()


def hold(value, *after):
    return run(
        hold_body,
        [shape(value.shape, value.dtype)],
        [value],
        in_specs=[ANY],
        out_specs=[ANY],
        scratch=[pltpu.SemaphoreType.DMA(())],
        after=after,
        limit=4,
    )[0]


def on_device(
    block_input,
    in_proj,
    out_proj,
    gate_proj,
    up_proj,
    down_proj,
    norm_one,
    norm_two,
    conv_kernel,
    out_cotangent,
):
    shards = lax.axis_size("fsdp")
    blocks = lax.axis_size("seq")
    f = lax.axis_index("fsdp")
    c = lax.axis_index("dp")
    z = lax.axis_index("seq")
    others = range(1, shards)
    seqs, length, width = block_input.shape
    rows = seqs * length
    group = shards * rows
    part = in_proj.shape[0]
    hidden = down_proj.shape[0]
    taps = conv_kernel.shape[0]
    rim = taps - 1
    edge = 16
    half_part = part // 2
    half = width // 2
    slab = width // (blocks * 2 * shards)
    tile = 512
    h_steps = pl.cdiv(hidden, tile)
    d_steps = width // tile
    chunk = half // blocks
    place = jnp.stack([f, c, z % 2]).astype(jnp.int32)
    SMEM = pl.BlockSpec(memory_space=pltpu.SMEM)
    VMEM = pl.BlockSpec(memory_space=pltpu.VMEM)

    def send_tokens(local):
        return [swap(local, "fsdp", k) for k in others]

    def turn(all_ref, own, keep_ref, send_ref):
        for h in range(2):
            value = all_ref[:, h * half : (h + 1) * half].T

            @pl.when(own == h)
            def _():
                keep_ref[...] = value

            @pl.when(own != h)
            def _():
                send_ref[...] = value

    def pack(pieces, after=()):
        count = len(pieces)

        def body(*refs):
            got, out_ref, sems = refs[:count], refs[count], refs[count + 1]
            copies = [pltpu.make_async_copy(got[i], out_ref.at[i], sems.at[i]) for i in range(count)]
            for copy in copies:
                copy.start()
            for copy in copies:
                copy.wait()

        return run(
            body,
            [shape((count, *pieces[0].shape))],
            pieces,
            in_specs=[ANY] * count,
            out_specs=[VMEM],
            scratch=[pltpu.SemaphoreType.DMA((count,))],
            after=after,
            limit=6,
        )[0]

    def assemble(own, parts, after=(), out=shape, out_spec=VMEM, in_spec=ANY, limit=14):
        planes, columns = parts[0][0].shape[1], parts[0][0].shape[3]
        count = len(others)
        arrays = [p for p, _ in parts]
        starts = jnp.stack([f] + [h for _, h in parts]).astype(jnp.int32)

        def body(place_ref, own_ref, *refs):
            got, out_ref, sems = refs[: len(arrays)], refs[-2], refs[-1]
            f_ = place_ref[0]
            copies = []
            for p in range(planes):
                row = pl.ds(pl.multiple_of(f_ * part, part), part)
                if own.ndim == 3:
                    copies.append(pltpu.make_async_copy(own_ref.at[p], out_ref.at[p, row], sems.at[len(copies)]))
                else:
                    for t in range(columns // part):
                        source = own_ref.at[:, pl.ds(pl.multiple_of(t * width + f_ * part, part), part)]
                        target = out_ref.at[p, row, pl.ds(t * part, part)]
                        copies.append(pltpu.make_async_copy(source, target, sems.at[len(copies)]))
                for j, ref in enumerate(got):
                    size = ref.shape[2]
                    for i, k in enumerate(others):
                        start = pl.multiple_of((f_ ^ k) * part + place_ref[1 + j], size)
                        target = out_ref.at[p, pl.ds(start, size)]
                        copies.append(pltpu.make_async_copy(ref.at[i, p], target, sems.at[len(copies)]))
            for copy in copies:
                copy.start()
            for copy in copies:
                copy.wait()

        return run(
            body,
            [out((planes, width, columns))],
            [starts, own, *arrays],
            in_specs=[SMEM] + [in_spec] * (1 + len(arrays)),
            out_specs=[out_spec],
            scratch=[pltpu.SemaphoreType.DMA((planes * (4 + len(arrays) * count),))],
            after=after,
            limit=limit,
        )[0]

    quarter = half_part // 2
    here, there = (z % 2) * quarter, (1 - z % 2) * quarter

    def in_body(place_ref, w_ref, *refs):
        outs, sems = refs[: len(others)], refs[-1]
        copies = []
        first = pl.multiple_of(place_ref[1] * half_part + place_ref[2] * quarter, quarter)
        for i, k in enumerate(others):
            for t in range(3):
                start = pl.multiple_of(t * width + (place_ref[0] ^ k) * part, part)
                source = w_ref.at[pl.ds(first, quarter), pl.ds(start, part)]
                target = outs[i].at[:, pl.ds(t * part, part)]
                copies.append(pltpu.make_async_copy(source, target, sems.at[i * 3 + t]))
        for copy in copies:
            copy.start()
        for copy in copies:
            copy.wait()

    in_sent = run(
        in_body,
        [shape((quarter, 3 * part))] * len(others),
        [place, in_far(in_proj)],
        in_specs=[SMEM, ANY],
        out_specs=[VMEM] * len(others),
        scratch=[pltpu.SemaphoreType.DMA((3 * len(others),))],
    )
    in_got = [swap(m, "fsdp", k) for m, k in zip(in_sent, others)]

    x_local = block_input.reshape(rows, width)
    cot_local = out_cotangent.reshape(rows, width)
    in_mine = pack(in_got)
    tail = shifted(wait_for(x_local[rows - edge :], in_mine), "seq", 1)
    small = jnp.concatenate([norm_one[None], norm_two[None], conv_kernel], axis=0)
    small = jnp.pad(small, ((0, edge - taps - 2), (0, 0)))

    def join_body(x_ref, t_ref, small_ref, out_ref):
        out_ref[:rows] = x_ref[...]
        out_ref[rows:] = t_ref[...]
        row = lax.broadcasted_iota(jnp.int32, (edge, part), 0)
        out_ref[rows:, :part] = jnp.where(row < taps + 2, small_ref[...], t_ref[:, :part])

    (message,) = run(join_body, [shape((rows + edge, width))], [x_local, tail, small])
    messages = [message] + send_tokens(message)
    taps_own = conv_kernel.astype(f32)

    in_next = swap(in_mine, "seq", 1)

    def both_piece(j, start, size):
        return jnp.stack(
            [lax.dynamic_slice(weight, (start, j * hidden), (size, hidden)) for weight in (gate_proj, up_proj)]
        )

    both_sent = [both_piece(f ^ k, c * half_part + here, quarter) for k in others]
    both_sent = wait_all(both_sent, *in_got)
    both_got = [swap(piece, "fsdp", k) for piece, k in zip(both_sent, others)]

    both_mine = pack(both_got, (in_next, message))
    both_next = swap(both_mine, "seq", 1)

    def norm_body(place_ref, *refs):
        xs, (n_ref, nh_ref, gain_ref) = refs[:shards], refs[shards:]
        for s in range(shards):
            pick = xs[0][rows:, :part]
            for k in others:
                pick = jnp.where((place_ref[0] ^ k) == s, xs[k][rows:, :part], pick)
            gain_ref[:, s * part : (s + 1) * part] = pick[:8].astype(f32)
        gain = gain_ref[0:1]

        def normed(v):
            v = v.astype(f32)
            r = lax.rsqrt(jnp.mean(v * v, axis=-1, keepdims=True) + epsilon)
            return (v * r * gain).astype(bf16)

        for k in range(shards):
            n_ref[k * rows : (k + 1) * rows] = normed(xs[k][:rows])
            nh_ref[k * edge : (k + 1) * edge] = normed(xs[k][rows:])

    normed_one, normed_edge, gains = run(
        norm_body,
        [shape((group, width)), shape((shards * edge, width)), shape((8, width), f32)],
        [place, *[in_far(m) for m in messages]],
        in_specs=[SMEM] + [whole(m) for m in messages],
        after=(both_mine,),
        us=2,
    )

    w_in = assemble(
        in_far(in_proj),
        [
            (in_mine[:, None], c * half_part + here),
            (in_next[:, None], c * half_part + there),
            (swap(in_mine, "dp", 1)[:, None], (1 - c) * half_part + here),
            (swap(in_next, "dp", 1)[:, None], (1 - c) * half_part + there),
        ],
        (both_mine,),
    )[0]

    cot_held = hold(cot_local, both_mine)
    cot_blocks = [cot_held] + send_tokens(cot_held)

    def mixer_body(n_ref, nh_ref, taps_ref, w_ref, o_ref, far_ref, edge_ref, gated_ref, *refs):
        p_refs, (ph_ref, ext_ref, proj_ref, sem) = refs[:shards], refs[shards:]
        for t in range(3):
            cols = slice(t * part, (t + 1) * part)
            w = w_ref[:, cols]
            proj_ref[:, cols] = mm(n_ref[...], w)
            if t != 1:
                ph_ref[:, cols] = mm(nh_ref[...], w)
        leave = pltpu.make_async_copy(proj_ref, far_ref, sem)
        leave.start()
        edge_ref[...] = ph_ref[:, :part] * ph_ref[:, 2 * part :]
        for k in range(shards):
            r = slice(k * rows, (k + 1) * rows)
            ext_ref[:edge] = edge_ref[k * edge : (k + 1) * edge]
            ext_ref[edge:] = proj_ref[r, :part] * proj_ref[r, 2 * part :]
            conv = taps_ref[rim : rim + 1] * ext_ref[edge:]
            for t in range(rim):
                conv = conv + taps_ref[t : t + 1] * ext_ref[edge - rim + t : edge - rim + t + rows]
            gated_ref[r] = (proj_ref[r, part : 2 * part] * conv).astype(bf16)
        for t in range(width // 512):
            cols = slice(t * 512, (t + 1) * 512)
            o = mm(gated_ref[...], o_ref[:, cols]).astype(bf16)
            for k in range(shards):
                p_refs[k][:, cols] = o[k * rows : (k + 1) * rows]
        leave.wait()

    projected, edge_product, gated, *mix_parts = run(
        mixer_body,
        [
            far((group, 3 * part), f32),
            far((shards * edge, part), f32),
            shape((group, part)),
        ]
        + [shape((rows, width))] * shards,
        [normed_one, normed_edge, taps_own, w_in, out_proj],
        out_specs=[ANY, whole(shape((shards * edge, part))), whole(shape((group, part)))]
        + [whole(shape((rows, width)))] * shards,
        scratch=[
            pltpu.VMEM((shards * edge, 3 * part), f32),
            pltpu.VMEM((edge + rows, part), f32),
            pltpu.VMEM((group, 3 * part), f32),
            pltpu.SemaphoreType.DMA(()),
        ],
        after=(cot_held,),
        us=5.5,
        limit=10,
    )

    def cot_body(place_ref, *refs):
        blocks_, (down_ref, dh_ref, keep_ref, send_ref, all_ref) = refs[:shards], refs[shards:]

        @pl.when(pl.program_id(0) == 0)
        def _():
            for k in range(shards):
                all_ref[k * rows : (k + 1) * rows] = blocks_[k][...]
            turn(all_ref, place_ref[1], keep_ref, send_ref)

        dh_ref[...] = mm_t(all_ref[...], down_ref[...])

    d_hidden, cot_keep, cot_send = run(
        cot_body,
        [shape((group, hidden), f32), far((half, group)), far((half, group))],
        [place, *cot_blocks, in_far(down_proj)],
        grid=(h_steps,),
        in_specs=[SMEM] + [whole(b) for b in cot_blocks] + [tiles((tile, width), 0)],
        out_specs=[tiles((group, tile), 1), whole(shape((half, group))), whole(shape((half, group)))],
        scratch=[pltpu.VMEM((group, width), bf16)],
        after=(gated,),
        us=5,
        limit=14,
    )

    cot_come = swap(cot_send, "dp", 1)
    mix_got = [swap(mix_parts[k], "fsdp", k) for k in others]

    def second_body(*refs):
        parts, x_ref, gain_ref, s_ref, n_ref = refs[:shards], *refs[shards:]
        total = x_ref[...].astype(f32)
        for p in parts:
            total = total + p[...].astype(f32)
        s_ref[...] = total
        r = lax.rsqrt(jnp.mean(total * total, axis=-1, keepdims=True) + epsilon)
        n_ref[...] = (total * r * gain_ref[1:2]).astype(bf16)

    second, normed_two = run(
        second_body,
        [shape((rows, width), f32), shape((rows, width))],
        [mix_parts[0], *mix_got, x_local, gains],
        after=(d_hidden,),
    )
    two_blocks = [normed_two] + send_tokens(normed_two)

    both_next = wait_for(both_next, normed_two)
    w_both = assemble(
        both_piece(f, 0, part),
        [
            (both_mine, c * half_part + here),
            (both_next, c * half_part + there),
            (swap(both_mine, "dp", 1), (1 - c) * half_part + here),
            (swap(both_next, "dp", 1), (1 - c) * half_part + there),
        ],
        (normed_two,),
        out=far,
        out_spec=ANY,
        in_spec=VMEM,
        limit=20,
    )
    w_both = in_far(w_both)
    turned = shape((half, group))

    def turn_two_body(place_ref, *refs):
        blocks_, (all_ref, keep_ref, send_ref) = refs[:shards], refs[shards:]
        for k in range(shards):
            all_ref[k * rows : (k + 1) * rows] = blocks_[k][...]
        turn(all_ref, place_ref[1], keep_ref, send_ref)

    two_all, two_keep, two_send = run(
        turn_two_body,
        [shape((group, width)), turned, turned],
        [place, *two_blocks],
        in_specs=[SMEM] + [whole(b) for b in two_blocks],
        after=(w_both,),
    )
    two_come = swap(two_send, "dp", 1)

    bundle = 32
    units = (group // bundle, bundle, hidden)
    wide = 896
    wide_units = tiles((group // bundle, bundle, wide), 2)
    unit_tiles = tiles((group // bundle, bundle, tile), 2)
    def gate_body(all_ref, w_ref, dh_ref, g_ref, du_ref):
        gate_ = mm(all_ref[...], w_ref[...])
        g_ref[...] = gate_
        du = dh_ref[...] * (gate_ * jax.nn.sigmoid(gate_))
        du_ref[...] = du.astype(bf16).reshape(du_ref.shape)

    gate, d_up = run(
        gate_body,
        [far((group, hidden), f32), far(units)],
        [two_all, w_both, d_hidden],
        grid=(pl.cdiv(hidden, wide),),
        in_specs=[
            whole(two_all),
            pl.BlockSpec((None, width, wide), lambda step: (0, 0, step)),
            tiles((group, wide), 1),
        ],
        out_specs=[tiles((group, wide), 1), wide_units],
        us=6,
        limit=18,
    )
    gate = in_far(gate)
    d_up = wait_for(d_up, two_come, keep=True)
    d_up_come = swap(d_up, "dp", 1)

    def flat(ref):
        return ref[...].reshape(group, ref.shape[2])

    def up_own_body(own_ref, du_ref, out_ref):
        out_ref[...] = mm(own_ref[...], flat(du_ref)).astype(bf16)

    (up_own,) = run(
        up_own_body,
        [shape((half, hidden))],
        [two_keep, in_far(d_up)],
        grid=(pl.cdiv(hidden, wide),),
        in_specs=[whole(turned), wide_units],
        out_specs=[tiles((half, wide), 1)],
        us=3,
        limit=8,
    )

    def up_sum_body(term_ref, come_ref, duc_ref, out_ref):
        total = term_ref[...].astype(f32) + mm(come_ref[...], flat(duc_ref))
        out_ref[...] = total.astype(bf16).reshape(blocks, chunk, wide)

    (up_both,) = run(
        up_sum_body,
        [far((blocks, chunk, hidden))],
        [up_own, two_come, d_up_come],
        grid=(pl.cdiv(hidden, wide),),
        in_specs=[tiles((half, wide), 1), whole(turned), wide_units],
        out_specs=[tiles((blocks, chunk, wide), 2)],
        us=5,
        limit=11,
    )
    up_sum = lax.psum_scatter(up_both, "seq", scatter_dimension=0, tiled=True).reshape(chunk, hidden)

    def up_body(all_ref, w_ref, g_ref, dh_ref, dg_ref, h_ref):
        upward = mm(all_ref[...], w_ref[...])
        gate_ = g_ref[...]
        s = jax.nn.sigmoid(gate_)
        dg = dh_ref[...] * upward * s * (1.0 + gate_ * (1.0 - s))
        dg_ref[...] = dg.astype(bf16).reshape(dg_ref.shape)
        h_ref[...] = (gate_ * s * upward).astype(bf16).reshape(h_ref.shape)

    d_gate, hidden_all = run(
        up_body,
        [far(units)] * 2,
        [two_all, w_both, gate, d_hidden],
        grid=(h_steps,),
        in_specs=[
            whole(two_all),
            pl.BlockSpec((None, width, tile), lambda step: (1, 0, step)),
            tiles((group, tile), 1),
            tiles((group, tile), 1),
        ],
        out_specs=[unit_tiles] * 2,
        after=(in_far(up_both),),
        us=7,
        limit=18,
    )
    d_gate_come = swap(d_gate, "dp", 1)
    hidden_come = swap(hidden_all, "dp", 1)

    def back_two_body(dg_ref, du_ref, wg_ref, wu_ref, *p_refs):
        d = (mm_t(flat(dg_ref), wg_ref[...]) + mm_t(flat(du_ref), wu_ref[...])).astype(bf16)
        for k in range(shards):
            p_refs[k][...] = d[k * rows : (k + 1) * rows]

    back_two = run(
        back_two_body,
        [shape((rows, width))] * shards,
        [d_gate, d_up, w_both, w_both],
        grid=(d_steps,),
        in_specs=[
            whole(d_gate),
            whole(d_up),
            pl.BlockSpec((None, tile, hidden), lambda step: (0, step, 0)),
            pl.BlockSpec((None, tile, hidden), lambda step: (1, step, 0)),
        ],
        out_specs=[tiles((rows, tile), 1)] * shards,
        us=7,
        limit=16,
        hbm=True,
    )
    back_two_got = [swap(back_two[k], "fsdp", k) for k in others]

    main = hidden // 128 * 128
    rest = hidden - main
    last_main = main - (h_steps - 1) * tile

    def two_sum_body(own_ref, come_ref, cot_own_ref, cot_come_ref, dg_ref, dgc_ref, h_ref, hc_ref, out_ref):
        step = pl.program_id(0)
        gate_ = mm(own_ref[...], flat(dg_ref)) + mm(come_ref[...], flat(dgc_ref))
        gate_ = gate_.reshape(blocks, chunk, tile)
        down_ = mm(cot_own_ref[...], flat(h_ref)) + mm(cot_come_ref[...], flat(hc_ref))
        down_ = down_.reshape(blocks, chunk, tile)

        @pl.when(step < h_steps - 1)
        def _():
            at = pl.multiple_of(step * tile, 128)
            out_ref[:, :, pl.ds(at, tile)] = gate_.astype(bf16)
            out_ref[:, :, pl.ds(main + at, tile)] = down_.astype(bf16)

        @pl.when(step == h_steps - 1)
        def _():
            out_ref[:, :, main - last_main : main] = gate_[:, :, :last_main].astype(bf16)
            out_ref[:, :, 2 * main - last_main : 2 * main] = down_[:, :, :last_main].astype(bf16)
            rests = [v[:, :, last_main : last_main + rest] for v in (gate_, down_)]
            out_ref[:, :, 2 * main :] = jnp.concatenate(rests, axis=2).astype(bf16)

    (two_both,) = run(
        two_sum_body,
        [shape((blocks, chunk, 2 * hidden))],
        [two_keep, two_come, cot_keep, cot_come, d_gate, d_gate_come, hidden_all, hidden_come],
        grid=(h_steps,),
        in_specs=[whole(turned)] * 4 + [unit_tiles] * 4,
        out_specs=[whole(shape((blocks, chunk, 2 * hidden)))],
        after=(in_far(back_two[0]),),
        us=10,
        limit=24,
        hbm=True,
        near=(0, 1, 2, 3, 5, 7),
    )
    two_sum = lax.psum_scatter(two_both, "seq", scatter_dimension=0, tiled=True)
    two_sum = two_sum.reshape(chunk, 2 * hidden)

    def second_grad_body(*refs):
        parts, (s_ref, cot_ref, gain_ref, d_ref, mix_ref, term_ref) = refs[:shards], refs[shards:]
        dn = parts[0][...].astype(f32)
        for p in parts[1:]:
            dn = dn + p[...].astype(f32)
        s = s_ref[...]
        r = lax.rsqrt(jnp.mean(s * s, axis=-1, keepdims=True) + epsilon)
        term_ref[...] = jnp.sum(dn * s * r, axis=0, keepdims=True)
        a = dn * gain_ref[1:2]
        d = cot_ref[...].astype(f32) + r * a - s * (r * r * r) * jnp.mean(a * s, axis=-1, keepdims=True)
        d_ref[...] = d
        mix_ref[...] = d.astype(bf16)

    d_second, d_mix, two_term = run(
        second_grad_body,
        [shape((rows, width), f32), shape((rows, width)), shape((1, width), f32)],
        [back_two[0], *back_two_got, second, cot_local, gains],
    )
    mix_blocks = [d_mix] + send_tokens(d_mix)

    runs = part // (shards * slab)
    channels = part // shards

    def owner_body(place_ref, g_ref, *out_refs):
        row = lax.broadcasted_iota(jnp.int32, (part, channels), 0)
        col = lax.broadcasted_iota(jnp.int32, (part, channels), 1)
        for k in range(shards):
            source = (col // slab) * (shards * slab) + (place_ref[0] ^ k) * slab + col % slab
            out_refs[k][...] = mm(g_ref[...], (row == source).astype(bf16)).astype(bf16)

    owner = run(
        owner_body,
        [shape((group, channels))] * shards,
        [place, gated],
        in_specs=[SMEM, whole(gated)],
        after=(in_far(two_both),),
    )
    owner_got = [owner[0]] + [swap(owner[k], "fsdp", k) for k in others]

    def gated_grad_body(*refs):
        blocks_, (o_ref, proj_ref, edge_ref, taps_ref) = refs[:shards], refs[shards : shards + 4]
        all_ref, dc_ref, dconv_ref, head_ref, term_ref, ext_ref = refs[shards + 4 :]
        for k in range(shards):
            all_ref[k * rows : (k + 1) * rows] = blocks_[k][...]
        dg = mm_t(all_ref[...], o_ref[...])
        dconv_ref[...] = dg * proj_ref[:, part : 2 * part]
        terms = [jnp.zeros((1, part), f32)] * taps
        for k in range(shards):
            r = slice(k * rows, (k + 1) * rows)
            d = dconv_ref[r]
            head_ref[k * 8 : (k + 1) * 8] = d[:8]
            ext_ref[:edge] = edge_ref[k * edge : (k + 1) * edge]
            ext_ref[edge:] = proj_ref[r, :part] * proj_ref[r, 2 * part :]
            conv = jnp.zeros((rows, part), f32)
            for t in range(taps):
                e = ext_ref[edge - rim + t : edge - rim + t + rows]
                conv = conv + taps_ref[t : t + 1] * e
                terms[t] = terms[t] + jnp.sum(d * e, axis=0, keepdims=True)
            dc_ref[r] = (dg[k * rows : (k + 1) * rows] * conv).astype(bf16)
        for t in range(taps):
            term_ref[t : t + 1] = terms[t]

    mix_all, d_c, d_conv, heads, tap_terms = run(
        gated_grad_body,
        [
            shape((group, width)),
            shape((group, part)),
            shape((group, part), f32),
            shape((shards * 8, part), f32),
            shape((taps, part), f32),
        ],
        [*mix_blocks, out_proj, projected, edge_product, taps_own],
        scratch=[pltpu.VMEM((edge + rows, part), f32)],
    )
    behind = shifted(heads, "seq", -1)

    def turn_body(place_ref, n_ref, *refs):
        got, (nt_ref, ot_ref) = refs[:shards], refs[shards:]
        for h in range(2):
            nt_ref[h] = n_ref[:, h * half : (h + 1) * half].T
        row = lax.broadcasted_iota(jnp.int32, (channels, part), 0)
        col = lax.broadcasted_iota(jnp.int32, (channels, part), 1)
        for b in range(shards):
            both = jnp.zeros((rows, part), f32)
            for k in range(shards):
                spread = (col == row + (place_ref[0] ^ k) * channels).astype(bf16)
                both = both + mm(got[k][(b ^ k) * rows : ((b ^ k) + 1) * rows], spread)
            both = both.astype(bf16)
            for h in range(2):
                wide = both[:, h * (part // 2) : (h + 1) * (part // 2)]
                ot_ref[h, :, b * rows : (b + 1) * rows] = wide.astype(f32).T.astype(bf16)

    one_turned, own_turned = run(
        turn_body,
        [shape((2, half, group)), shape((2, part // 2, group))],
        [place, normed_one, *owner_got],
        in_specs=[SMEM, whole(normed_one)] + [whole(o) for o in owner_got],
        after=(mix_blocks[0],),
    )

    def projected_grad_body(
        place_ref, dconv_ref, behind_ref, taps_ref, proj_ref, dc_ref, nt_ref, ot_ref, mix_ref,
        dp_ref, in_ref, out_ref, ext_ref,
    ):
        other = 1 - place_ref[1]
        for k in range(shards):
            r = slice(k * rows, (k + 1) * rows)
            ext_ref[:rows] = dconv_ref[r]
            ext_ref[rows:] = behind_ref[k * 8 : (k + 1) * 8]
            d = taps_ref[rim : rim + 1] * ext_ref[:rows]
            for t in range(rim):
                d = d + taps_ref[t : t + 1] * ext_ref[rim - t : rim - t + rows]
            dp_ref[r, :part] = (d * proj_ref[r, 2 * part :]).astype(bf16)
            dp_ref[r, part : 2 * part] = dc_ref[r]
            dp_ref[r, 2 * part :] = (d * proj_ref[r, :part]).astype(bf16)
        for t in range(3):
            cols = slice(t * part, (t + 1) * part)
            in_ref[:, :, cols] = mm(nt_ref[other], dp_ref[:, cols]).astype(bf16).reshape(blocks, chunk, part)
        for t in range(width // 512):
            cols = slice(t * 512, (t + 1) * 512)
            out_ref[:, cols] = mm(ot_ref[other], mix_ref[:, cols]).astype(bf16)

    d_projected, in_there, out_there = run(
        projected_grad_body,
        [shape((group, 3 * part)), shape((blocks, chunk, 3 * part)), shape((part // 2, width))],
        [place, d_conv, behind, taps_own, projected, d_c, one_turned, own_turned, mix_all],
        in_specs=[SMEM] + [whole(a) for a in (d_conv, behind, taps_own, projected, d_c, one_turned, own_turned, mix_all)],
        scratch=[pltpu.VMEM((rows + 8, part), f32)],
        us=3,
    )
    in_come = swap(in_there, "dp", 1)
    out_come = swap(out_there, "dp", 1)

    def back_one_body(dp_ref, w_ref, *p_refs):
        d = mm_t(dp_ref[...], w_ref[...]).astype(bf16)
        for k in range(shards):
            p_refs[k][...] = d[k * rows : (k + 1) * rows]

    back_one = run(
        back_one_body,
        [shape((rows, width))] * shards,
        [d_projected, w_in],
        grid=(d_steps,),
        in_specs=[whole(d_projected), tiles((tile, 3 * part), 0)],
        out_specs=[tiles((rows, tile), 1)] * shards,
        us=4,
        limit=14,
        hbm=True,
    )
    back_one_got = [swap(back_one[k], "fsdp", k) for k in others]

    def mixer_sum_body(place_ref, nt_ref, dp_ref, in_come_ref, ot_ref, mix_ref, out_come_ref, in_ref, out_ref):
        own = place_ref[1]
        for t in range(3):
            cols = slice(t * part, (t + 1) * part)
            here = mm(nt_ref[own], dp_ref[:, cols]).reshape(blocks, chunk, part)
            in_ref[:, :, cols] = (here + in_come_ref[:, :, cols].astype(f32)).astype(bf16)
        for t in range(width // 512):
            cols = slice(t * 512, (t + 1) * 512)
            here = mm(ot_ref[own], mix_ref[:, cols])
            out_ref[:, cols] = (here + out_come_ref[:, cols].astype(f32)).astype(bf16)

    in_both, out_both = run(
        mixer_sum_body,
        [shape((blocks, chunk, 3 * part)), shape((blocks * slab, width))],
        [place, one_turned, d_projected, in_come, own_turned, mix_all, out_come],
        in_specs=[SMEM]
        + [whole(a) for a in (one_turned, d_projected, in_come, own_turned, mix_all, out_come)],
        after=(in_far(back_one[0]),),
    )

    def final_body(h_ref, w_ref, *p_refs):
        d = mm(flat(h_ref), w_ref[...]).astype(bf16)
        for k in range(shards):
            p_refs[k][...] = d[k * rows : (k + 1) * rows]

    final_parts = run(
        final_body,
        [shape((rows, width))] * shards,
        [hidden_all, in_far(down_proj)],
        grid=(d_steps,),
        in_specs=[whole(hidden_all), tiles((hidden, tile), 1)],
        out_specs=[tiles((rows, tile), 1)] * shards,
        after=(in_both,),
        us=4,
        limit=14,
        hbm=True,
    )

    in_rows = in_both.reshape(blocks, shards, slab, 3 * part)

    def rows_for(k):
        return lax.dynamic_index_in_dim(in_rows, f ^ k, 1, keepdims=False)

    in_pieces = [rows_for(0)] + [swap(rows_for(k), "fsdp", k) for k in others]

    def place_body(place_ref, *refs):
        got, (o_ref, out_ref) = refs[:shards], refs[shards:]
        for s in range(shards):
            pick = got[0][...]
            for k in others:
                pick = jnp.where((place_ref[0] ^ k) == s, got[k][...], pick)
            for t in range(3):
                start = t * width + s * part
                out_ref[:, :, start : start + part] = pick[:, :, t * part : (t + 1) * part]
        out_ref[:, :, 3 * width :] = o_ref[...]

    (mix_both,) = run(
        place_body,
        [far((blocks, slab, 4 * width))],
        [place, *in_pieces, out_both.reshape(blocks, slab, width)],
        in_specs=[SMEM] + [VMEM] * (shards + 1),
        after=(in_far(final_parts[0]),),
        limit=12,
    )
    mix_sum = lax.psum_scatter(mix_both, "seq", scatter_dimension=0, tiled=True).reshape(slab, 4 * width)

    def input_grad_body(*refs):
        parts, (x_ref, d_ref, gain_ref, out_ref, term_ref) = refs[:shards], refs[shards:]
        dn = parts[0][...].astype(f32)
        for p in parts[1:]:
            dn = dn + p[...].astype(f32)
        x = x_ref[...].astype(f32)
        r = lax.rsqrt(jnp.mean(x * x, axis=-1, keepdims=True) + epsilon)
        term_ref[...] = jnp.sum(dn * x * r, axis=0, keepdims=True)
        a = dn * gain_ref[0:1]
        out_ref[...] = d_ref[...] + r * a - x * (r * r * r) * jnp.mean(a * x, axis=-1, keepdims=True)

    input_grad, one_term = run(
        input_grad_body,
        [shape((rows, width), f32), shape((1, width), f32)],
        [back_one[0], *back_one_got, x_local, d_second, gains],
        after=(in_far(mix_both),),
    )
    input_grad = input_grad.reshape(seqs, length, width)


    two_sum = wait_for(two_sum, one_term)
    up_rows = up_sum.reshape(shards, slab, hidden)
    two_rows = two_sum.reshape(shards, slab, 2 * hidden)

    def feed_rows(k):
        parts = [lax.dynamic_index_in_dim(r, f ^ k, 0, keepdims=False) for r in (two_rows, up_rows)]
        return jnp.concatenate(parts, axis=1)

    feed_pieces = [feed_rows(0)] + [swap(feed_rows(k), "fsdp", k) for k in others]

    final_got = [swap(final_parts[k], "fsdp", k) for k in others]
    final_got = wait_all(final_got, feed_pieces[0])
    total = second + final_parts[0].astype(f32)
    for piece in final_got:
        total = total + piece.astype(f32)
    block_output = total.astype(bf16).reshape(seqs, length, width)

    spread_taps = [jnp.where(f == s, tap_terms, 0.0) for s in range(shards)]
    terms = jnp.concatenate([one_term, two_term, jnp.concatenate(spread_taps, axis=1)], axis=0)
    terms = sum_over(sum_over(sum_over(terms, "dp", feed_pieces[:1]), "seq"), "fsdp", feed_pieces[1:])
    own = lax.dynamic_slice_in_dim(terms, ((c * blocks + z) * shards + f) * slab, slab, 1)

    def spread_body(place_ref, *refs):
        got, (up_ref, gate_ref, down_ref) = refs[:shards], refs[shards:]

        def pick(s, start, size):
            value = got[0][:, start : start + size]
            for k in others:
                value = jnp.where((place_ref[0] ^ k) == s, got[k][:, start : start + size], value)
            return value.astype(f32)

        for s in range(shards):
            at = s * hidden
            up_ref[:, at : at + hidden] = pick(s, 2 * hidden, hidden)
            gate_ref[:, at : at + main] = pick(s, 0, main)
            down_ref[:, at : at + main] = pick(s, main, main)
            gate_ref[:, at + main : at + hidden] = pick(s, 2 * main, rest)
            down_ref[:, at + main : at + hidden] = pick(s, 2 * main + rest, rest)

    up_grad, gate_grad, down_rows = run(
        spread_body,
        [far((slab, shards * hidden), f32)] * 3,
        [place, *feed_pieces],
        in_specs=[SMEM] + [whole(p) for p in feed_pieces],
        limit=12,
    )
    down_grad = jnp.transpose(down_rows)

    def last_body(sum_ref, in_ref, out_ref):
        in_ref[...] = sum_ref[:, : 3 * width].astype(f32)
        out_ref[...] = sum_ref[:, 3 * width :].astype(f32)

    in_grad, out_grad = run(
        last_body, [far((slab, 3 * width), f32), far((slab, width), f32)], [in_far(mix_sum)], after=(in_far(gate_grad), in_far(block_output), own)
    )
    return (
        block_output,
        input_grad,
        in_grad,
        out_grad,
        gate_grad,
        up_grad,
        down_grad,
        own[0],
        own[1],
        own[2:],
    )


def solution(mesh):
    placed = (
        P(("dp", "fsdp"), "seq", None),
        P("fsdp", None),
        P("fsdp", None),
        P("fsdp", None),
        P("fsdp", None),
        P("fsdp", None),
        P("fsdp"),
        P("fsdp"),
        P(None, "fsdp"),
        P(("dp", "fsdp"), "seq", None),
    )
    return jax.shard_map(
        on_device,
        mesh=mesh,
        in_specs=placed,
        out_specs=(
            P(("dp", "fsdp"), "seq", None),
            P(("dp", "fsdp"), "seq", None),
            P(("dp", "seq", "fsdp"), None),
            P(("dp", "seq", "fsdp"), None),
            P(("dp", "seq", "fsdp"), None),
            P(("dp", "seq", "fsdp"), None),
            P(None, ("dp", "seq", "fsdp")),
            P(("dp", "seq", "fsdp")),
            P(("dp", "seq", "fsdp")),
            P(None, ("dp", "seq", "fsdp")),
        ),
        check_vma=False,
    )
```
